128 devices in a mesh: lat: 4 (over y_hi, core), lon: 32 (over z, x, y_lo).
Axes of the slice: x: 4, y: 4 (y_hi: 2, y_lo: 2; y = y_hi * 2 + y_lo), z: 4, core: 2. Of those that a mesh axis runs over, the one named last changes fastest.
Arguments:
- tokens: bfloat16 [2, 24, 1536, 192], P(None, 'lat', 'lon'), may hold values from -6 to 6
- cotangent: bfloat16 [2, 24, 1536, 192], P(None, 'lat', 'lon'), may hold values from -6 to 6
- norm_gains: float32 [2, 2, 192], replicated, may hold values from 0.1 to 1.9
- w_qkv: bfloat16 [2, 192, 576], replicated, may hold values from -0.4375 to 0.4375
- w_proj: bfloat16 [2, 192, 192], replicated, may hold values from -0.4375 to 0.4375
- w_up: bfloat16 [2, 192, 768], replicated, may hold values from -0.4375 to 0.4375
- w_down: bfloat16 [2, 768, 192], replicated, may hold values from -0.21875 to 0.21875
- pos_bias: float32 [2, 6, 144, 144], replicated, may hold values from -4 to 300
Outputs:
- grad_input: bfloat16 [2, 24, 1536, 192], P(None, 'lat', 'lon')
- grad_matrix: float32 [2, 192, 2304], P(None, None, ('lat', 'lon'))
- grad_other: float32 [2, 124800], P(None, ('lat', 'lon'))
The draws below stay inside these ranges and needn't reach their ends.
All inputs are finite; a program needn't handle non-finite values.
Results may differ from the reference program's by a relative error of at most 0.03.
Values may be sent and summed in bfloat16 or wider, within the bound.
A program may use at most 128 MiB of HBM per device.

```python
import math
import jax
import jax.numpy as jnp
from jax import lax

C = 192
HEADS = 6
FFN = 768
PL = 2
WLAT = 6
WLON = 12
SLAT = 3
SLON = 6
WT = 144
LAT = 24
LON = 1536
VECB = 124800


def draw_pos_bias(key, part):
    key = jax.random.fold_in(key, 7)
    table_shape = (2, HEADS, WT, WT)
    table = jax.random.truncated_normal(key, -4.0, 4.0, table_shape, jnp.float32)
    return table


def shard_levels(own_key, extent, shards, low, top_value):
    factor_of = 1.0
    for dim, shards_of in shards:
        draws = jax.random.uniform(jax.random.fold_in(jax.random.fold_in(own_key, 6), dim), (shards_of,), jnp.float32, low / len(shards), top_value / len(shards))
        factor_of = factor_of * jnp.repeat(jnp.exp(draws), extent[dim] // shards_of).reshape((-1,) + (1,) * (len(extent) - 1 - dim))
    return factor_of


def gaussian(key, extent, scale, bound, pieces=(), kind=jnp.bfloat16):
    gain = shard_levels(key, extent, pieces, -0.22, 0.18) if pieces else 1.0
    entries = jax.random.normal(key, extent, jnp.float32) * scale * gain
    return jnp.minimum(jnp.maximum(entries, -bound), bound).astype(kind)


def setup_inputs(seed: int = 0) -> dict:
    key_list = jax.random.split(jax.random.key(seed), 9)
    tokens = gaussian(key_list[0], (PL, LAT, LON, C), 1.0, 6.0, ((1, 4), (2, 32)))
    cotangent = gaussian(key_list[1], (PL, LAT, LON, C), 1.0, 6.0, ((1, 4), (2, 32)))
    norm_gains = jnp.clip(1.0 + 0.18 * jax.random.normal(key_list[2], (2, 2, C), jnp.float32), 0.1, 1.9)
    w_qkv = gaussian(key_list[3], (2, C, 3 * C), C ** -0.5, 0.4375)
    w_proj = gaussian(key_list[4], (2, C, C), C ** -0.5, 0.4375)
    w_up = gaussian(key_list[5], (2, C, FFN), C ** -0.5, 0.4375)
    w_down = gaussian(key_list[6], (2, FFN, C), FFN ** -0.5, 0.21875)
    pos_bias = draw_pos_bias(jax.random.fold_in(key_list[8], 71), 0)
    return {"tokens": tokens, "cotangent": cotangent, "norm_gains": norm_gains, "w_qkv": w_qkv, "w_proj": w_proj, "w_up": w_up, "w_down": w_down, "pos_bias": pos_bias}


def layer_norm(values, gain_vec):
    widened = values.astype(jnp.float32)
    center = widened - lax.optimization_barrier(jnp.mean(widened, axis=-1, keepdims=True))
    spread = lax.optimization_barrier(jnp.mean(center * center, axis=-1, keepdims=True))
    return (center * lax.rsqrt(spread + 1e-05) * gain_vec).astype(jnp.bfloat16)

def to_windows(grid_field):
    levels, lat_rows, lon_cols, channels = grid_field.shape
    blocks_view = grid_field.reshape(levels, lat_rows // WLAT, WLAT, lon_cols // WLON, WLON, channels)
    blocks_view = blocks_view.transpose(1, 3, 0, 2, 4, 5)
    return blocks_view.reshape(lat_rows // WLAT * (lon_cols // WLON), levels * WLAT * WLON, channels)

def from_windows(windows, levels, lat_rows, lon_cols):
    channels = windows.shape[-1]
    blocks_view = windows.reshape(lat_rows // WLAT, lon_cols // WLON, levels, WLAT, WLON, channels)
    return blocks_view.transpose(2, 0, 3, 1, 4, 5).reshape(levels, lat_rows, lon_cols, channels)

def window_attention(normed, w_qkv, w_proj, bias_table, keys_kept):
    window_count, tokens_win, channels = normed.shape
    head_size = channels // HEADS
    packed = jnp.dot(normed.reshape(window_count * tokens_win, channels), w_qkv, preferred_element_type=jnp.float32)
    packed = lax.optimization_barrier(packed.astype(jnp.bfloat16)).astype(jnp.float32)
    packed = packed.reshape(window_count, tokens_win, 3, HEADS, head_size)
    scores = jnp.einsum('nqhd,nkhd->nhqk', packed[:, :, 0], packed[:, :, 1]) * head_size ** (-0.5) + bias_table[None]
    scores = jnp.where(keys_kept[:, None, None, :], scores, -1e+30)
    weights = jax.nn.softmax(scores, axis=-1)
    weights = lax.optimization_barrier(weights.astype(jnp.bfloat16)).astype(jnp.float32)
    mixed_heads = jnp.einsum('nhqk,nkhd->nqhd', weights, packed[:, :, 2]).astype(jnp.bfloat16)
    result = jnp.dot(mixed_heads.reshape(window_count * tokens_win, channels), w_proj, preferred_element_type=jnp.float32)
    return result.astype(jnp.bfloat16).reshape(window_count, tokens_win, channels)

def attend_rows(normed, w_qkv, w_proj, bias_table, keys_kept, per_row):
    window_count, tokens_win, channels = normed.shape

    def attend_one(pair_item):
        return window_attention(pair_item[0], w_qkv, w_proj, bias_table, pair_item[1])
    grouped = (normed.reshape(window_count // per_row, per_row, tokens_win, channels), keys_kept.reshape(window_count // per_row, per_row, tokens_win))
    result = lax.map(jax.checkpoint(attend_one), grouped)
    return result.reshape(window_count, tokens_win, channels)

def feed_forward(hidden, gain_vec, w_up, w_down):
    in_shape = hidden.shape
    normed = layer_norm(hidden, gain_vec).reshape(-1, in_shape[-1])
    inner_act = jax.nn.gelu(jnp.dot(normed, w_up, preferred_element_type=jnp.float32), approximate=False)
    inner_act = inner_act.astype(jnp.bfloat16)
    result = jnp.dot(inner_act, w_down, preferred_element_type=jnp.float32).reshape(in_shape)
    return (hidden + result).astype(jnp.bfloat16)

def plain_block(tokens, gains, w_qkv, w_proj, w_up, w_down, bias_table):
    levels, lat_rows, lon_cols, channels = tokens.shape
    normed = to_windows(layer_norm(tokens, gains[0]))
    keys_kept = jnp.ones(normed.shape[:2], dtype=bool)
    attended = attend_rows(normed, w_qkv, w_proj, bias_table, keys_kept, lon_cols // WLON)
    attended = from_windows(attended, levels, lat_rows, lon_cols)
    hidden = tokens.astype(jnp.float32) + attended.astype(jnp.float32)
    return feed_forward(hidden, gains[1], w_up, w_down)

def shifted_block(after_first, gains, w_qkv, w_proj, w_up, w_down, bias_table):
    levels, lat_rows, lon_cols, channels = after_first.shape
    normed = layer_norm(after_first, gains[0])
    rolled = jnp.roll(normed, SLON, axis=2)
    padded = jnp.pad(rolled, ((0, 0), (SLAT, SLAT), (0, 0), (0, 0)))
    row_index = lax.broadcasted_iota(jnp.int32, (levels, lat_rows + 2 * SLAT, lon_cols, 1), 1)
    inside = (row_index >= SLAT) & (row_index < lat_rows + SLAT)
    keys_kept = to_windows(inside)[..., 0]
    attended = attend_rows(to_windows(padded), w_qkv, w_proj, bias_table, keys_kept, lon_cols // WLON)
    attended = from_windows(attended, levels, lat_rows + 2 * SLAT, lon_cols)
    attended = jnp.roll(attended[:, SLAT:SLAT + lat_rows], -SLON, axis=2)
    hidden = after_first.astype(jnp.float32) + attended.astype(jnp.float32)
    return feed_forward(hidden, gains[1], w_up, w_down)

def reference(tokens, cotangent, norm_gains, w_qkv, w_proj, w_up, w_down, pos_bias):

    def forward(tokens, norm_gains, w_qkv, w_proj, w_up, w_down, pos_bias):
        after_first = plain_block(tokens, norm_gains[0], w_qkv[0], w_proj[0], w_up[0], w_down[0], pos_bias[0])
        return shifted_block(after_first, norm_gains[1], w_qkv[1], w_proj[1], w_up[1], w_down[1], pos_bias[1])
    _, pull_back = jax.vjp(forward, tokens, norm_gains, w_qkv, w_proj, w_up, w_down, pos_bias)
    grad_tokens, grad_gains, grad_qkv, grad_proj, grad_up, grad_down, grad_bias = pull_back(cotangent)
    matrix = jnp.concatenate([grad_qkv.astype(jnp.float32), grad_proj.astype(jnp.float32), grad_up.astype(jnp.float32), jnp.swapaxes(grad_down, 1, 2).astype(jnp.float32)], axis=2)
    remainder = jnp.concatenate([grad_bias.reshape(2, -1), grad_gains.reshape(2, -1)], axis=1)
    sum_squares = jnp.sum(matrix * matrix) + jnp.sum(remainder * remainder)
    ceiling = math.sqrt(24 * C * C + 2 * VECB)
    factor = jnp.minimum(1.0, ceiling / (jnp.sqrt(sum_squares) + 1e-06))
    return (grad_tokens, matrix * factor, remainder * factor)
```

```python
import functools
import math

import jax
import jax.numpy as jnp
import numpy as np
from jax import lax
from jax.experimental import pallas as pl
from jax.experimental.pallas import tpu as pltpu
from jax.sharding import PartitionSpec as P

C = 192
HEADS = 6
HEAD = 32
FFN = 768
WT = 144
NT = 576
NR = 640
QT = 160
MAIN = 112
VECB = 124800
BROWS = HEADS * WT
MROWS = 2304
OROWS = 880
GROWS = MROWS + OROWS
LOG2E = math.log2(math.e)
MESH = pl.DeviceIdType.MESH
BF = jnp.bfloat16
F32 = jnp.float32
VMEM_LIMIT = 56 * 1024 * 1024


def nat(l, r, c):
    return l * 288 + r * 48 + c


def one_hot(sources, width):
    mat = np.zeros((len(sources), width), np.float32)
    for i, s in enumerate(sources):
        if s >= 0:
            mat[i, s] = 1.0
    return mat


@functools.cache
def orders():
    win = [nat(l, r, 12 * w + c) for w in range(4) for l in range(2) for r in range(6) for c in range(12)]

    def cells(rows, cols, size):
        out = [nat(l, r, c) for l in range(2) for r in rows for c in cols]
        return out + [-1] * (size - len(out))

    top, low = range(0, 3), range(3, 6)
    send = []
    for rows in (top, low):
        send += cells(rows, range(0, 18), MAIN)
        send += cells(rows, range(42, 48), QT - MAIN)
        send += cells(rows, range(24, 42), MAIN)
        send += cells(rows, range(18, 24), QT - MAIN)
    slots = []
    for s in range(4):
        for l in range(2):
            for half in range(2):
                for r in range(3):
                    for cc in range(12):
                        col = 12 * (s % 2) + cc
                        base = QT * (2 * (s // 2) + half)
                        if col >= 6:
                            slots.append(base + (l * 3 + r) * 18 + col - 6)
                        else:
                            slots.append(base + MAIN + (l * 3 + r) * 6 + col)
    win_at = {n: i for i, n in enumerate(win)}
    send_win = [win_at[n] if n >= 0 else -1 for n in send]
    to_win = one_hot(win, NT)
    send_from_win = one_hot(send_win, NT)
    send_from_nat = one_hot(send, NT)
    to_slots = one_hot(slots, NR)
    return {
        "to_win": to_win,
        "to_nat": to_win.T.copy(),
        "send_win": send_from_win,
        "win_send": send_from_win.T.copy(),
        "send_nat": send_from_nat,
        "to_slots": to_slots,
        "from_slots": to_slots.T.copy(),
    }


def const(name):
    return jnp.asarray(orders()[name], BF)


def nn(a, b):
    return lax.dot_general(a, b, (((1,), (0,)), ((), ())), preferred_element_type=F32)


def nt(a, b):
    return lax.dot_general(a, b, (((1,), (1,)), ((), ())), preferred_element_type=F32)


def tn(a, b):
    return lax.dot_general(a, b, (((0,), (0,)), ((), ())), preferred_element_type=F32)


def shuffle(mat, x):
    return nn(mat, x).astype(BF)


def stats(x):
    center = x - jnp.mean(x, axis=-1, keepdims=True)
    r = lax.rsqrt(jnp.mean(center * center, axis=-1, keepdims=True) + 1e-05)
    return center * r, r


def norm_back(dn, gain, xhat, r):
    t = dn * gain
    return r * (t - jnp.mean(t, axis=-1, keepdims=True) - xhat * jnp.mean(t * xhat, axis=-1, keepdims=True))


def head_mask(h, dtype):
    lane = lax.broadcasted_iota(jnp.int32, (1, C), 1)
    return ((lane >= h * HEAD) & (lane < (h + 1) * HEAD)).astype(F32).astype(dtype)


def forward_windows(x_ref, gains, wq_ref, wproj_ref, wup_ref, wdown_ref, bias_of, q_ref, k_ref, v_ref, p_ref, mix_ref, hid_ref, a_ref, gp_ref, out_ref):
    g0, g1 = gains

    def window(w, carry):
        rows = pl.ds(pl.multiple_of(w * WT, WT), WT)
        x = x_ref[rows, :].astype(F32)
        u = (stats(x)[0] * g0).astype(BF)
        q = nn(u, wq_ref[0]).astype(BF)
        k = nn(u, wq_ref[1]).astype(BF)
        v = nn(u, wq_ref[2]).astype(BF)
        q_ref[rows, :] = q
        k_ref[rows, :] = k
        v_ref[rows, :] = v
        mixed = jnp.zeros((WT, C), F32)
        for h in range(HEADS):
            s = nt(q * head_mask(h, BF), k) * (HEAD ** -0.5 * LOG2E) + bias_of(w, h)
            e = jnp.exp2(s - jnp.max(s, axis=-1, keepdims=True))
            p = (e * (1.0 / jnp.sum(e, axis=-1, keepdims=True))).astype(BF)
            p_ref[pl.ds(pl.multiple_of(w * BROWS + h * WT, WT), WT), :] = p
            mixed = mixed + nn(p, v) * head_mask(h, F32)
        mixed = mixed.astype(BF)
        mix_ref[rows, :] = mixed
        attended = nn(mixed, wproj_ref[...]).astype(BF)
        hidden = x + attended.astype(F32)
        hid_ref[rows, :] = hidden
        n2 = (stats(hidden)[0] * g1).astype(BF)
        total = hidden
        for j in range(3):
            cols = slice(256 * j, 256 * j + 256)
            up = nn(n2, wup_ref[:, cols])
            cdf = 0.5 + 0.5 * lax.erf(up * (0.5 ** 0.5))
            slope = cdf + up * jnp.exp2(up * up * (-0.5 * LOG2E)) * (1.0 / math.sqrt(2 * math.pi))
            act = (up * cdf).astype(BF)
            a_ref[rows, cols] = act
            gp_ref[rows, cols] = slope.astype(BF)
            if out_ref is not None:
                total = total + nn(act, wdown_ref[cols, :])
        if out_ref is not None:
            out_ref[rows, :] = total.astype(BF)
        return carry

    lax.fori_loop(0, 4, window, 0)


def backward_windows(dout_ref, x_ref, gains, wq_ref, wproj_ref, wup_ref, wdown_ref, q_ref, k_ref, v_ref, p_ref, mix_ref, hid_ref, a_ref, gp_ref,
                     dbias_of, dg_ref, dup_ref, n2_ref, datt_ref, dq_ref, dk_ref, dv_ref, u_ref, dom_ref, qm_ref, ds_ref, dx_ref):
    g0, g1 = gains
    dg_ref[...] = jnp.zeros((2, C), F32)

    def window(w, carry):
        rows = pl.ds(pl.multiple_of(w * WT, WT), WT)
        dy = dout_ref[rows, :]
        dn2 = jnp.zeros((WT, C), F32)
        for j in range(3):
            cols = slice(256 * j, 256 * j + 256)
            da = nt(dy, wdown_ref[cols, :]).astype(BF).astype(F32)
            dup = (da * gp_ref[rows, cols].astype(F32)).astype(BF)
            dup_ref[rows, cols] = dup
            dn2 = dn2 + nt(dup, wup_ref[:, cols])
        dn2 = dn2.astype(BF).astype(F32)
        xhat, r = stats(hid_ref[rows, :])
        n2_ref[rows, :] = (xhat * g1).astype(BF)
        dg_ref[1:2, :] += jnp.sum(dn2 * xhat, axis=0, keepdims=True)
        dhid = dy.astype(F32) + norm_back(dn2, g1, xhat, r)
        datt = dhid.astype(BF)
        datt_ref[rows, :] = datt
        dmix = nt(datt, wproj_ref[...]).astype(BF)
        q = q_ref[rows, :]
        k = k_ref[rows, :]
        v = v_ref[rows, :]
        dq = jnp.zeros((WT, C), F32)
        for h in range(HEADS):
            part = slice(h * WT, h * WT + WT)
            prow = pl.ds(pl.multiple_of(w * BROWS + h * WT, WT), WT)
            dom = dmix * head_mask(h, BF)
            dom_ref[part, :] = dom
            qm_ref[part, :] = q * head_mask(h, BF)
            dp = nt(dom, v)
            p = p_ref[prow, :].astype(F32)
            t = p * dp
            ds = t - p * jnp.sum(t, axis=-1, keepdims=True)
            dbias_of(w, h, ds)
            dsb = ds.astype(BF)
            ds_ref[part, :] = dsb
            dq = dq + nn(dsb, k) * head_mask(h, F32)
        pw = p_ref[pl.ds(pl.multiple_of(w * BROWS, WT), BROWS), :]
        dq = (dq * HEAD ** -0.5).astype(BF)
        dk = (tn(ds_ref[...], qm_ref[...]) * HEAD ** -0.5).astype(BF)
        dv = tn(pw, dom_ref[...]).astype(BF)
        dq_ref[rows, :] = dq
        dk_ref[rows, :] = dk
        dv_ref[rows, :] = dv
        du = nt(dq, wq_ref[0]) + nt(dk, wq_ref[1]) + nt(dv, wq_ref[2])
        du = du.astype(BF).astype(F32)
        xhat, r = stats(x_ref[rows, :].astype(F32))
        u_ref[rows, :] = (xhat * g0).astype(BF)
        dg_ref[0:1, :] += jnp.sum(du * xhat, axis=0, keepdims=True)
        dx = norm_back(du, g0, xhat, r).astype(BF).astype(F32) + datt.astype(F32)
        dx_ref[rows, :] = dx.astype(BF)
        return carry

    lax.fori_loop(0, 4, window, 0)


def split_qkv(wqkv_ref, wq_ref):
    for i in range(3):
        wq_ref[i] = wqkv_ref[:, C * i:C * i + C]


def weight_products(emit, u, n2, mix, dout, dq_ref, dk_ref, dv_ref, datt_ref, dup_ref, a_ref):
    emit(0, tn(dq_ref[...], u))
    emit(192, tn(dk_ref[...], u))
    emit(384, tn(dv_ref[...], u))
    emit(576, tn(datt_ref[...], mix))
    for j in range(3):
        cols = slice(256 * j, 256 * j + 256)
        emit(768 + 256 * j, tn(dup_ref[:, cols], n2))
    for j in range(3):
        cols = slice(256 * j, 256 * j + 256)
        emit(1536 + 256 * j, tn(a_ref[:, cols], dout))


def first_forward(tok_ref, cot_ref, gains_ref, wqkv_ref, wproj_ref, wup_ref, wdown_ref, bias_ref, to_win_ref, send_win_ref, send_nat_ref,
                  x_ref, q_ref, k_ref, v_ref, p_ref, mix_ref, hid_ref, a_ref, gp_ref, send_ref, wq_ref, lbias_ref, out_ref):
    x_ref[...] = shuffle(to_win_ref[...], tok_ref[...])
    split_qkv(wqkv_ref, wq_ref)
    lbias_ref[...] = bias_ref[...] * LOG2E
    gains = (gains_ref[0:1, :], gains_ref[1:2, :])

    def bias_of(w, h):
        return lbias_ref[h * WT:h * WT + WT, :]

    forward_windows(x_ref, gains, wq_ref, wproj_ref, wup_ref, wdown_ref, bias_of, q_ref, k_ref, v_ref, p_ref, mix_ref, hid_ref, a_ref, gp_ref, out_ref)
    send_ref[:, 0:C] = shuffle(send_win_ref[...], out_ref[...])
    send_ref[:, C:2 * C] = shuffle(send_nat_ref[...], cot_ref[...])


def whole(shape):
    return pl.BlockSpec(shape, lambda i: (0,) * len(shape))


def block_of(shape, b):
    return pl.BlockSpec((pl.squeezed,) + shape, lambda i: (b,) + (0,) * len(shape))


def params(**kw):
    return pltpu.CompilerParams(vmem_limit_bytes=VMEM_LIMIT, **kw)


def weight_specs(b):
    return [block_of((2, C), b), block_of((C, 3 * C), b), block_of((C, C), b), block_of((C, FFN), b), block_of((FFN, C), b), block_of((BROWS, WT), b)]


RESIDUALS = [((NT, C), BF), ((NT, C), BF), ((NT, C), BF), ((NT, C), BF), ((4 * BROWS, WT), BF), ((NT, C), BF), ((NT, C), F32), ((NT, FFN), BF), ((NT, FFN), BF)]


def run_first_forward(tok, cot, weights):
    perms = [const("to_win"), const("send_win"), const("send_nat")]
    outs = RESIDUALS + [((NR, 2 * C), BF)]
    return pl.pallas_call(
        first_forward,
        grid=(1,),
        in_specs=[whole((NT, C)), whole((NT, C))] + weight_specs(0) + [whole(p.shape) for p in perms],
        out_specs=[whole(s) for s, _ in outs],
        out_shape=[jax.ShapeDtypeStruct(s, d) for s, d in outs],
        scratch_shapes=[pltpu.VMEM((3, C, C), BF), pltpu.VMEM((BROWS, WT), F32), pltpu.VMEM((NT, C), BF)],
        compiler_params=params(),
        name="first_forward",
    )(tok, cot, *weights, *perms)


BACK_SCRATCH = [
    pltpu.VMEM((2, C), F32), pltpu.VMEM((NT, FFN), BF), pltpu.VMEM((NT, C), BF), pltpu.VMEM((NT, C), BF),
    pltpu.VMEM((NT, C), BF), pltpu.VMEM((NT, C), BF), pltpu.VMEM((NT, C), BF), pltpu.VMEM((NT, C), BF),
    pltpu.VMEM((BROWS, C), BF), pltpu.VMEM((BROWS, C), BF), pltpu.VMEM((BROWS, WT), BF), pltpu.VMEM((NT, C), BF),
]


def half_of(shape, axis):
    return (lax.broadcasted_iota(jnp.int32, shape, axis) // 36) % 2


def lane_moves(low):
    src = lax.broadcasted_iota(jnp.int32, (WT, WT), 0)
    dst = lax.broadcasted_iota(jnp.int32, (WT, WT), 1)
    keep = dst - 36 * ((dst // 36) % 2) + (0 if low else 36)
    return (src == keep).astype(F32)


def polar_bias(table, low):
    moved = jnp.dot(table, lane_moves(low), precision=lax.Precision.HIGHEST, preferred_element_type=F32)
    half = half_of((WT, WT), 0)
    if low:
        moved = jnp.where(half == 0, moved, pltpu.roll(moved, 36, 0))
    else:
        moved = jnp.where(half == 1, moved, pltpu.roll(moved, WT - 36, 0))
    return jnp.where(half == half_of((WT, WT), 1), moved, -1e30)


def polar_back(grad, low):
    half = half_of((WT, WT), 0)
    if low:
        folded = jnp.where(half == 0, grad + pltpu.roll(grad, WT - 36, 0), 0.0)
    else:
        folded = jnp.where(half == 1, grad + pltpu.roll(grad, 36, 0), 0.0)
    return lax.dot_general(folded, lane_moves(low), (((1,), (1,)), ((), ())), precision=lax.Precision.HIGHEST, preferred_element_type=F32)


def second_block(band_ref, recv_ref, gains_ref, wqkv_ref, wproj_ref, wup_ref, wdown_ref, bias_ref, to_slots_ref, from_slots_ref,
                 back_ref, grad_ref, dbias_ref, dg_ref,
                 wq_ref, lbias_ref, q_ref, k_ref, v_ref, p_ref, mix_ref, hid_ref, a_ref, gp_ref, x_ref, cot_ref,
                 dgs_ref, dup_ref, n2_ref, datt_ref, dq_ref, dk_ref, dv_ref, u_ref, dom_ref, qm_ref, ds_ref, dx_ref, dbs_ref):
    x_ref[...] = shuffle(to_slots_ref[...], recv_ref[:, 0:C])
    cot_ref[...] = shuffle(to_slots_ref[...], recv_ref[:, C:2 * C])
    split_qkv(wqkv_ref, wq_ref)
    band = band_ref[0]
    gains = (gains_ref[0:1, :], gains_ref[1:2, :])
    for group in range(2):
        polar = band == (0 if group == 0 else 3)

        @pl.when(polar)
        def _():
            for h in range(HEADS):
                rows = slice(h * WT, h * WT + WT)
                lbias_ref[group, rows, :] = polar_bias(bias_ref[rows, :] * LOG2E, group == 1)

        @pl.when(jnp.logical_not(polar))
        def _():
            lbias_ref[group] = bias_ref[...] * LOG2E

    dbs_ref[...] = jnp.zeros((2, BROWS, WT), F32)

    def bias_of(w, h):
        return lbias_ref[w // 2, h * WT:h * WT + WT, :]

    def dbias_of(w, h, ds):
        dbs_ref[w // 2, h * WT:h * WT + WT, :] += ds

    forward_windows(x_ref, gains, wq_ref, wproj_ref, wup_ref, wdown_ref, bias_of, q_ref, k_ref, v_ref, p_ref, mix_ref, hid_ref, a_ref, gp_ref, None)
    backward_windows(cot_ref, x_ref, gains, wq_ref, wproj_ref, wup_ref, wdown_ref, q_ref, k_ref, v_ref, p_ref, mix_ref, hid_ref, a_ref, gp_ref,
                     dbias_of, dgs_ref, dup_ref, n2_ref, datt_ref, dq_ref, dk_ref, dv_ref, u_ref, dom_ref, qm_ref, ds_ref, dx_ref)
    back_ref[...] = shuffle(from_slots_ref[...], dx_ref[...])
    dg_ref[...] = dgs_ref[...]
    for group in range(2):
        polar = band == (0 if group == 0 else 3)

        @pl.when(polar)
        def _():
            for h in range(HEADS):
                rows = slice(h * WT, h * WT + WT)
                dbs_ref[group, rows, :] = polar_back(dbs_ref[group, rows, :], group == 1)

    dbias_ref[...] = dbs_ref[0] + dbs_ref[1]

    def shifted(ref):
        return jnp.concatenate([jnp.zeros((NT, 64), BF), ref[...]], axis=1)

    def emit(row, value):
        grad_ref[row:row + value.shape[0], :] = value.astype(BF)

    weight_products(emit, shifted(u_ref), shifted(n2_ref), shifted(mix_ref), shifted(cot_ref), dq_ref, dk_ref, dv_ref, datt_ref, dup_ref, a_ref)


def run_second_block(band, recv, weights):
    perms = [const("to_slots"), const("from_slots")]
    outs = [((NR, C), BF), ((MROWS, 256), BF), ((BROWS, WT), F32), ((2, C), F32)]
    fwd_scratch = [pltpu.VMEM(s, d) for s, d in RESIDUALS[1:]]
    return pl.pallas_call(
        second_block,
        grid=(1,),
        in_specs=[pl.BlockSpec(memory_space=pltpu.SMEM), whole((NR, 2 * C))] + weight_specs(1) + [whole(p.shape) for p in perms],
        out_specs=[whole(s) for s, _ in outs],
        out_shape=[jax.ShapeDtypeStruct(s, d) for s, d in outs],
        scratch_shapes=[pltpu.VMEM((3, C, C), BF), pltpu.VMEM((2, BROWS, WT), F32)] + fwd_scratch
        + [pltpu.VMEM((NT, C), BF), pltpu.VMEM((NT, C), BF)] + BACK_SCRATCH + [pltpu.VMEM((2, BROWS, WT), F32)],
        compiler_params=params(),
        name="second_block",
    )(band, recv, *weights, *perms)


def first_backward(ret_ref, gains_ref, wqkv_ref, wproj_ref, wup_ref, wdown_ref, bias_ref, x_ref, q_ref, k_ref, v_ref, p_ref, mix_ref, hid_ref,
                   a_ref, gp_ref, grad2_ref, dbias2_ref, dg2_ref, win_send_ref, to_nat_ref,
                   gtok_ref, grad_ref,
                   wq_ref, dout_ref, dg_ref, dup_ref, n2_ref, datt_ref, dq_ref, dk_ref, dv_ref, u_ref, dom_ref, qm_ref, ds_ref, dx_ref, dbs_ref):
    dout_ref[...] = shuffle(win_send_ref[...], ret_ref[...])
    split_qkv(wqkv_ref, wq_ref)
    gains = (gains_ref[0:1, :], gains_ref[1:2, :])
    dbs_ref[...] = jnp.zeros((BROWS, WT), F32)

    def dbias_of(w, h, ds):
        dbs_ref[h * WT:h * WT + WT, :] += ds

    backward_windows(dout_ref, x_ref, gains, wq_ref, wproj_ref, wup_ref, wdown_ref, q_ref, k_ref, v_ref, p_ref, mix_ref, hid_ref, a_ref, gp_ref,
                     dbias_of, dg_ref, dup_ref, n2_ref, datt_ref, dq_ref, dk_ref, dv_ref, u_ref, dom_ref, qm_ref, ds_ref, dx_ref)
    gtok_ref[...] = shuffle(to_nat_ref[...], dx_ref[...])

    def widened(ref):
        return jnp.concatenate([ref[...], jnp.zeros((NT, 64), BF)], axis=1)

    def emit(row, value):
        rows = slice(row, row + value.shape[0])
        other = grad2_ref[rows, :]
        grad_ref[rows, 0:128] = value[:, 0:128].astype(BF)
        grad_ref[rows, 128:256] = (value[:, 128:256] + other[:, 0:128].astype(F32)).astype(BF)
        grad_ref[rows, 256:384] = other[:, 128:256]

    weight_products(emit, widened(u_ref), widened(n2_ref), widened(mix_ref), widened(dout_ref), dq_ref, dk_ref, dv_ref, datt_ref, dup_ref, a_ref)
    pad = jnp.zeros((BROWS, 384 - 2 * WT), F32)
    grad_ref[MROWS:MROWS + BROWS, :] = jnp.concatenate([dbs_ref[...], dbias2_ref[...], pad], axis=1).astype(BF)

    def gain_rows(ref):
        flat = jnp.concatenate([ref[0:1, :], ref[1:2, :], jnp.zeros((1, 3 * WT - 2 * C), F32)], axis=1)
        return jnp.concatenate([flat[:, 0:WT], flat[:, WT:2 * WT], flat[:, 2 * WT:3 * WT]], axis=0)

    gains_out = jnp.concatenate([gain_rows(dg_ref), gain_rows(dg2_ref), jnp.zeros((3, 384 - 2 * WT), F32)], axis=1)
    grad_ref[MROWS + BROWS:GROWS, :] = jnp.concatenate([gains_out, jnp.zeros((GROWS - MROWS - BROWS - 3, 384), F32)], axis=0).astype(BF)


def run_first_backward(ret, weights, residuals, grad2, dbias2, dg2):
    perms = [const("win_send"), const("to_nat")]
    outs = [((NT, C), BF), ((GROWS, 384), BF)]
    extra = [grad2, dbias2, dg2]
    return pl.pallas_call(
        first_backward,
        grid=(1,),
        in_specs=[whole((NR, C))] + weight_specs(0) + [whole(s) for s, _ in RESIDUALS] + [whole(e.shape) for e in extra] + [whole(p.shape) for p in perms],
        out_specs=[whole(s) for s, _ in outs],
        out_shape=[jax.ShapeDtypeStruct(s, d) for s, d in outs],
        scratch_shapes=[pltpu.VMEM((3, C, C), BF), pltpu.VMEM((NT, C), BF)] + BACK_SCRATCH + [pltpu.VMEM((BROWS, WT), F32)],
        compiler_params=params(),
        name="first_backward",
    )(ret, *weights, *residuals, *extra, *perms)


def greet(peers, count):
    barrier = pltpu.get_barrier_semaphore()
    for cond, dev in peers:
        if cond is None:
            pl.semaphore_signal(barrier, inc=1, device_id=dev, device_id_type=MESH)
        else:
            @pl.when(cond)
            def _():
                pl.semaphore_signal(barrier, inc=1, device_id=dev, device_id_type=MESH)
    pl.semaphore_wait(barrier, count)


def exchange(moves_of, nlat, nlon, src, dst, send_sem, recv_sem, local_sem):
    b = lax.axis_index("lat")
    j = lax.axis_index("lon")
    east, west = lax.rem(j + 1, nlon), lax.rem(j + nlon - 1, nlon)
    up, down = jnp.maximum(b - 1, 0), jnp.minimum(b + 1, nlat - 1)
    first, last = b == 0, b == nlat - 1
    inner_up, inner_down = b > 0, b < nlat - 1
    greet([(None, (b, east)), (None, (b, west)), (inner_up, (up, j)), (inner_down, (down, j)), (inner_up, (up, east)), (inner_down, (down, west))], jnp.where(jnp.logical_or(first, last), 4, 6))
    sends, locals_, recvs = moves_of(b, j, east, west, up, down, first, last, inner_up, inner_down)

    def remote(i, s, d, size, dev):
        return pltpu.make_async_remote_copy(src_ref=src.at[pl.ds(s, size), :], dst_ref=dst.at[pl.ds(d, size), :], send_sem=send_sem.at[i], recv_sem=recv_sem.at[i], device_id=dev, device_id_type=MESH)

    def local(i, s, d, size):
        return pltpu.make_async_copy(src.at[pl.ds(s, size), :], dst.at[pl.ds(d, size), :], local_sem.at[i])

    def guarded(cond, act):
        if cond is None:
            act()
        else:
            pl.when(cond)(act)

    for i, cond, s, d, size, dev in sends:
        guarded(cond, lambda: remote(i, s, d, size, dev).start())
    for i, (cond, s, d, size) in enumerate(locals_):
        guarded(cond, lambda: local(i, s, d, size).start())
    for i, cond, d, size in recvs:
        guarded(cond, lambda: remote(i, 0, d, size, (b, east)).wait_recv())
    for i, (cond, s, d, size) in enumerate(locals_):
        guarded(cond, lambda: local(i, s, d, size).wait())
    for i, cond, s, d, size, dev in sends:
        guarded(cond, lambda: remote(i, s, d, size, dev).wait_send())


def moves_out(b, j, east, west, up, down, first, last, inner_up, inner_down):
    sends = [
        (0, None, 432, 432, 48, (b, east)),
        (1, inner_up, 112, 592, 48, (up, east)),
        (2, first, 112, 112, 48, (b, east)),
        (3, inner_up, 0, 480, 112, (up, j)),
        (4, inner_down, 480, 0, 160, (down, j)),
    ]
    locals_ = [(None, 160, 160, 272), (first, 0, 0, 112), (last, 480, 480, 160)]
    recvs = [(0, None, 432, 48), (1, inner_down, 592, 48), (2, first, 112, 48), (3, inner_down, 480, 112), (4, inner_up, 0, 160)]
    return sends, locals_, recvs


def moves_back(b, j, east, west, up, down, first, last, inner_up, inner_down):
    sends = [
        (0, None, 432, 432, 48, (b, west)),
        (1, inner_down, 592, 112, 48, (down, west)),
        (2, first, 112, 112, 48, (b, west)),
        (3, inner_down, 480, 0, 112, (down, j)),
        (4, inner_up, 0, 480, 160, (up, j)),
    ]
    locals_ = [(None, 160, 160, 272), (first, 0, 0, 112), (last, 480, 480, 160)]
    recvs = [(0, None, 432, 48), (1, inner_up, 112, 48), (2, first, 112, 48), (3, inner_up, 0, 112), (4, inner_down, 480, 160)]
    return sends, locals_, recvs


def run_exchange(x, moves, nlat, nlon, ident):
    return pl.pallas_call(
        functools.partial(exchange, moves, nlat, nlon),
        in_specs=[pl.BlockSpec(memory_space=pl.ANY)],
        out_specs=pl.BlockSpec(memory_space=pl.ANY),
        out_shape=jax.ShapeDtypeStruct(x.shape, x.dtype),
        scratch_shapes=[pltpu.SemaphoreType.DMA((5,)), pltpu.SemaphoreType.DMA((5,)), pltpu.SemaphoreType.DMA((3,))],
        compiler_params=pltpu.CompilerParams(collective_id=ident, has_side_effects=True),
        name="exchange_out" if ident == 1 else "exchange_back",
    )(x)


def lat_row(lat):
    return ((650 * lat) // 48) * 16


def lon_row(lat, z):
    return ((1300 * lat + 325 * z) // 96) * 16


def x_row(lat, z, x):
    return ((5200 * lat + 1300 * z + 325 * x) // 384) * 16


def al(v):
    return pl.multiple_of(v, 16)


def reduce_kernel(g_ref, m_ref, o_ref, got_core, sum_core, got_z, sum_z, got_y, sum_y, got_x, sum_x, got_l, parts, send_sem, recv_sem):
    lat = lax.axis_index("lat")
    lon = lax.axis_index("lon")
    yh, core = lat // 2, lat % 2
    z, x, yl = lon // 8, (lon // 2) % 4, lon % 2

    def device(yh_, core_, z_, x_, yl_):
        return (yh_ * 2 + core_, z_ * 8 + x_ * 2 + yl_)

    plane = [(dz, dx) for dz in range(4) for dx in range(4) if (dz, dx) != (0, 0)]
    plane_dev = [device(yh, core, (z + dz) % 4, (x + dx) % 4, yl) for dz, dx in plane]
    cube = [(a, c, e) for a in range(2) for c in range(2) for e in range(2) if (a, c, e) != (0, 0, 0)]
    cube_dev = [device((yh + a) % 2, (core + c) % 2, z, x, (yl + e) % 2) for a, c, e in cube]
    greet([(None, d) for d in plane_dev + cube_dev], 22)

    def remote(i, s, d, dev):
        return pltpu.make_async_remote_copy(src_ref=s, dst_ref=d, send_sem=send_sem.at[i], recv_sem=recv_sem.at[i], device_id=dev, device_id_type=MESH)

    def total(*terms):
        out = terms[0].astype(F32)
        for t in terms[1:]:
            out = out + t.astype(F32)
        return out

    pal = device(yh, 1 - core, z, x, yl)
    copies = []
    for h in range(2):
        other = 2 * h + 1 - core
        copies.append(remote(2 * h, g_ref.at[pl.ds(al(576 * other), 576), :], got_core.at[h, pl.ds(0, 576), :], pal))
        copies.append(remote(2 * h + 1, g_ref.at[pl.ds(al(MROWS + lat_row(other)), 240), :], got_core.at[h, pl.ds(576, 240), :], pal))
    for c in copies:
        c.start()
    for c in copies:
        c.wait()
    for h in range(2):
        mine = 2 * h + core
        for t in range(4):
            rows = slice(144 * t, 144 * t + 144)
            sum_core[h, rows, :] = total(g_ref[pl.ds(al(576 * mine + 144 * t), 144), :], got_core[h, rows, :]).astype(BF)
        sum_core[h, 576:816, :] = total(g_ref[pl.ds(al(MROWS + lat_row(mine)), 240), :], got_core[h, 576:816, :]).astype(BF)

    copies = []
    for dz in range(1, 4):
        z_ = (z + dz) % 4
        dev = device(yh, core, z_, x, yl)
        i = 4 + 3 * (dz - 1)
        copies.append(remote(i, sum_core.at[:, pl.ds(al(144 * z_), 144), :], got_z.at[dz - 1, :, pl.ds(0, 144), :], dev))
        for h in range(2):
            lt = 2 * h + core
            copies.append(remote(i + 1 + h, sum_core.at[h, pl.ds(al(576 + lon_row(lt, z_) - lat_row(lt)), 80), :], got_z.at[dz - 1, h, pl.ds(144, 80), :], dev))
    for c in copies:
        c.start()
    for c in copies:
        c.wait()
    for h in range(2):
        lt = 2 * h + core
        own = sum_core[h, pl.ds(al(144 * z), 144), :]
        sum_z[h, 0:144, :] = total(own, *[got_z[t, h, 0:144, :] for t in range(3)]).astype(BF)
        own = sum_core[h, pl.ds(al(576 + lon_row(lt, z) - lat_row(lt)), 80), :]
        sum_z[h, 144:224, :] = total(own, *[got_z[t, h, 144:224, :] for t in range(3)]).astype(BF)

    c = remote(13, sum_z.at[1 - yh], got_y, device(1 - yh, core, z, x, yl))
    c.start()
    c.wait()
    sum_y[...] = total(sum_z[yh], got_y[...]).astype(BF)

    copies = []
    for dx in range(1, 4):
        x_ = (x + dx) % 4
        dev = device(yh, core, z, x_, yl)
        i = 14 + 2 * (dx - 1)
        copies.append(remote(i, sum_y.at[pl.ds(al(32 * x_), 48), :], got_x.at[dx - 1, pl.ds(0, 48), :], dev))
        copies.append(remote(i + 1, sum_y.at[pl.ds(al(144 + x_row(lat, z, x_) - lon_row(lat, z)), 32), :], got_x.at[dx - 1, pl.ds(48, 32), :], dev))
    for c in copies:
        c.start()
    for c in copies:
        c.wait()
    own = sum_y[pl.ds(al(32 * x), 48), :]
    sum_x[0:48, :] = total(own, *[got_x[t, 0:48, :] for t in range(3)]).astype(BF)
    own = sum_y[pl.ds(al(144 + x_row(lat, z, x) - lon_row(lat, z)), 32), :]
    sum_x[48:80, :] = total(own, *[got_x[t, 48:80, :] for t in range(3)]).astype(BF)

    c = remote(20, sum_x, got_l, device(yh, core, z, x, 1 - yl))
    c.start()
    c.wait()
    final = total(sum_x[...], got_l[...])
    matrix, other = final[0:48, :], final[48:80, :]

    first_row = 4 * x + 18 * yl
    row = lax.broadcasted_iota(jnp.int32, (48, 384), 0)
    squares = jnp.where((row >= first_row) & (row < first_row + 18), matrix * matrix, 0.0)
    lane = lax.broadcasted_iota(jnp.int32, (32, 384), 1)
    row = lax.broadcasted_iota(jnp.int32, (32, 384), 0)
    index = (row + x_row(lat, z, x)) * WT + lane - jnp.where(lane >= WT, WT, 0)
    low = 975 * (32 * lat + lon)
    inside = (index >= low) & (index < low + 975) & (lane < 2 * WT)
    squares = jnp.sum(squares, axis=0, keepdims=True) + jnp.sum(jnp.where(inside, other * other, 0.0), axis=0, keepdims=True)
    mine = jnp.sum(squares, axis=1, keepdims=True)

    parts[0] = jnp.broadcast_to(mine, (8, 128))
    copies = [remote(21 + t, parts.at[0], parts.at[1 + t], plane_dev[t]) for t in range(15)]
    for c in copies:
        c.start()
    for c in copies:
        c.wait()
    acc = parts[0]
    for t in range(15):
        acc = acc + parts[1 + t]
    parts[16] = acc
    copies = [remote(36 + t, parts.at[16], parts.at[17 + t], cube_dev[t]) for t in range(7)]
    for c in copies:
        c.start()
    for c in copies:
        c.wait()
    for t in range(7):
        acc = acc + parts[17 + t]
    ceiling = math.sqrt(24 * C * C + 2 * VECB)
    factor = jnp.minimum(1.0, ceiling / (jnp.sqrt(acc) + 1e-06))[0:1, 0:1]
    m_ref[...] = matrix * factor
    o_ref[...] = other * factor


def run_reduce(g):
    slots = 43
    return pl.pallas_call(
        reduce_kernel,
        in_specs=[pl.BlockSpec(memory_space=pltpu.VMEM)],
        out_specs=[pl.BlockSpec(memory_space=pltpu.VMEM)] * 2,
        out_shape=[jax.ShapeDtypeStruct((48, 384), F32), jax.ShapeDtypeStruct((32, 384), F32)],
        scratch_shapes=[
            pltpu.VMEM((2, 816, 384), BF), pltpu.VMEM((2, 816, 384), BF),
            pltpu.VMEM((3, 2, 224, 384), BF), pltpu.VMEM((2, 224, 384), BF),
            pltpu.VMEM((224, 384), BF), pltpu.VMEM((224, 384), BF),
            pltpu.VMEM((3, 80, 384), BF), pltpu.VMEM((80, 384), BF), pltpu.VMEM((80, 384), BF),
            pltpu.VMEM((24, 8, 128), F32),
            pltpu.SemaphoreType.DMA((slots,)), pltpu.SemaphoreType.DMA((slots,)),
        ],
        compiler_params=params(collective_id=3, has_side_effects=True),
        name="reduce_gradient",
    )(g)


def compute_part(nlat, nlon, tokens, cotangent, norm_gains, w_qkv, w_proj, w_up, w_down, pos_bias):
    weights = (norm_gains, w_qkv, w_proj, w_up, w_down, pos_bias.reshape(2, BROWS, WT))
    band = lax.axis_index("lat").astype(jnp.int32).reshape(1)
    *residuals, send = run_first_forward(tokens.reshape(NT, C), cotangent.reshape(NT, C), weights)
    recv = run_exchange(send, moves_out, nlat, nlon, 1)
    back, grad2, dbias2, dg2 = run_second_block(band, recv, weights)
    ret = run_exchange(back, moves_back, nlat, nlon, 2)
    gtok, grad = run_first_backward(ret, weights, residuals, grad2, dbias2, dg2)
    return gtok.reshape(tokens.shape), grad


def shards(nlat, nlon, *args):
    gtok, grad = compute_part(nlat, nlon, *args)
    m, o = run_reduce(grad)
    lat, lon = lax.axis_index("lat"), lax.axis_index("lon")
    z, x, yl = lon // 8, (lon // 2) % 4, lon % 2
    m = lax.dynamic_slice_in_dim(m, 4 * x + 18 * yl, 18, axis=0)
    matrix = m.reshape(18, 2, C).transpose(1, 2, 0)
    flat = o[:, :2 * WT].reshape(32, 2, WT).transpose(1, 0, 2).reshape(2, 32 * WT)
    other = lax.dynamic_slice_in_dim(flat, 975 * (32 * lat + lon) - x_row(lat, z, x) * WT, 975, axis=1)
    return gtok, matrix, other


def solution(mesh):
    grid = P(None, "lat", "lon", None)
    return jax.shard_map(
        functools.partial(shards, mesh.shape["lat"], mesh.shape["lon"]),
        mesh=mesh,
        in_specs=(grid, grid) + (P(),) * 6,
        out_specs=(grid, P(None, None, ("lat", "lon")), P(None, ("lat", "lon"))),
        check_vma=False,
    )
```

```python
import functools
import math
import types

import jax
import jax.numpy as jnp
import numpy as np
from jax import lax
from jax.experimental import pallas as pl
from jax.experimental.pallas import tpu as pltpu
from jax.sharding import PartitionSpec as P

C = 192
HEADS = 6
HEAD = 32
FFN = 768
WT = 144
NT = 576
NR = 640
QT = 160
MAIN = 112
VECB = 124800
BROWS = HEADS * WT
MROWS = 2304
OROWS = 880
GROWS = MROWS + OROWS
LOG2E = math.log2(math.e)
MESH = pl.DeviceIdType.MESH
BF = jnp.bfloat16
F32 = jnp.float32
VMEM_LIMIT = 56 * 1024 * 1024


def nat(l, r, c):
    return l * 288 + r * 48 + c


def one_hot(sources, width):
    mat = np.zeros((len(sources), width), np.float32)
    for i, s in enumerate(sources):
        if s >= 0:
            mat[i, s] = 1.0
    return mat


@functools.cache
def orders():
    win = [nat(l, r, 12 * w + c) for w in range(4) for l in range(2) for r in range(6) for c in range(12)]

    def cells(rows, cols, size):
        out = [nat(l, r, c) for l in range(2) for r in rows for c in cols]
        return out + [-1] * (size - len(out))

    top, low = range(0, 3), range(3, 6)
    send = []
    for rows in (top, low):
        send += cells(rows, range(0, 18), MAIN)
        send += cells(rows, range(42, 48), QT - MAIN)
        send += cells(rows, range(24, 42), MAIN)
        send += cells(rows, range(18, 24), QT - MAIN)
    slots = []
    for s in range(4):
        for l in range(2):
            for half in range(2):
                for r in range(3):
                    for cc in range(12):
                        col = 12 * (s % 2) + cc
                        base = QT * (2 * (s // 2) + half)
                        if col >= 6:
                            slots.append(base + (l * 3 + r) * 18 + col - 6)
                        else:
                            slots.append(base + MAIN + (l * 3 + r) * 6 + col)
    win_at = {n: i for i, n in enumerate(win)}
    send_win = [win_at[n] if n >= 0 else -1 for n in send]
    to_win = one_hot(win, NT)
    send_from_win = one_hot(send_win, NT)
    send_from_nat = one_hot(send, NT)
    to_slots = one_hot(slots, NR)
    return {
        "to_win": to_win,
        "to_nat": to_win.T.copy(),
        "send_win": send_from_win,
        "win_send": send_from_win.T.copy(),
        "send_nat": send_from_nat,
        "to_slots": to_slots,
        "from_slots": to_slots.T.copy(),
    }


def const(name):
    return jnp.asarray(orders()[name], BF)


def nn(a, b):
    return lax.dot_general(a, b, (((1,), (0,)), ((), ())), preferred_element_type=F32)


def nt(a, b):
    return lax.dot_general(a, b, (((1,), (1,)), ((), ())), preferred_element_type=F32)


def tn(a, b):
    return lax.dot_general(a, b, (((0,), (0,)), ((), ())), preferred_element_type=F32)


def shuffle(mat, x):
    return nn(mat, x).astype(BF)


def stats(x):
    center = x - jnp.mean(x, axis=-1, keepdims=True)
    r = lax.rsqrt(jnp.mean(center * center, axis=-1, keepdims=True) + 1e-05)
    return center * r, r


def norm_back(dn, gain, xhat, r):
    t = dn * gain
    return r * (t - jnp.mean(t, axis=-1, keepdims=True) - xhat * jnp.mean(t * xhat, axis=-1, keepdims=True))


def head_mask(h, dtype):
    lane = lax.broadcasted_iota(jnp.int32, (1, C), 1)
    return ((lane >= h * HEAD) & (lane < (h + 1) * HEAD)).astype(F32).astype(dtype)


def forward_windows(t, b, bias_of, last):
    g0, g1 = t.gains[b, 0:1, :], t.gains[b, 1:2, :]

    def window(w, carry):
        rows = pl.ds(pl.multiple_of(w * WT, WT), WT)
        x = t.x[rows, :].astype(F32)
        u = (stats(x)[0] * g0).astype(BF)
        q = nn(u, t.wq[0]).astype(BF)
        k = nn(u, t.wq[1]).astype(BF)
        v = nn(u, t.wq[2]).astype(BF)
        t.q[rows, :] = q
        t.k[rows, :] = k
        t.v[rows, :] = v
        mixed = jnp.zeros((WT, C), F32)
        for h in range(HEADS):
            s = nt(q * head_mask(h, BF), k) * (HEAD ** -0.5 * LOG2E) + bias_of(w, h)
            e = jnp.exp2(s - jnp.max(s, axis=-1, keepdims=True))
            p = (e * (1.0 / jnp.sum(e, axis=-1, keepdims=True))).astype(BF)
            t.p[pl.ds(pl.multiple_of(w * BROWS + h * WT, WT), WT), :] = p
            mixed = mixed + nn(p, v) * head_mask(h, F32)
        mixed = mixed.astype(BF)
        t.mix[rows, :] = mixed
        attended = nn(mixed, t.w_proj[b]).astype(BF)
        hidden = x + attended.astype(F32)
        t.hid[rows, :] = hidden
        n2 = (stats(hidden)[0] * g1).astype(BF)
        total = hidden
        for j in range(3):
            cols = slice(256 * j, 256 * j + 256)
            up = nn(n2, t.w_up[b, :, cols])
            cdf = 0.5 + 0.5 * lax.erf(up * (0.5 ** 0.5))
            slope = cdf + up * jnp.exp2(up * up * (-0.5 * LOG2E)) * (1.0 / math.sqrt(2 * math.pi))
            act = (up * cdf).astype(BF)
            t.a[rows, cols] = act
            t.gp[rows, cols] = slope.astype(BF)
            if not last:
                total = total + nt(act, t.w_down[b, :, cols])
        if not last:
            t.out[rows, :] = total.astype(BF)
        return carry

    lax.fori_loop(0, 4, window, 0)


def backward_windows(t, b, dbias_of, after_window):
    g0, g1 = t.gains[b, 0:1, :], t.gains[b, 1:2, :]
    t.dg[...] = jnp.zeros((2, C), F32)

    def window(w, carry):
        rows = pl.ds(pl.multiple_of(w * WT, WT), WT)
        dy = t.dout[rows, :]
        dn2 = jnp.zeros((WT, C), F32)
        for j in range(3):
            cols = slice(256 * j, 256 * j + 256)
            da = nn(dy, t.w_down[b, :, cols]).astype(BF).astype(F32)
            dup = (da * t.gp[rows, cols].astype(F32)).astype(BF)
            t.dup[rows, cols] = dup
            dn2 = dn2 + nt(dup, t.w_up[b, :, cols])
        dn2 = dn2.astype(BF).astype(F32)
        xhat, r = stats(t.hid[rows, :])
        t.n2[rows, :] = (xhat * g1).astype(BF)
        t.dg[1:2, :] += jnp.sum(dn2 * xhat, axis=0, keepdims=True)
        dhid = dy.astype(F32) + norm_back(dn2, g1, xhat, r)
        datt = dhid.astype(BF)
        t.datt[rows, :] = datt
        dmix = nt(datt, t.w_proj[b]).astype(BF)
        q = t.q[rows, :]
        k = t.k[rows, :]
        v = t.v[rows, :]
        dq = jnp.zeros((WT, C), F32)
        for h in range(HEADS):
            part = slice(h * WT, h * WT + WT)
            prow = pl.ds(pl.multiple_of(w * BROWS + h * WT, WT), WT)
            dom = dmix * head_mask(h, BF)
            t.dom[part, :] = dom
            t.qm[part, :] = q * head_mask(h, BF)
            dp = nt(dom, v)
            p = t.p[prow, :].astype(F32)
            pd = p * dp
            ds = pd - p * jnp.sum(pd, axis=-1, keepdims=True)
            dbias_of(w, h, ds)
            dsb = ds.astype(BF)
            t.ds[part, :] = dsb
            dq = dq + nn(dsb, k) * head_mask(h, F32)
        pw = t.p[pl.ds(pl.multiple_of(w * BROWS, WT), BROWS), :]
        dq = (dq * HEAD ** -0.5).astype(BF)
        dk = (tn(t.ds[...], t.qm[...]) * HEAD ** -0.5).astype(BF)
        dv = tn(pw, t.dom[...]).astype(BF)
        t.dq[rows, :] = dq
        t.dk[rows, :] = dk
        t.dv[rows, :] = dv
        du = nt(dq, t.wq[0]) + nt(dk, t.wq[1]) + nt(dv, t.wq[2])
        du = du.astype(BF).astype(F32)
        xhat, r = stats(t.x[rows, :].astype(F32))
        t.u[rows, :] = (xhat * g0).astype(BF)
        t.dg[0:1, :] += jnp.sum(du * xhat, axis=0, keepdims=True)
        dx = norm_back(du, g0, xhat, r).astype(BF).astype(F32) + datt.astype(F32)
        t.dx[rows, :] = dx.astype(BF)
        after_window(w)
        return carry

    lax.fori_loop(0, 4, window, 0)


def weight_products(t, part):
    pad = jnp.zeros((NT, 64), BF)

    def left(lhs, x):
        return tn(lhs, jnp.concatenate([x, pad], axis=1))

    def right(lhs, x):
        return tn(lhs, jnp.concatenate([pad, x], axis=1))

    def put(core, row, lft, rgt):
        rows = slice(row, row + lft.shape[0])
        part[core, rows, 0:128] = lft[:, 0:128].astype(BF)
        part[core, rows, 128:256] = (lft[:, 128:256] + rgt[:, 0:128]).astype(BF)
        part[core, rows, 256:384] = rgt[:, 128:256].astype(BF)

    u, n2, dout = t.u[...], t.n2[...], t.dout[...]
    up_low = left(t.dup[:, 0:384], n2)
    up_high = right(t.dup[:, 384:768], n2)
    put(0, 0, left(t.dq[...], u), up_high[0:192])
    put(0, 192, left(t.dk[...], u), up_high[192:384])
    down = right(t.a[:, 0:384], dout)
    put(0, 384, left(t.dv[...], u), down[0:192])
    put(1, 0, left(t.datt[...], t.mix[...]), down[192:384])
    down = right(t.a[:, 384:768], dout)
    put(1, 192, up_low[0:192], down[0:192])
    put(1, 384, up_low[192:384], down[192:384])


def other_rows(t, part):
    flat = jnp.concatenate([t.dg[0:1, :], t.dg[1:2, :], jnp.zeros((1, 3 * WT - 2 * C), F32)], axis=1)
    t.db[BROWS:OROWS, :] = jnp.concatenate([flat[:, 0:WT], flat[:, WT:2 * WT], flat[:, 2 * WT:3 * WT], jnp.zeros((OROWS - BROWS - 3, WT), F32)], axis=0)
    gap = jnp.zeros((240, 48), F32)
    for core in range(2):
        lft = t.db[lat_row(core):lat_row(core) + 240, :]
        rgt = t.db[lat_row(2 + core):lat_row(2 + core) + 240, :]
        part[core, 576:816, :] = jnp.concatenate([lft, gap, rgt, gap], axis=1).astype(BF)


def half_of(shape, axis):
    return (lax.broadcasted_iota(jnp.int32, shape, axis) // 36) % 2


def lane_moves(low):
    src = lax.broadcasted_iota(jnp.int32, (WT, WT), 0)
    dst = lax.broadcasted_iota(jnp.int32, (WT, WT), 1)
    keep = dst - 36 * ((dst // 36) % 2) + (0 if low else 36)
    return (src == keep).astype(F32)


def polar_bias(table, low):
    moved = jnp.dot(table, lane_moves(low), precision=lax.Precision.HIGHEST, preferred_element_type=F32)
    half = half_of((WT, WT), 0)
    if low:
        moved = jnp.where(half == 0, moved, pltpu.roll(moved, 36, 0))
    else:
        moved = jnp.where(half == 1, moved, pltpu.roll(moved, WT - 36, 0))
    return jnp.where(half == half_of((WT, WT), 1), moved, -1e30)


def polar_back(grad, low):
    half = half_of((WT, WT), 0)
    if low:
        folded = jnp.where(half == 0, grad + pltpu.roll(grad, WT - 36, 0), 0.0)
    else:
        folded = jnp.where(half == 1, grad + pltpu.roll(grad, 36, 0), 0.0)
    return lax.dot_general(folded, lane_moves(low), (((1,), (1,)), ((), ())), precision=lax.Precision.HIGHEST, preferred_element_type=F32)


def greet(peers, count):
    barrier = pltpu.get_barrier_semaphore()
    for cond, dev in peers:
        if cond is None:
            pl.semaphore_signal(barrier, inc=1, device_id=dev, device_id_type=MESH)
        else:
            @pl.when(cond)
            def _():
                pl.semaphore_signal(barrier, inc=1, device_id=dev, device_id_type=MESH)
    pl.semaphore_wait(barrier, count)


def guarded(cond, act):
    if cond is None:
        act()
    else:
        pl.when(cond)(act)


class Exchange:
    def __init__(self, moves, src, dst, send_sem, recv_sem, base, here):
        self.sends, self.locals, self.recvs = moves
        self.src, self.dst, self.send_sem, self.recv_sem, self.base, self.here = src, dst, send_sem, recv_sem, base, here

    def remote(self, i, s, d, size, dev):
        return pltpu.make_async_remote_copy(
            src_ref=self.src.at[pl.ds(s, size), :], dst_ref=self.dst.at[pl.ds(d, size), :], send_sem=self.send_sem.at[self.base + i],
            recv_sem=self.recv_sem.at[self.base + i], device_id=dev, device_id_type=MESH)

    def start(self):
        for i, cond, s, d, size, dev in self.sends:
            guarded(cond, lambda: self.remote(i, s, d, size, dev).start())
        for cond, s, d, size in self.locals:
            def keep():
                self.dst[d:d + size, :] = self.src[s:s + size, :]
            guarded(cond, keep)

    def finish(self):
        for i, cond, d, size in self.recvs:
            guarded(cond, lambda: self.remote(i, 0, d, size, self.here).wait_recv())
        for i, cond, s, d, size, dev in self.sends:
            guarded(cond, lambda: self.remote(i, s, d, size, dev).wait_send())


def moves_out(n):
    sends = [
        (0, None, 432, 432, 48, (n.b, n.east)),
        (1, n.inner_up, 112, 592, 48, (n.up, n.east)),
        (2, n.first, 112, 112, 48, (n.b, n.east)),
        (3, n.inner_up, 0, 480, 112, (n.up, n.j)),
        (4, n.inner_down, 480, 0, 160, (n.down, n.j)),
    ]
    locals_ = [(None, 160, 160, 272), (n.first, 0, 0, 112), (n.last, 480, 480, 160)]
    recvs = [(0, None, 432, 48), (1, n.inner_down, 592, 48), (2, n.first, 112, 48), (3, n.inner_down, 480, 112), (4, n.inner_up, 0, 160)]
    return sends, locals_, recvs


def moves_back(n):
    sends = [
        (0, None, 432, 432, 48, (n.b, n.west)),
        (1, n.inner_down, 592, 112, 48, (n.down, n.west)),
        (2, n.first, 112, 112, 48, (n.b, n.west)),
        (3, n.inner_down, 480, 0, 112, (n.down, n.j)),
        (4, n.inner_up, 0, 480, 160, (n.up, n.j)),
    ]
    locals_ = [(None, 160, 160, 272), (n.first, 0, 0, 112), (n.last, 480, 480, 160)]
    recvs = [(0, None, 432, 48), (1, n.inner_up, 112, 48), (2, n.first, 112, 48), (3, n.inner_up, 0, 112), (4, n.inner_down, 480, 160)]
    return sends, locals_, recvs


def lat_row(lat):
    return ((650 * lat) // 48) * 16


def z_row(core, z):
    return ((52 * core + 325 * z) // 96) * 16


def x_row(lat, z, x):
    return ((5200 * lat + 1300 * z + 325 * x) // 384) * 16


def al(v):
    return pl.multiple_of(v, 16)


def total(*terms):
    out = terms[0].astype(F32)
    for term in terms[1:]:
        out = out + term.astype(F32)
    return out


class Reduce:
    def __init__(self, n, t, send_sem, recv_sem, base):
        self.n, self.t, self.send_sem, self.recv_sem, self.base = n, t, send_sem, recv_sem, base

    def remote(self, i, s, d, dev):
        i = self.base + i
        return pltpu.make_async_remote_copy(src_ref=s, dst_ref=d, send_sem=self.send_sem.at[i], recv_sem=self.recv_sem.at[i], device_id=dev, device_id_type=MESH)

    def core_copies(self):
        n, t = self.n, self.t
        return [self.remote(0, t.part.at[1 - n.core], t.got_core, n.device(core=1 - n.core))]

    def z_copies(self):
        n, t = self.n, self.t
        out = []
        for d in range(1, 4):
            z = (n.z + d) % 4
            dev = n.device(z=z)
            out.append(self.remote(2 * d - 1, t.sum_core.at[pl.ds(al(144 * z), 144), :], t.got_z.at[d - 1, pl.ds(0, 144), :], dev))
            out.append(self.remote(2 * d, t.sum_core.at[pl.ds(al(576 + z_row(n.core, z)), 80), :], t.got_z.at[d - 1, pl.ds(144, 80), :], dev))
        return out

    def y_copies(self):
        n, t = self.n, self.t
        return [self.remote(7, t.sum_z.at[:, pl.ds(pl.multiple_of(128 * (1 - n.yh), 128), 256)], t.got_y, n.device(yh=1 - n.yh))]

    def x_window(self, x):
        n = self.n
        return al(144 + x_row(n.b, n.z, x) - lat_row(n.b) - z_row(n.core, n.z))

    def x_copies(self):
        n, t = self.n, self.t
        out = []
        for d in range(1, 4):
            x = (n.x + d) % 4
            dev = n.device(x=x)
            out.append(self.remote(6 + 2 * d, t.sum_y.at[pl.ds(al(32 * x), 48), :], t.got_x.at[d - 1, pl.ds(0, 48), :], dev))
            out.append(self.remote(7 + 2 * d, t.sum_y.at[pl.ds(self.x_window(x), 32), :], t.got_x.at[d - 1, pl.ds(48, 32), :], dev))
        return out

    def l_copies(self):
        return [self.remote(14, self.t.sum_x, self.t.got_l, self.n.device(yl=1 - self.n.yl))]

    def start(self, copies):
        for c in copies:
            c.start()

    def wait(self, copies):
        for c in copies:
            c.wait()

    def core_start(self):
        self.start(self.core_copies())

    def core_to_z(self):
        n, t = self.n, self.t
        self.wait(self.core_copies())
        for i in range(3):
            rows = slice(272 * i, 272 * i + 272)
            t.sum_core[rows, :] = total(t.part[n.core, rows, :], t.got_core[rows, :]).astype(BF)
        self.start(self.z_copies())

    def z_to_y(self):
        n, t = self.n, self.t
        self.wait(self.z_copies())
        own = t.sum_core[pl.ds(al(144 * n.z), 144), :]
        t.sum_z[0:144, :] = total(own, *[t.got_z[i, 0:144, :] for i in range(3)]).astype(BF)
        own = t.sum_core[pl.ds(al(576 + z_row(n.core, n.z)), 80), :]
        t.sum_z[144:224, :] = total(own, *[t.got_z[i, 144:224, :] for i in range(3)]).astype(BF)
        self.start(self.y_copies())

    def y_to_x(self):
        n, t = self.n, self.t
        self.wait(self.y_copies())
        own = t.sum_z[:, pl.ds(pl.multiple_of(128 * n.yh, 128), 256)]
        t.sum_y[...] = total(own, t.got_y[...]).astype(BF)
        self.start(self.x_copies())

    def x_to_l(self):
        n, t = self.n, self.t
        self.wait(self.x_copies())
        own = t.sum_y[pl.ds(al(32 * n.x), 48), :]
        t.sum_x[0:48, :] = total(own, *[t.got_x[i, 0:48, :] for i in range(3)]).astype(BF)
        own = t.sum_y[pl.ds(self.x_window(n.x), 32), :]
        t.sum_x[48:80, :] = total(own, *[t.got_x[i, 48:80, :] for i in range(3)]).astype(BF)
        self.start(self.l_copies())

    def finish(self):
        self.wait(self.l_copies())
        final = total(self.t.sum_x[...], self.t.got_l[...])
        return jnp.where(self.n.yh == 1, pltpu.roll(final, 192, 1), final)


def share_squares(n, final):
    matrix, other = final[0:48, :], final[48:80, :]
    row = lax.broadcasted_iota(jnp.int32, (48, 256), 0)
    lane = lax.broadcasted_iota(jnp.int32, (48, 256), 1)
    low = 4 * n.x + 18 * n.yl
    squares = jnp.sum(jnp.where((row >= low) & (row < low + 18) & (lane < C), matrix * matrix, 0.0), axis=0, keepdims=True)
    row = lax.broadcasted_iota(jnp.int32, (32, 256), 0)
    lane = lax.broadcasted_iota(jnp.int32, (32, 256), 1)
    index = (row + x_row(n.b, n.z, n.x)) * WT + lane
    low = 975 * (32 * n.b + n.j)
    inside = (index >= low) & (index < low + 975) & (lane < WT)
    squares = squares + jnp.sum(jnp.where(inside, other * other, 0.0), axis=0, keepdims=True)
    return jnp.sum(squares, axis=1, keepdims=True)


INPUTS = ["tok", "cot", "gains", "w_qkv", "w_proj", "w_up", "w_down", "bias", "to_win", "to_nat", "send_win", "win_send", "send_nat", "to_slots", "from_slots"]
PERMS = INPUTS[8:]
OUTPUTS = [("gtok", (NT, C), BF), ("m", (2, 48, 256), F32), ("o", (2, 32, 256), F32)]
BLOCK = [
    ("x", (NT, C), BF), ("wq", (3, C, C), BF), ("q", (NT, C), BF), ("k", (NT, C), BF), ("v", (NT, C), BF), ("p", (4 * BROWS, WT), BF),
    ("mix", (NT, C), BF), ("hid", (NT, C), F32), ("a", (NT, FFN), BF), ("gp", (NT, FFN), BF), ("dout", (NT, C), BF), ("part", (2, 816, 384), BF),
    ("got_core", (816, 384), BF), ("sum_core", (816, 384), BF), ("got_z", (3, 224, 384), BF), ("sum_z", (224, 384), BF),
    ("got_y", (224, 256), BF), ("sum_y", (224, 256), BF), ("got_x", (3, 80, 256), BF), ("sum_x", (80, 256), BF), ("got_l", (80, 256), BF),
    ("db", (OROWS, WT), F32), ("dg", (2, C), F32),
]
SHARED = [
    ("out", (NT, C), BF), ("dx", (NT, C), BF), ("u", (NT, C), BF), ("n2", (NT, C), BF), ("datt", (NT, C), BF), ("dq", (NT, C), BF), ("dk", (NT, C), BF),
    ("dv", (NT, C), BF), ("dup", (NT, FFN), BF), ("dom", (BROWS, C), BF), ("qm", (BROWS, C), BF), ("ds", (BROWS, WT), BF),
    ("lbias", (3, BROWS, WT), F32), ("db_b", (BROWS, WT), F32), ("parts", (24, 8, 128), F32),
    ("cot_src", (NR, C), BF), ("cot_dst", (NR, C), BF), ("mid_src", (NR, C), BF), ("mid_dst", (NR, C), BF), ("back_src", (NR, C), BF), ("back_dst", (NR, C), BF),
]
SEMS = 15 + 30 + 22


def place(nlat, nlon):
    n = types.SimpleNamespace()
    n.b, n.j = lax.axis_index("lat"), lax.axis_index("lon")
    n.east, n.west = lax.rem(n.j + 1, nlon), lax.rem(n.j + nlon - 1, nlon)
    n.up, n.down = jnp.maximum(n.b - 1, 0), jnp.minimum(n.b + 1, nlat - 1)
    n.first, n.last = n.b == 0, n.b == nlat - 1
    n.inner_up, n.inner_down = n.b > 0, n.b < nlat - 1
    n.yh, n.core = n.b // 2, n.b % 2
    n.z, n.x, n.yl = n.j // 8, (n.j // 2) % 4, n.j % 2

    def device(yh=n.yh, core=n.core, z=n.z, x=n.x, yl=n.yl):
        return (yh * 2 + core, z * 8 + x * 2 + yl)

    n.device = device
    return n


def kernel(nlat, nlon, reduce, *refs):
    names = INPUTS + [o[0] for o in OUTPUTS] + ["first_" + e[0] for e in BLOCK] + ["second_" + e[0] for e in BLOCK] + [e[0] for e in SHARED] + ["send_sem", "recv_sem"]
    r = dict(zip(names, refs, strict=True))
    weights = {k: r[k] for k in INPUTS}
    blocks = []
    for label in ("first_", "second_"):
        blocks.append(types.SimpleNamespace(**weights, **{e[0]: r[e[0]] for e in SHARED}, **{e[0]: r[label + e[0]] for e in BLOCK}))
    one, two = blocks
    n = place(nlat, nlon)
    sems = (r["send_sem"], r["recv_sem"])
    here = (n.b, n.j)
    ex_cot = Exchange(moves_out(n), one.cot_src, one.cot_dst, *sems, 0, here)
    ex_mid = Exchange(moves_out(n), one.mid_src, one.mid_dst, *sems, 5, here)
    ex_back = Exchange(moves_back(n), one.back_src, one.back_dst, *sems, 10, here)

    plane = [(dz, dx) for dz in range(4) for dx in range(4) if (dz, dx) != (0, 0)]
    plane_dev = [n.device(z=(n.z + dz) % 4, x=(n.x + dx) % 4) for dz, dx in plane]
    cube = [(a, c, e) for a in range(2) for c in range(2) for e in range(2) if (a, c, e) != (0, 0, 0)]
    cube_dev = [n.device(yh=(n.yh + a) % 2, core=(n.core + c) % 2, yl=(n.yl + e) % 2) for a, c, e in cube]
    far = plane_dev + cube_dev if reduce else []
    greet(
        [(None, (n.b, n.east)), (None, (n.b, n.west)), (n.inner_up, (n.up, n.j)), (n.inner_down, (n.down, n.j)), (n.inner_up, (n.up, n.east)), (n.inner_down, (n.down, n.west))]
        + [(None, d) for d in far],
        jnp.where(jnp.logical_or(n.first, n.last), 4, 6) + len(far),
    )

    one.cot_src[...] = shuffle(one.send_nat[...], one.cot[...])
    ex_cot.start()
    one.x[...] = shuffle(one.to_win[...], one.tok[...])
    for b, t in enumerate(blocks):
        for i in range(3):
            t.wq[i] = t.w_qkv[b, :, C * i:C * i + C]
    one.lbias[0] = one.bias[0] * LOG2E
    forward_windows(one, 0, lambda w, h: one.lbias[0, h * WT:h * WT + WT, :], False)
    one.mid_src[...] = shuffle(one.send_win[...], one.out[...])
    ex_mid.start()

    for group in range(2):
        polar = n.first if group == 0 else n.last

        @pl.when(polar)
        def _():
            for h in range(HEADS):
                rows = slice(h * WT, h * WT + WT)
                two.lbias[1 + group, rows, :] = polar_bias(two.bias[1, rows, :] * LOG2E, group == 1)

        @pl.when(jnp.logical_not(polar))
        def _():
            two.lbias[1 + group] = two.bias[1] * LOG2E

    two.db[...] = jnp.zeros((OROWS, WT), F32)
    two.db_b[...] = jnp.zeros((BROWS, WT), F32)
    ex_cot.finish()
    two.dout[...] = shuffle(two.to_slots[...], two.cot_dst[...])
    ex_mid.finish()
    two.x[...] = shuffle(two.to_slots[...], two.mid_dst[...])
    forward_windows(two, 1, lambda w, h: two.lbias[1 + w // 2, h * WT:h * WT + WT, :], True)

    def dbias_two(w, h, ds):
        rows = slice(h * WT, h * WT + WT)

        @pl.when(w < 2)
        def _():
            two.db[rows, :] += ds

        @pl.when(w >= 2)
        def _():
            two.db_b[rows, :] += ds

    backward_windows(two, 1, dbias_two, lambda w: None)
    two.back_src[...] = shuffle(two.from_slots[...], two.dx[...])
    ex_back.start()
    for group, ref in enumerate((two.db, two.db_b)):
        @pl.when(n.first if group == 0 else n.last)
        def _():
            for h in range(HEADS):
                rows = slice(h * WT, h * WT + WT)
                ref[rows, :] = polar_back(ref[rows, :], group == 1)

    two.db[0:BROWS, :] += two.db_b[...]
    weight_products(two, two.part)
    other_rows(two, two.part)
    red_one = Reduce(n, one, *sems, 15)
    red_two = Reduce(n, two, *sems, 30)
    if reduce:
        red_two.core_start()

    ex_back.finish()
    one.dout[...] = shuffle(one.win_send[...], one.back_dst[...])
    one.db[...] = jnp.zeros((OROWS, WT), F32)

    def dbias_one(w, h, ds):
        one.db[h * WT:h * WT + WT, :] += ds

    def step(w):
        if reduce:
            pl.when(w == 0)(red_two.core_to_z)
            pl.when(w == 2)(red_two.z_to_y)
            pl.when(w == 3)(red_two.y_to_x)

    backward_windows(one, 0, dbias_one, step)
    weight_products(one, one.part)
    other_rows(one, one.part)
    if reduce:
        red_one.core_start()
    r["gtok"][...] = shuffle(one.to_nat[...], one.dx[...])
    if not reduce:
        return
    red_two.x_to_l()
    red_one.core_to_z()
    two_final = red_two.finish()
    red_one.z_to_y()
    red_one.y_to_x()
    red_one.x_to_l()
    one_final = red_one.finish()

    parts = one.parts
    parts[0] = jnp.broadcast_to(share_squares(n, one_final) + share_squares(n, two_final), (8, 128))

    def spread(base, source, target, devices):
        copies = [
            pltpu.make_async_remote_copy(src_ref=parts.at[source], dst_ref=parts.at[target + i], send_sem=sems[0].at[base + i], recv_sem=sems[1].at[base + i], device_id=d, device_id_type=MESH)
            for i, d in enumerate(devices)
        ]
        for c in copies:
            c.start()
        for c in copies:
            c.wait()
        acc = parts[source]
        for i in range(len(devices)):
            acc = acc + parts[target + i]
        return acc

    parts[16] = spread(45, 0, 1, plane_dev)
    acc = spread(60, 16, 17, cube_dev)
    ceiling = math.sqrt(24 * C * C + 2 * VECB)
    factor = jnp.minimum(1.0, ceiling / (jnp.sqrt(acc) + 1e-06))[0:1, 0:1]
    for b, final in enumerate((one_final, two_final)):
        r["m"][b] = final[0:48, :] * factor
        r["o"][b] = final[48:80, :] * factor


def run(nlat, nlon, reduce, tokens, cotangent, norm_gains, w_qkv, w_proj, w_up, w_down, pos_bias):
    args = [tokens.reshape(NT, C), cotangent.reshape(NT, C), norm_gains, w_qkv, w_proj, w_up, jnp.swapaxes(w_down, 1, 2), pos_bias.reshape(2, BROWS, WT)]
    args += [const(p) for p in PERMS]
    vmem = pl.BlockSpec(memory_space=pltpu.VMEM)
    return pl.pallas_call(
        functools.partial(kernel, nlat, nlon, reduce),
        in_specs=[vmem] * len(args),
        out_specs=[vmem] * len(OUTPUTS),
        out_shape=[jax.ShapeDtypeStruct(s, d) for _, s, d in OUTPUTS],
        scratch_shapes=[pltpu.VMEM(s, d) for _, s, d in BLOCK + BLOCK + SHARED] + [pltpu.SemaphoreType.DMA((SEMS,))] * 2,
        compiler_params=pltpu.CompilerParams(vmem_limit_bytes=VMEM_LIMIT, collective_id=1, has_side_effects=True),
        name="two_blocks",
    )(*args)


def shards(nlat, nlon, tokens, *args):
    gtok, m, o = run(nlat, nlon, True, tokens, *args)
    n = place(nlat, nlon)
    m = lax.dynamic_slice_in_dim(m, 4 * n.x + 18 * n.yl, 18, axis=1)[:, :, :C]
    flat = o[:, :, :WT].reshape(2, 32 * WT)
    other = lax.dynamic_slice_in_dim(flat, 975 * (32 * n.b + n.j) - x_row(n.b, n.z, n.x) * WT, 975, axis=1)
    return gtok.reshape(tokens.shape), m.transpose(0, 2, 1), other


def solution(mesh):
    grid = P(None, "lat", "lon", None)
    return jax.shard_map(
        functools.partial(shards, mesh.shape["lat"], mesh.shape["lon"]),
        mesh=mesh,
        in_specs=(grid, grid) + (P(),) * 6,
        out_specs=(grid, P(None, None, ("lat", "lon")), P(None, ("lat", "lon"))),
        check_vma=False,
    )
```

```python
import functools
import math
import types

import jax
import jax.numpy as jnp
import numpy as np
from jax import lax
from jax.experimental import pallas as pl
from jax.experimental.pallas import tpu as pltpu
from jax.sharding import PartitionSpec as P

C = 192
HEADS = 6
HEAD = 32
FFN = 768
WT = 144
NT = 576
NR = 640
QT = 160
MAIN = 112
VECB = 124800
BROWS = HEADS * WT
MROWS = 2304
OROWS = 880
GROWS = MROWS + OROWS
LOG2E = math.log2(math.e)
MESH = pl.DeviceIdType.MESH
BF = jnp.bfloat16
F32 = jnp.float32
VMEM_LIMIT = 56 * 1024 * 1024


def nat(l, r, c):
    return l * 288 + r * 48 + c


def one_hot(sources, width):
    mat = np.zeros((len(sources), width), np.float32)
    for i, s in enumerate(sources):
        if s >= 0:
            mat[i, s] = 1.0
    return mat


@functools.cache
def orders():
    win = [nat(l, r, 12 * w + c) for w in range(4) for l in range(2) for r in range(6) for c in range(12)]

    def cells(rows, cols, size):
        out = [nat(l, r, c) for l in range(2) for r in rows for c in cols]
        return out + [-1] * (size - len(out))

    top, low = range(0, 3), range(3, 6)
    send = []
    for rows in (top, low):
        send += cells(rows, range(0, 18), MAIN)
        send += cells(rows, range(42, 48), QT - MAIN)
        send += cells(rows, range(24, 42), MAIN)
        send += cells(rows, range(18, 24), QT - MAIN)
    slots = []
    for s in range(4):
        for l in range(2):
            for half in range(2):
                for r in range(3):
                    for cc in range(12):
                        col = 12 * (s % 2) + cc
                        base = QT * (2 * (s // 2) + half)
                        if col >= 6:
                            slots.append(base + (l * 3 + r) * 18 + col - 6)
                        else:
                            slots.append(base + MAIN + (l * 3 + r) * 6 + col)
    win_at = {n: i for i, n in enumerate(win)}
    send_win = [win_at[n] if n >= 0 else -1 for n in send]
    to_win = one_hot(win, NT)
    send_from_win = one_hot(send_win, NT)
    send_from_nat = one_hot(send, NT)
    to_slots = one_hot(slots, NR)
    return {
        "to_win": to_win,
        "to_nat": to_win.T.copy(),
        "send_win": send_from_win,
        "win_send": send_from_win.T.copy(),
        "send_nat": send_from_nat,
        "to_slots": to_slots,
        "from_slots": to_slots.T.copy(),
    }


def const(name):
    return jnp.asarray(orders()[name], BF)


def nn(a, b):
    return lax.dot_general(a, b, (((1,), (0,)), ((), ())), preferred_element_type=F32)


def nt(a, b):
    return lax.dot_general(a, b, (((1,), (1,)), ((), ())), preferred_element_type=F32)


def tn(a, b):
    return lax.dot_general(a, b, (((0,), (0,)), ((), ())), preferred_element_type=F32)


def shuffle(mat, x):
    return nn(mat, x).astype(BF)


def stats(x):
    center = x - jnp.mean(x, axis=-1, keepdims=True)
    r = lax.rsqrt(jnp.mean(center * center, axis=-1, keepdims=True) + 1e-05)
    return center * r, r


def norm_back(dn, gain, xhat, r):
    t = dn * gain
    return r * (t - jnp.mean(t, axis=-1, keepdims=True) - xhat * jnp.mean(t * xhat, axis=-1, keepdims=True))


def head_mask(h, dtype):
    lane = lax.broadcasted_iota(jnp.int32, (1, C), 1)
    return ((lane >= h * HEAD) & (lane < (h + 1) * HEAD)).astype(F32).astype(dtype)


def forward_windows(t, b, bias_of, last):
    g0, g1 = t.gains[b, 0:1, :], t.gains[b, 1:2, :]

    def window(w, carry):
        rows = pl.ds(pl.multiple_of(w * WT, WT), WT)
        x = t.x[rows, :].astype(F32)
        u = (stats(x)[0] * g0).astype(BF)
        q = nn(u, t.wq[0]).astype(BF)
        k = nn(u, t.wq[1]).astype(BF)
        v = nn(u, t.wq[2]).astype(BF)
        t.q[rows, :] = q
        t.k[rows, :] = k
        t.v[rows, :] = v
        mixed = jnp.zeros((WT, C), F32)
        for h in range(HEADS):
            s = nt(q * head_mask(h, BF), k) * (HEAD ** -0.5 * LOG2E) + bias_of(w, h)
            e = jnp.exp2(s - jnp.max(s, axis=-1, keepdims=True))
            p = (e * (1.0 / jnp.sum(e, axis=-1, keepdims=True))).astype(BF)
            t.p[pl.ds(pl.multiple_of(w * BROWS + h * WT, WT), WT), :] = p
            mixed = mixed + nn(p, v) * head_mask(h, F32)
        mixed = mixed.astype(BF)
        t.mix[rows, :] = mixed
        attended = nn(mixed, t.w_proj[b]).astype(BF)
        hidden = x + attended.astype(F32)
        t.hid[rows, :] = hidden
        n2 = (stats(hidden)[0] * g1).astype(BF)
        total = hidden
        for j in range(3):
            cols = slice(256 * j, 256 * j + 256)
            up = nn(n2, t.w_up[b, :, cols])
            cdf = 0.5 + 0.5 * lax.erf(up * (0.5 ** 0.5))
            slope = cdf + up * jnp.exp2(up * up * (-0.5 * LOG2E)) * (1.0 / math.sqrt(2 * math.pi))
            act = (up * cdf).astype(BF)
            t.a[rows, cols] = act
            t.gp[rows, cols] = slope.astype(BF)
            if not last:
                total = total + nt(act, t.w_down[b, :, cols])
        if not last:
            t.out[rows, :] = total.astype(BF)
        return carry

    lax.fori_loop(0, 4, window, 0, unroll=2)


def backward_windows(t, b, dbias_of, after_window):
    g0, g1 = t.gains[b, 0:1, :], t.gains[b, 1:2, :]
    t.dg[...] = jnp.zeros((2, C), F32)

    def window(w, carry):
        rows = pl.ds(pl.multiple_of(w * WT, WT), WT)
        dy = t.dout[rows, :]
        dn2 = jnp.zeros((WT, C), F32)
        for j in range(3):
            cols = slice(256 * j, 256 * j + 256)
            da = nn(dy, t.w_down[b, :, cols]).astype(BF).astype(F32)
            dup = (da * t.gp[rows, cols].astype(F32)).astype(BF)
            t.dup[rows, cols] = dup
            dn2 = dn2 + nt(dup, t.w_up[b, :, cols])
        dn2 = dn2.astype(BF).astype(F32)
        xhat, r = stats(t.hid[rows, :])
        t.n2[rows, :] = (xhat * g1).astype(BF)
        t.dg[1:2, :] += jnp.sum(dn2 * xhat, axis=0, keepdims=True)
        dhid = dy.astype(F32) + norm_back(dn2, g1, xhat, r)
        datt = dhid.astype(BF)
        t.datt[rows, :] = datt
        dmix = nt(datt, t.w_proj[b]).astype(BF)
        q = t.q[rows, :]
        k = t.k[rows, :]
        v = t.v[rows, :]
        doms = jnp.concatenate([dmix * head_mask(h, BF) for h in range(HEADS)], axis=0)
        qms = jnp.concatenate([q * head_mask(h, BF) for h in range(HEADS)], axis=0)
        dps = nt(doms, v)
        pw = t.p[pl.ds(pl.multiple_of(w * BROWS, WT), BROWS), :]
        dss = []
        for h in range(HEADS):
            part = slice(h * WT, h * WT + WT)
            p = pw[part].astype(F32)
            pd = p * dps[part]
            ds = pd - p * jnp.sum(pd, axis=-1, keepdims=True)
            dbias_of(w, h, ds)
            dss.append(ds.astype(BF))
        dss = jnp.concatenate(dss, axis=0)
        dqs = nn(dss, k)
        dq = dqs[0:WT] * head_mask(0, F32)
        for h in range(1, HEADS):
            dq = dq + dqs[h * WT:h * WT + WT] * head_mask(h, F32)
        dq = (dq * HEAD ** -0.5).astype(BF)
        dk = (tn(dss, qms) * HEAD ** -0.5).astype(BF)
        dv = tn(pw, doms).astype(BF)
        t.dq[rows, :] = dq
        t.dk[rows, :] = dk
        t.dv[rows, :] = dv
        du = nt(dq, t.wq[0]) + nt(dk, t.wq[1]) + nt(dv, t.wq[2])
        du = du.astype(BF).astype(F32)
        xhat, r = stats(t.x[rows, :].astype(F32))
        t.u[rows, :] = (xhat * g0).astype(BF)
        t.dg[0:1, :] += jnp.sum(du * xhat, axis=0, keepdims=True)
        dx = norm_back(du, g0, xhat, r).astype(BF).astype(F32) + datt.astype(F32)
        t.dx[rows, :] = dx.astype(BF)
        after_window(w)
        return carry

    lax.fori_loop(0, 4, window, 0, unroll=2)


def weight_products(t, part):
    pad = jnp.zeros((NT, 64), BF)

    def left(lhs, x):
        return tn(lhs, jnp.concatenate([x, pad], axis=1))

    def right(lhs, x):
        return tn(lhs, jnp.concatenate([pad, x], axis=1))

    def put(core, row, lft, rgt):
        rows = slice(row, row + lft.shape[0])
        part[core, rows, 0:128] = lft[:, 0:128].astype(BF)
        part[core, rows, 128:256] = (lft[:, 128:256] + rgt[:, 0:128]).astype(BF)
        part[core, rows, 256:384] = rgt[:, 128:256].astype(BF)

    u, n2, dout = t.u[...], t.n2[...], t.dout[...]
    up_low = left(t.dup[:, 0:384], n2)
    up_high = right(t.dup[:, 384:768], n2)
    put(0, 0, left(t.dq[...], u), up_high[0:192])
    put(0, 192, left(t.dk[...], u), up_high[192:384])
    down = right(t.a[:, 0:384], dout)
    put(0, 384, left(t.dv[...], u), down[0:192])
    put(1, 0, left(t.datt[...], t.mix[...]), down[192:384])
    down = right(t.a[:, 384:768], dout)
    put(1, 192, up_low[0:192], down[0:192])
    put(1, 384, up_low[192:384], down[192:384])


def other_rows(t, part):
    flat = jnp.concatenate([t.dg[0:1, :], t.dg[1:2, :], jnp.zeros((1, 3 * WT - 2 * C), F32)], axis=1)
    t.db[BROWS:OROWS, :] = jnp.concatenate([flat[:, 0:WT], flat[:, WT:2 * WT], flat[:, 2 * WT:3 * WT], jnp.zeros((OROWS - BROWS - 3, WT), F32)], axis=0)
    gap = jnp.zeros((240, 48), F32)
    for core in range(2):
        lft = t.db[lat_row(core):lat_row(core) + 240, :]
        rgt = t.db[lat_row(2 + core):lat_row(2 + core) + 240, :]
        part[core, 576:816, :] = jnp.concatenate([lft, gap, rgt, gap], axis=1).astype(BF)


def half_of(shape, axis):
    return (lax.broadcasted_iota(jnp.int32, shape, axis) // 36) % 2


def lane_moves(low):
    src = lax.broadcasted_iota(jnp.int32, (WT, WT), 0)
    dst = lax.broadcasted_iota(jnp.int32, (WT, WT), 1)
    keep = dst - 36 * ((dst // 36) % 2) + (0 if low else 36)
    return (src == keep).astype(F32)


def polar_bias(table, low):
    moved = jnp.dot(table, lane_moves(low), precision=lax.Precision.HIGHEST, preferred_element_type=F32)
    half = half_of((WT, WT), 0)
    if low:
        moved = jnp.where(half == 0, moved, pltpu.roll(moved, 36, 0))
    else:
        moved = jnp.where(half == 1, moved, pltpu.roll(moved, WT - 36, 0))
    return jnp.where(half == half_of((WT, WT), 1), moved, -1e30)


def polar_back(grad, low):
    half = half_of((WT, WT), 0)
    if low:
        folded = jnp.where(half == 0, grad + pltpu.roll(grad, WT - 36, 0), 0.0)
    else:
        folded = jnp.where(half == 1, grad + pltpu.roll(grad, 36, 0), 0.0)
    return lax.dot_general(folded, lane_moves(low), (((1,), (1,)), ((), ())), precision=lax.Precision.HIGHEST, preferred_element_type=F32)


def greet(peers):
    barrier = pltpu.get_barrier_semaphore()
    for cond, dev in peers:
        if cond is None:
            pl.semaphore_signal(barrier, inc=1, device_id=dev, device_id_type=MESH)
        else:
            @pl.when(cond)
            def _():
                pl.semaphore_signal(barrier, inc=1, device_id=dev, device_id_type=MESH)


def guarded(cond, act):
    if cond is None:
        act()
    else:
        pl.when(cond)(act)


class Exchange:
    def __init__(self, moves, src, dst, send_sem, recv_sem, base, here):
        self.sends, self.locals, self.recvs = moves
        self.src, self.dst, self.send_sem, self.recv_sem, self.base, self.here = src, dst, send_sem, recv_sem, base, here

    def remote(self, i, s, d, size, dev):
        return pltpu.make_async_remote_copy(
            src_ref=self.src.at[pl.ds(s, size), :], dst_ref=self.dst.at[pl.ds(d, size), :], send_sem=self.send_sem.at[self.base + i],
            recv_sem=self.recv_sem.at[self.base + i], device_id=dev, device_id_type=MESH)

    def start(self):
        for i, cond, s, d, size, dev in self.sends:
            guarded(cond, lambda: self.remote(i, s, d, size, dev).start())
        for cond, s, d, size in self.locals:
            def keep():
                self.dst[d:d + size, :] = self.src[s:s + size, :]
            guarded(cond, keep)

    def finish(self):
        for i, cond, d, size in self.recvs:
            guarded(cond, lambda: self.remote(i, 0, d, size, self.here).wait_recv())
        for i, cond, s, d, size, dev in self.sends:
            guarded(cond, lambda: self.remote(i, s, d, size, dev).wait_send())


def moves_out(n):
    sends = [
        (0, None, 432, 432, 48, (n.b, n.east)),
        (1, n.inner_up, 112, 592, 48, (n.up, n.east)),
        (2, n.first, 112, 112, 48, (n.b, n.east)),
        (3, n.inner_up, 0, 480, 112, (n.up, n.j)),
        (4, n.inner_down, 480, 0, 160, (n.down, n.j)),
    ]
    locals_ = [(None, 160, 160, 272), (n.first, 0, 0, 112), (n.last, 480, 480, 160)]
    recvs = [(0, None, 432, 48), (1, n.inner_down, 592, 48), (2, n.first, 112, 48), (3, n.inner_down, 480, 112), (4, n.inner_up, 0, 160)]
    return sends, locals_, recvs


def moves_back(n):
    sends = [
        (0, None, 432, 432, 48, (n.b, n.west)),
        (1, n.inner_down, 592, 112, 48, (n.down, n.west)),
        (2, n.first, 112, 112, 48, (n.b, n.west)),
        (3, n.inner_down, 480, 0, 112, (n.down, n.j)),
        (4, n.inner_up, 0, 480, 160, (n.up, n.j)),
    ]
    locals_ = [(None, 160, 160, 272), (n.first, 0, 0, 112), (n.last, 480, 480, 160)]
    recvs = [(0, None, 432, 48), (1, n.inner_up, 112, 48), (2, n.first, 112, 48), (3, n.inner_up, 0, 112), (4, n.inner_down, 480, 160)]
    return sends, locals_, recvs


def lat_row(lat):
    return ((650 * lat) // 48) * 16


def z_row(core, z):
    return ((52 * core + 325 * z) // 96) * 16


def x_row(core, z, x):
    return ((208 * core + 1300 * z + 325 * x) // 384) * 16


def al(v):
    return pl.multiple_of(v, 16)


def total(*terms):
    out = terms[0].astype(F32)
    for term in terms[1:]:
        out = out + term.astype(F32)
    return out


class Reduce:
    def __init__(self, n, t, send_sem, recv_sem, base):
        self.n, self.t, self.send_sem, self.recv_sem, self.base = n, t, send_sem, recv_sem, base

    def remote(self, i, s, d, dev):
        i = self.base + i
        return pltpu.make_async_remote_copy(src_ref=s, dst_ref=d, send_sem=self.send_sem.at[i], recv_sem=self.recv_sem.at[i], device_id=dev, device_id_type=MESH)

    def core_copies(self):
        n, t = self.n, self.t
        return [self.remote(0, t.part.at[1 - n.core], t.got_core, n.device(core=1 - n.core))]

    def first_copies(self):
        n, t = self.n, self.t
        out = []
        for d in range(1, 4):
            i = 3 * d - 2
            z = (n.z + d) % 4
            x = (n.x + d) % 4
            out.append(self.remote(i, t.sum_m.at[:, pl.ds(al(32 * x), 48), pl.ds(128, 256)], t.got_x.at[d - 1], n.device(x=x)))
            dev = n.device(z=z)
            out.append(self.remote(i + 1, t.sum_o.at[pl.ds(al(z_row(n.core, z)), 80), :], t.got_o.at[d - 1], dev))
            out.append(self.remote(i + 2, t.sum_m.at[z, :, pl.ds(0, 128)], t.got_z.at[d - 1], dev))
        return out

    def x_window(self, x):
        return al(x_row(self.n.core, self.n.z, x) - z_row(self.n.core, self.n.z))

    def second_copies(self):
        n, t = self.n, self.t
        out = []
        for d in range(1, 4):
            i = 3 * d + 7
            z = (n.z + d) % 4
            x = (n.x + d) % 4
            out.append(self.remote(i, t.sum_x.at[z], t.got_xz.at[d - 1], n.device(z=z)))
            dev = n.device(x=x)
            out.append(self.remote(i + 1, t.sum_zo.at[pl.ds(self.x_window(x), 32), :], t.got_ox.at[d - 1], dev))
            out.append(self.remote(i + 2, t.sum_z.at[pl.ds(al(32 * x), 48), :], t.got_zx.at[d - 1], dev))
        return out

    def third_copies(self):
        n, t = self.n, self.t
        devices = [n.device(yl=1 - n.yl), n.device(yh=1 - n.yh), n.device(yl=1 - n.yl, yh=1 - n.yh)]
        return [self.remote(19 + i, t.mid, t.got_y.at[i], dev) for i, dev in enumerate(devices)]

    def start(self, copies):
        for c in copies:
            c.start()

    def wait(self, copies):
        for c in copies:
            c.wait()

    def core_start(self):
        self.start(self.core_copies())

    def core_to_first(self):
        n, t = self.n, self.t
        self.wait(self.core_copies())
        for z in range(4):
            rows = slice(144 * z, 144 * z + 144)
            t.sum_m[z] = total(t.part[n.core, rows, :], t.got_core[rows, :]).astype(BF)
        t.sum_o[...] = total(t.part[n.core, 576:816, :], t.got_core[576:816, :]).astype(BF)
        self.start(self.first_copies())

    def first_to_second(self):
        n, t = self.n, self.t
        self.wait(self.first_copies())
        t.sum_x[...] = total(t.sum_m[:, pl.ds(al(32 * n.x), 48), 128:384], *[t.got_x[i] for i in range(3)]).astype(BF)
        t.sum_zo[...] = total(t.sum_o[pl.ds(al(z_row(n.core, n.z)), 80), :], *[t.got_o[i] for i in range(3)]).astype(BF)
        t.sum_z[...] = total(t.sum_m[n.z, :, 0:128], *[t.got_z[i] for i in range(3)]).astype(BF)
        self.start(self.second_copies())

    def second_to_third(self):
        n, t = self.n, self.t
        self.wait(self.second_copies())
        t.mid[0:48, 0:128] = total(t.sum_z[pl.ds(al(32 * n.x), 48), :], *[t.got_zx[i] for i in range(3)]).astype(BF)
        t.mid[0:48, 128:384] = total(t.sum_x[n.z], *[t.got_xz[i] for i in range(3)]).astype(BF)
        t.mid[48:80, :] = total(t.sum_zo[pl.ds(self.x_window(n.x), 32), :], *[t.got_ox[i] for i in range(3)]).astype(BF)
        self.start(self.third_copies())

    def finish(self):
        self.wait(self.third_copies())
        return total(self.t.mid[...], *[self.t.got_y[i] for i in range(3)])


def group_squares(n, final):
    matrix, other = final[0:48, :], final[48:80, :]
    row = lax.broadcasted_iota(jnp.int32, (48, 384), 0)
    low = 4 * n.x
    squares = jnp.sum(jnp.where((row >= low) & (row < low + 36), matrix * matrix, 0.0), axis=0, keepdims=True)
    lane = lax.broadcasted_iota(jnp.int32, (32, 384), 1)
    row = lax.broadcasted_iota(jnp.int32, (32, 384), 0) + x_row(n.core, n.z, n.x)
    for yh in range(2):
        lat = 2 * yh + n.core
        at = lane - C * yh
        index = (row + lat_row(lat)) * WT + at
        low = 975 * (32 * lat + 8 * n.z + 2 * n.x)
        inside = (index >= low) & (index < low + 1950) & (at >= 0) & (at < WT)
        squares = squares + jnp.sum(jnp.where(inside, other * other, 0.0), axis=0, keepdims=True)
    return jnp.sum(squares, axis=1, keepdims=True)


def own_lanes(n, final):
    return jnp.where(n.yh == 1, pltpu.roll(final, C, 1), final)[:, 0:256]


INPUTS = ["tok", "cot", "gains", "w_qkv", "w_proj", "w_up", "w_down", "bias", "to_win", "to_nat", "send_win", "win_send", "send_nat", "to_slots", "from_slots"]
PERMS = INPUTS[8:]
OUTPUTS = [("gtok", (NT, C), BF), ("m", (2, 48, 256), F32), ("o", (2, 32, 256), F32)]
BLOCK = [
    ("x", (NT, C), BF), ("wq", (3, C, C), BF), ("q", (NT, C), BF), ("k", (NT, C), BF), ("v", (NT, C), BF), ("p", (4 * BROWS, WT), BF),
    ("mix", (NT, C), BF), ("hid", (NT, C), F32), ("a", (NT, FFN), BF), ("gp", (NT, FFN), BF), ("dout", (NT, C), BF), ("part", (2, 816, 384), BF),
    ("got_core", (816, 384), BF), ("sum_m", (4, 144, 384), BF), ("sum_o", (240, 384), BF),
    ("got_x", (3, 4, 48, 256), BF), ("got_o", (3, 80, 384), BF), ("got_z", (3, 144, 128), BF),
    ("sum_x", (4, 48, 256), BF), ("sum_zo", (80, 384), BF), ("sum_z", (144, 128), BF),
    ("got_xz", (3, 48, 256), BF), ("got_ox", (3, 32, 384), BF), ("got_zx", (3, 48, 128), BF),
    ("mid", (80, 384), BF), ("got_y", (3, 80, 384), BF),
    ("db", (OROWS, WT), F32), ("dg", (2, C), F32),
]
SHARED = [
    ("out", (NT, C), BF), ("dx", (NT, C), BF), ("u", (NT, C), BF), ("n2", (NT, C), BF), ("datt", (NT, C), BF), ("dq", (NT, C), BF), ("dk", (NT, C), BF),
    ("dv", (NT, C), BF), ("dup", (NT, FFN), BF),
    ("lbias", (3, BROWS, WT), F32), ("db_b", (BROWS, WT), F32), ("parts", (24, 8, 128), F32),
    ("cot_src", (NR, C), BF), ("cot_dst", (NR, C), BF), ("mid_src", (NR, C), BF), ("mid_dst", (NR, C), BF), ("back_src", (NR, C), BF), ("back_dst", (NR, C), BF),
]
SEMS = 15 + 44 + 16


def place(nlat, nlon):
    n = types.SimpleNamespace()
    n.b, n.j = lax.axis_index("lat"), lax.axis_index("lon")
    n.east, n.west = lax.rem(n.j + 1, nlon), lax.rem(n.j + nlon - 1, nlon)
    n.up, n.down = jnp.maximum(n.b - 1, 0), jnp.minimum(n.b + 1, nlat - 1)
    n.first, n.last = n.b == 0, n.b == nlat - 1
    n.inner_up, n.inner_down = n.b > 0, n.b < nlat - 1
    n.yh, n.core = n.b // 2, n.b % 2
    n.z, n.x, n.yl = n.j // 8, (n.j // 2) % 4, n.j % 2

    def device(yh=n.yh, core=n.core, z=n.z, x=n.x, yl=n.yl):
        return (yh * 2 + core, z * 8 + x * 2 + yl)

    n.device = device
    return n


def kernel(nlat, nlon, reduce, *refs):
    names = INPUTS + [o[0] for o in OUTPUTS] + ["first_" + e[0] for e in BLOCK] + ["second_" + e[0] for e in BLOCK] + [e[0] for e in SHARED] + ["send_sem", "recv_sem"]
    r = dict(zip(names, refs, strict=True))
    weights = {k: r[k] for k in INPUTS}
    blocks = []
    for label in ("first_", "second_"):
        blocks.append(types.SimpleNamespace(**weights, **{e[0]: r[e[0]] for e in SHARED}, **{e[0]: r[label + e[0]] for e in BLOCK}))
    one, two = blocks
    n = place(nlat, nlon)
    sems = (r["send_sem"], r["recv_sem"])
    here = (n.b, n.j)
    ex_cot = Exchange(moves_out(n), one.cot_src, one.cot_dst, *sems, 0, here)
    ex_mid = Exchange(moves_out(n), one.mid_src, one.mid_dst, *sems, 5, here)
    ex_back = Exchange(moves_back(n), one.back_src, one.back_dst, *sems, 10, here)

    plane = [(dz, dx) for dz in range(4) for dx in range(4) if (dz, dx) != (0, 0)]
    plane_dev = [n.device(z=(n.z + dz) % 4, x=(n.x + dx) % 4) for dz, dx in plane]
    pal = n.device(core=1 - n.core)
    y_dev = [n.device(yl=1 - n.yl), n.device(yh=1 - n.yh), n.device(yl=1 - n.yl, yh=1 - n.yh)]
    far = plane_dev + y_dev + [pal] if reduce else []
    greet(
        [(None, (n.b, n.east)), (None, (n.b, n.west)), (n.inner_up, (n.up, n.j)), (n.inner_down, (n.down, n.j)), (n.inner_up, (n.up, n.east)), (n.inner_down, (n.down, n.west))]
        + [(None, d) for d in far]
    )

    one.cot_src[...] = shuffle(one.send_nat[...], one.cot[...])
    one.x[...] = shuffle(one.to_win[...], one.tok[...])
    for b, t in enumerate(blocks):
        for i in range(3):
            t.wq[i] = t.w_qkv[b, :, C * i:C * i + C]
    one.lbias[0] = one.bias[0] * LOG2E
    forward_windows(one, 0, lambda w, h: one.lbias[0, h * WT:h * WT + WT, :], False)
    one.mid_src[...] = shuffle(one.send_win[...], one.out[...])
    pl.semaphore_wait(pltpu.get_barrier_semaphore(), jnp.where(jnp.logical_or(n.first, n.last), 4, 6) + len(far))
    ex_mid.start()
    ex_cot.start()

    for group in range(2):
        polar = n.first if group == 0 else n.last

        @pl.when(polar)
        def _():
            for h in range(HEADS):
                rows = slice(h * WT, h * WT + WT)
                two.lbias[1 + group, rows, :] = polar_bias(two.bias[1, rows, :] * LOG2E, group == 1)

        @pl.when(jnp.logical_not(polar))
        def _():
            two.lbias[1 + group] = two.bias[1] * LOG2E

    two.db[...] = jnp.zeros((OROWS, WT), F32)
    two.db_b[...] = jnp.zeros((BROWS, WT), F32)
    ex_mid.finish()
    two.x[...] = shuffle(two.to_slots[...], two.mid_dst[...])
    forward_windows(two, 1, lambda w, h: two.lbias[1 + w // 2, h * WT:h * WT + WT, :], True)

    def dbias_two(w, h, ds):
        rows = slice(h * WT, h * WT + WT)

        @pl.when(w < 2)
        def _():
            two.db[rows, :] += ds

        @pl.when(w >= 2)
        def _():
            two.db_b[rows, :] += ds

    ex_cot.finish()
    two.dout[...] = shuffle(two.to_slots[...], two.cot_dst[...])
    backward_windows(two, 1, dbias_two, lambda w: None)
    two.back_src[...] = shuffle(two.from_slots[...], two.dx[...])
    ex_back.start()
    for group, ref in enumerate((two.db, two.db_b)):
        @pl.when(n.first if group == 0 else n.last)
        def _():
            for h in range(HEADS):
                rows = slice(h * WT, h * WT + WT)
                ref[rows, :] = polar_back(ref[rows, :], group == 1)

    two.db[0:BROWS, :] += two.db_b[...]
    weight_products(two, two.part)
    other_rows(two, two.part)
    red_one = Reduce(n, one, *sems, 15)
    red_two = Reduce(n, two, *sems, 37)
    if reduce:
        red_two.core_start()

    ex_back.finish()
    one.dout[...] = shuffle(one.win_send[...], one.back_dst[...])
    one.db[...] = jnp.zeros((OROWS, WT), F32)

    def dbias_one(w, h, ds):
        one.db[h * WT:h * WT + WT, :] += ds

    def step(w):
        if reduce:
            pl.when(w == 1)(red_two.core_to_first)

    backward_windows(one, 0, dbias_one, step)
    weight_products(one, one.part)
    other_rows(one, one.part)
    if reduce:
        red_one.core_start()
    r["gtok"][...] = shuffle(one.to_nat[...], one.dx[...])
    if not reduce:
        return
    red_two.first_to_second()
    red_one.core_to_first()
    red_two.second_to_third()
    two_final = red_two.finish()
    squares = group_squares(n, two_final)
    red_one.first_to_second()
    red_one.second_to_third()
    one_final = red_one.finish()

    parts = one.parts
    parts[0] = jnp.broadcast_to(squares + group_squares(n, one_final), (8, 128))

    def spread(base, source, target, devices):
        copies = [
            pltpu.make_async_remote_copy(src_ref=parts.at[source], dst_ref=parts.at[target + i], send_sem=sems[0].at[base + i], recv_sem=sems[1].at[base + i], device_id=d, device_id_type=MESH)
            for i, d in enumerate(devices)
        ]
        for c in copies:
            c.start()
        for c in copies:
            c.wait()
        acc = parts[source]
        for i in range(len(devices)):
            acc = acc + parts[target + i]
        return acc

    parts[16] = spread(59, 0, 1, plane_dev)
    acc = spread(74, 16, 17, [pal])
    ceiling = math.sqrt(24 * C * C + 2 * VECB)
    factor = jnp.minimum(1.0, ceiling / (jnp.sqrt(acc) + 1e-06))[0:1, 0:1]
    for b, final in enumerate((one_final, two_final)):
        final = own_lanes(n, final)
        r["m"][b] = final[0:48, :] * factor
        r["o"][b] = final[48:80, :] * factor


def run(nlat, nlon, reduce, tokens, cotangent, norm_gains, w_qkv, w_proj, w_up, w_down, pos_bias):
    args = [tokens.reshape(NT, C), cotangent.reshape(NT, C), norm_gains, w_qkv, w_proj, w_up, jnp.swapaxes(w_down, 1, 2), pos_bias.reshape(2, BROWS, WT)]
    args += [const(p) for p in PERMS]
    vmem = pl.BlockSpec(memory_space=pltpu.VMEM)
    return pl.pallas_call(
        functools.partial(kernel, nlat, nlon, reduce),
        in_specs=[vmem] * len(args),
        out_specs=[vmem] * len(OUTPUTS),
        out_shape=[jax.ShapeDtypeStruct(s, d) for _, s, d in OUTPUTS],
        scratch_shapes=[pltpu.VMEM(s, d) for _, s, d in BLOCK + BLOCK + SHARED] + [pltpu.SemaphoreType.DMA((SEMS,))] * 2,
        compiler_params=pltpu.CompilerParams(vmem_limit_bytes=VMEM_LIMIT, collective_id=1, has_side_effects=True),
        name="two_blocks",
    )(*args)


def shards(nlat, nlon, tokens, *args):
    gtok, m, o = run(nlat, nlon, True, tokens, *args)
    n = place(nlat, nlon)
    m = lax.dynamic_slice_in_dim(m, 4 * n.x + 18 * n.yl, 18, axis=1)[:, :, :C]
    flat = o[:, :, :WT].reshape(2, 32 * WT)
    other = lax.dynamic_slice_in_dim(flat, 975 * (32 * n.b + n.j) - (lat_row(n.b) + x_row(n.core, n.z, n.x)) * WT, 975, axis=1)
    return gtok.reshape(tokens.shape), m.transpose(0, 2, 1), other


def solution(mesh):
    grid = P(None, "lat", "lon", None)
    return jax.shard_map(
        functools.partial(shards, mesh.shape["lat"], mesh.shape["lon"]),
        mesh=mesh,
        in_specs=(grid, grid) + (P(),) * 6,
        out_specs=(grid, P(None, None, ("lat", "lon")), P(None, ("lat", "lon"))),
        check_vma=False,
    )
```

```python
import functools
import math
import types

import jax
import jax.numpy as jnp
import numpy as np
from jax import lax
from jax.experimental import pallas as pl
from jax.experimental.pallas import tpu as pltpu
from jax.sharding import PartitionSpec as P

C = 192
HEADS = 6
HEAD = 32
FFN = 768
WT = 144
NT = 576
NR = 640
QT = 160
MAIN = 112
VECB = 124800
BROWS = HEADS * WT
MROWS = 2304
OROWS = 880
GROWS = MROWS + OROWS
LOG2E = math.log2(math.e)
MESH = pl.DeviceIdType.MESH
BF = jnp.bfloat16
F32 = jnp.float32
VMEM_LIMIT = 56 * 1024 * 1024


def nat(l, r, c):
    return l * 288 + r * 48 + c


def one_hot(sources, width):
    mat = np.zeros((len(sources), width), np.float32)
    for i, s in enumerate(sources):
        if s >= 0:
            mat[i, s] = 1.0
    return mat


@functools.cache
def orders():
    win = [nat(l, r, 12 * w + c) for w in range(4) for l in range(2) for r in range(6) for c in range(12)]

    def cells(rows, cols, size):
        out = [nat(l, r, c) for l in range(2) for r in rows for c in cols]
        return out + [-1] * (size - len(out))

    top, low = range(0, 3), range(3, 6)
    send = []
    for rows in (top, low):
        send += cells(rows, range(0, 18), MAIN)
        send += cells(rows, range(42, 48), QT - MAIN)
        send += cells(rows, range(24, 42), MAIN)
        send += cells(rows, range(18, 24), QT - MAIN)
    slots = []
    for s in range(4):
        for l in range(2):
            for half in range(2):
                for r in range(3):
                    for cc in range(12):
                        col = 12 * (s % 2) + cc
                        base = QT * (2 * (s // 2) + half)
                        if col >= 6:
                            slots.append(base + (l * 3 + r) * 18 + col - 6)
                        else:
                            slots.append(base + MAIN + (l * 3 + r) * 6 + col)
    win_at = {n: i for i, n in enumerate(win)}
    send_win = [win_at[n] if n >= 0 else -1 for n in send]
    to_win = one_hot(win, NT)
    send_from_win = one_hot(send_win, NT)
    send_from_nat = one_hot(send, NT)
    to_slots = one_hot(slots, NR)
    return {
        "to_win": to_win,
        "to_nat": to_win.T.copy(),
        "send_win": send_from_win,
        "win_send": send_from_win.T.copy(),
        "send_nat": send_from_nat,
        "to_slots": to_slots,
        "from_slots": to_slots.T.copy(),
    }


def const(name):
    return jnp.asarray(orders()[name], BF)


def nn(a, b):
    return lax.dot_general(a, b, (((1,), (0,)), ((), ())), preferred_element_type=F32)


def nt(a, b):
    return lax.dot_general(a, b, (((1,), (1,)), ((), ())), preferred_element_type=F32)


def tn(a, b):
    return lax.dot_general(a, b, (((0,), (0,)), ((), ())), preferred_element_type=F32)


def shuffle(mat, x):
    return nn(mat, x).astype(BF)


def stats(x):
    center = x - jnp.mean(x, axis=-1, keepdims=True)
    r = lax.rsqrt(jnp.mean(center * center, axis=-1, keepdims=True) + 1e-05)
    return center * r, r


def norm_back(dn, gain, xhat, r):
    t = dn * gain
    return r * (t - jnp.mean(t, axis=-1, keepdims=True) - xhat * jnp.mean(t * xhat, axis=-1, keepdims=True))


def head_mask(h, dtype):
    lane = lax.broadcasted_iota(jnp.int32, (1, C), 1)
    return ((lane >= h * HEAD) & (lane < (h + 1) * HEAD)).astype(F32).astype(dtype)


def forward_windows(t, b, bias_of, last):
    g0, g1 = t.gains[b, 0:1, :], t.gains[b, 1:2, :]

    def window(w, carry):
        rows = pl.ds(pl.multiple_of(w * WT, WT), WT)
        x = t.x[rows, :].astype(F32)
        u = (stats(x)[0] * g0).astype(BF)
        q = nn(u, t.wq[0]).astype(BF)
        k = nn(u, t.wq[1]).astype(BF)
        v = nn(u, t.wq[2]).astype(BF)
        t.q[rows, :] = q
        t.k[rows, :] = k
        t.v[rows, :] = v
        mixed = jnp.zeros((WT, C), F32)
        for h in range(HEADS):
            s = nt(q * head_mask(h, BF), k) * (HEAD ** -0.5 * LOG2E) + bias_of(w, h)
            e = jnp.exp2(s - jnp.max(s, axis=-1, keepdims=True))
            p = (e * (1.0 / jnp.sum(e, axis=-1, keepdims=True))).astype(BF)
            t.p[pl.ds(pl.multiple_of(w * BROWS + h * WT, WT), WT), :] = p
            mixed = mixed + nn(p, v) * head_mask(h, F32)
        mixed = mixed.astype(BF)
        t.mix[rows, :] = mixed
        attended = nn(mixed, t.w_proj[b]).astype(BF)
        hidden = x + attended.astype(F32)
        t.hid[rows, :] = hidden
        n2 = (stats(hidden)[0] * g1).astype(BF)
        total = hidden
        for j in range(3):
            cols = slice(256 * j, 256 * j + 256)
            up = nn(n2, t.w_up[b, :, cols])
            cdf = 0.5 + 0.5 * lax.erf(up * (0.5 ** 0.5))
            slope = cdf + up * jnp.exp2(up * up * (-0.5 * LOG2E)) * (1.0 / math.sqrt(2 * math.pi))
            act = (up * cdf).astype(BF)
            t.a[rows, cols] = act
            t.gp[rows, cols] = slope.astype(BF)
            if not last:
                total = total + nt(act, t.w_down[b, :, cols])
        if not last:
            t.out[rows, :] = total.astype(BF)
        return carry

    lax.fori_loop(0, 4, window, 0, unroll=2)


def backward_windows(t, b, dbias_of, after_window):
    g0, g1 = t.gains[b, 0:1, :], t.gains[b, 1:2, :]
    t.dg[...] = jnp.zeros((2, C), F32)

    def window(w, carry):
        rows = pl.ds(pl.multiple_of(w * WT, WT), WT)
        dy = t.dout[rows, :]
        dn2 = jnp.zeros((WT, C), F32)
        for j in range(3):
            cols = slice(256 * j, 256 * j + 256)
            da = nn(dy, t.w_down[b, :, cols]).astype(BF).astype(F32)
            dup = (da * t.gp[rows, cols].astype(F32)).astype(BF)
            t.dup[rows, cols] = dup
            dn2 = dn2 + nt(dup, t.w_up[b, :, cols])
        dn2 = dn2.astype(BF).astype(F32)
        xhat, r = stats(t.hid[rows, :])
        t.n2[rows, :] = (xhat * g1).astype(BF)
        t.dg[1:2, :] += jnp.sum(dn2 * xhat, axis=0, keepdims=True)
        dhid = dy.astype(F32) + norm_back(dn2, g1, xhat, r)
        datt = dhid.astype(BF)
        t.datt[rows, :] = datt
        dmix = nt(datt, t.w_proj[b]).astype(BF)
        q = t.q[rows, :]
        k = t.k[rows, :]
        v = t.v[rows, :]
        doms = jnp.concatenate([dmix * head_mask(h, BF) for h in range(HEADS)], axis=0)
        qms = jnp.concatenate([q * head_mask(h, BF) for h in range(HEADS)], axis=0)
        dps = nt(doms, v)
        pw = t.p[pl.ds(pl.multiple_of(w * BROWS, WT), BROWS), :]
        dss = []
        for h in range(HEADS):
            part = slice(h * WT, h * WT + WT)
            p = pw[part].astype(F32)
            pd = p * dps[part]
            ds = pd - p * jnp.sum(pd, axis=-1, keepdims=True)
            dbias_of(w, h, ds)
            dss.append(ds.astype(BF))
        dss = jnp.concatenate(dss, axis=0)
        dqs = nn(dss, k)
        dq = dqs[0:WT] * head_mask(0, F32)
        for h in range(1, HEADS):
            dq = dq + dqs[h * WT:h * WT + WT] * head_mask(h, F32)
        dq = (dq * HEAD ** -0.5).astype(BF)
        dk = (tn(dss, qms) * HEAD ** -0.5).astype(BF)
        dv = tn(pw, doms).astype(BF)
        t.dq[rows, :] = dq
        t.dk[rows, :] = dk
        t.dv[rows, :] = dv
        du = nt(dq, t.wq[0]) + nt(dk, t.wq[1]) + nt(dv, t.wq[2])
        du = du.astype(BF).astype(F32)
        xhat, r = stats(t.x[rows, :].astype(F32))
        t.u[rows, :] = (xhat * g0).astype(BF)
        t.dg[0:1, :] += jnp.sum(du * xhat, axis=0, keepdims=True)
        dx = norm_back(du, g0, xhat, r).astype(BF).astype(F32) + datt.astype(F32)
        t.dx[rows, :] = dx.astype(BF)
        after_window(w)
        return carry

    lax.fori_loop(0, 4, window, 0, unroll=2)


def weight_products(t, part):
    pad = jnp.zeros((NT, 64), BF)

    def left(lhs, x):
        return tn(lhs, jnp.concatenate([x, pad], axis=1))

    def right(lhs, x):
        return tn(lhs, jnp.concatenate([pad, x], axis=1))

    def put(core, row, lft, rgt):
        rows = slice(row, row + lft.shape[0])
        part[core, rows, 0:128] = lft[:, 0:128].astype(BF)
        part[core, rows, 128:256] = (lft[:, 128:256] + rgt[:, 0:128]).astype(BF)
        part[core, rows, 256:384] = rgt[:, 128:256].astype(BF)

    u, n2, dout = t.u[...], t.n2[...], t.dout[...]
    up_low = left(t.dup[:, 0:384], n2)
    up_high = right(t.dup[:, 384:768], n2)
    put(0, 0, left(t.dq[...], u), up_high[0:192])
    put(0, 192, left(t.dk[...], u), up_high[192:384])
    down = right(t.a[:, 0:384], dout)
    put(0, 384, left(t.dv[...], u), down[0:192])
    put(1, 0, left(t.datt[...], t.mix[...]), down[192:384])
    down = right(t.a[:, 384:768], dout)
    put(1, 192, up_low[0:192], down[0:192])
    put(1, 384, up_low[192:384], down[192:384])


def other_rows(t, part):
    flat = jnp.concatenate([t.dg[0:1, :], t.dg[1:2, :], jnp.zeros((1, 3 * WT - 2 * C), F32)], axis=1)
    t.db[BROWS:OROWS, :] = jnp.concatenate([flat[:, 0:WT], flat[:, WT:2 * WT], flat[:, 2 * WT:3 * WT], jnp.zeros((OROWS - BROWS - 3, WT), F32)], axis=0)
    gap = jnp.zeros((240, 48), F32)
    for core in range(2):
        lft = t.db[lat_row(core):lat_row(core) + 240, :]
        rgt = t.db[lat_row(2 + core):lat_row(2 + core) + 240, :]
        part[core, 576:816, :] = jnp.concatenate([lft, gap, rgt, gap], axis=1).astype(BF)


def half_of(shape, axis):
    return (lax.broadcasted_iota(jnp.int32, shape, axis) // 36) % 2


def lane_moves(low):
    src = lax.broadcasted_iota(jnp.int32, (WT, WT), 0)
    dst = lax.broadcasted_iota(jnp.int32, (WT, WT), 1)
    keep = dst - 36 * ((dst // 36) % 2) + (0 if low else 36)
    return (src == keep).astype(F32)


def polar_bias(table, low):
    moved = jnp.dot(table, lane_moves(low), precision=lax.Precision.HIGHEST, preferred_element_type=F32)
    half = half_of((WT, WT), 0)
    if low:
        moved = jnp.where(half == 0, moved, pltpu.roll(moved, 36, 0))
    else:
        moved = jnp.where(half == 1, moved, pltpu.roll(moved, WT - 36, 0))
    return jnp.where(half == half_of((WT, WT), 1), moved, -1e30)


def polar_back(grad, low):
    half = half_of((WT, WT), 0)
    if low:
        folded = jnp.where(half == 0, grad + pltpu.roll(grad, WT - 36, 0), 0.0)
    else:
        folded = jnp.where(half == 1, grad + pltpu.roll(grad, 36, 0), 0.0)
    return lax.dot_general(folded, lane_moves(low), (((1,), (1,)), ((), ())), precision=lax.Precision.HIGHEST, preferred_element_type=F32)


def greet(peers):
    barrier = pltpu.get_barrier_semaphore()
    for cond, dev in peers:
        if cond is None:
            pl.semaphore_signal(barrier, inc=1, device_id=dev, device_id_type=MESH)
        else:
            @pl.when(cond)
            def _():
                pl.semaphore_signal(barrier, inc=1, device_id=dev, device_id_type=MESH)


def guarded(cond, act):
    if cond is None:
        act()
    else:
        pl.when(cond)(act)


class Exchange:
    def __init__(self, moves, src, dst, send_sem, recv_sem, base, here):
        self.sends, self.locals, self.recvs = moves
        self.src, self.dst, self.send_sem, self.recv_sem, self.base, self.here = src, dst, send_sem, recv_sem, base, here

    def remote(self, i, s, d, size, dev):
        return pltpu.make_async_remote_copy(
            src_ref=self.src.at[pl.ds(s, size), :], dst_ref=self.dst.at[pl.ds(d, size), :], send_sem=self.send_sem.at[self.base + i],
            recv_sem=self.recv_sem.at[self.base + i], device_id=dev, device_id_type=MESH)

    def start(self):
        for i, cond, s, d, size, dev in self.sends:
            guarded(cond, lambda: self.remote(i, s, d, size, dev).start())
        for cond, s, d, size in self.locals:
            def keep():
                self.dst[d:d + size, :] = self.src[s:s + size, :]
            guarded(cond, keep)

    def finish(self):
        for i, cond, d, size in self.recvs:
            guarded(cond, lambda: self.remote(i, 0, d, size, self.here).wait_recv())
        for i, cond, s, d, size, dev in self.sends:
            guarded(cond, lambda: self.remote(i, s, d, size, dev).wait_send())


def moves_out(n):
    sends = [
        (0, None, 432, 432, 48, (n.b, n.east)),
        (1, n.inner_up, 112, 592, 48, (n.up, n.east)),
        (2, n.first, 112, 112, 48, (n.b, n.east)),
        (3, n.inner_up, 0, 480, 112, (n.up, n.j)),
        (4, n.inner_down, 480, 0, 160, (n.down, n.j)),
    ]
    locals_ = [(None, 160, 160, 272), (n.first, 0, 0, 112), (n.last, 480, 480, 160)]
    recvs = [(0, None, 432, 48), (1, n.inner_down, 592, 48), (2, n.first, 112, 48), (3, n.inner_down, 480, 112), (4, n.inner_up, 0, 160)]
    return sends, locals_, recvs


def moves_back(n):
    sends = [
        (0, None, 432, 432, 48, (n.b, n.west)),
        (1, n.inner_down, 592, 112, 48, (n.down, n.west)),
        (2, n.first, 112, 112, 48, (n.b, n.west)),
        (3, n.inner_down, 480, 0, 112, (n.down, n.j)),
        (4, n.inner_up, 0, 480, 160, (n.up, n.j)),
    ]
    locals_ = [(None, 160, 160, 272), (n.first, 0, 0, 112), (n.last, 480, 480, 160)]
    recvs = [(0, None, 432, 48), (1, n.inner_up, 112, 48), (2, n.first, 112, 48), (3, n.inner_up, 0, 112), (4, n.inner_down, 480, 160)]
    return sends, locals_, recvs


def lat_row(lat):
    return ((650 * lat) // 48) * 16


def z_row(core, z):
    return ((52 * core + 325 * z) // 96) * 16


def x_row(core, z, x):
    return ((208 * core + 1300 * z + 325 * x) // 384) * 16


def al(v):
    return pl.multiple_of(v, 16)


def total(*terms):
    out = terms[0].astype(F32)
    for term in terms[1:]:
        out = out + term.astype(F32)
    return out


class Reduce:
    def __init__(self, n, t, send_sem, recv_sem, base):
        self.n, self.t, self.send_sem, self.recv_sem, self.base = n, t, send_sem, recv_sem, base

    def remote(self, i, s, d, dev):
        i = self.base + i
        return pltpu.make_async_remote_copy(src_ref=s, dst_ref=d, send_sem=self.send_sem.at[i], recv_sem=self.recv_sem.at[i], device_id=dev, device_id_type=MESH)

    def core_copies(self):
        n, t = self.n, self.t
        return [self.remote(0, t.part.at[1 - n.core], t.got_core, n.device(core=1 - n.core))]

    def first_copies(self):
        n, t = self.n, self.t
        out = []
        for d in range(1, 4):
            i = 3 * d - 2
            z = (n.z + d) % 4
            x = (n.x + d) % 4
            out.append(self.remote(i, t.sum_m.at[:, pl.ds(al(32 * x), 48), pl.ds(128, 256)], t.got_x.at[d - 1], n.device(x=x)))
            dev = n.device(z=z)
            out.append(self.remote(i + 1, t.sum_o.at[pl.ds(al(z_row(n.core, z)), 80), :], t.got_o.at[d - 1], dev))
            out.append(self.remote(i + 2, t.sum_m.at[z, :, pl.ds(0, 128)], t.got_z.at[d - 1], dev))
        return out

    def x_window(self, x):
        return al(x_row(self.n.core, self.n.z, x) - z_row(self.n.core, self.n.z))

    def second_copies(self):
        n, t = self.n, self.t
        out = []
        for d in range(1, 4):
            i = 3 * d + 7
            z = (n.z + d) % 4
            x = (n.x + d) % 4
            out.append(self.remote(i, t.sum_x.at[z], t.got_xz.at[d - 1], n.device(z=z)))
            dev = n.device(x=x)
            out.append(self.remote(i + 1, t.sum_zo.at[pl.ds(self.x_window(x), 32), :], t.got_ox.at[d - 1], dev))
            out.append(self.remote(i + 2, t.sum_z.at[pl.ds(al(32 * x), 48), :], t.got_zx.at[d - 1], dev))
        return out

    def third_copies(self):
        n, t = self.n, self.t
        devices = [n.device(yl=1 - n.yl), n.device(yh=1 - n.yh), n.device(yl=1 - n.yl, yh=1 - n.yh)]
        return [self.remote(19 + i, t.mid, t.got_y.at[i], dev) for i, dev in enumerate(devices)]

    def start(self, copies):
        for c in copies:
            c.start()

    def wait(self, copies):
        for c in copies:
            c.wait()

    def core_start(self):
        self.start(self.core_copies())

    def core_to_first(self):
        n, t = self.n, self.t
        self.wait(self.core_copies())
        for z in range(4):
            rows = slice(144 * z, 144 * z + 144)
            t.sum_m[z] = total(t.part[n.core, rows, :], t.got_core[rows, :]).astype(BF)
        t.sum_o[...] = total(t.part[n.core, 576:816, :], t.got_core[576:816, :]).astype(BF)
        self.start(self.first_copies())

    def first_to_second(self):
        n, t = self.n, self.t
        self.wait(self.first_copies())
        t.sum_x[...] = total(t.sum_m[:, pl.ds(al(32 * n.x), 48), 128:384], *[t.got_x[i] for i in range(3)]).astype(BF)
        t.sum_zo[...] = total(t.sum_o[pl.ds(al(z_row(n.core, n.z)), 80), :], *[t.got_o[i] for i in range(3)]).astype(BF)
        t.sum_z[...] = total(t.sum_m[n.z, :, 0:128], *[t.got_z[i] for i in range(3)]).astype(BF)
        self.start(self.second_copies())

    def second_to_third(self):
        n, t = self.n, self.t
        self.wait(self.second_copies())
        t.mid[0:48, 0:128] = total(t.sum_z[pl.ds(al(32 * n.x), 48), :], *[t.got_zx[i] for i in range(3)]).astype(BF)
        t.mid[0:48, 128:384] = total(t.sum_x[n.z], *[t.got_xz[i] for i in range(3)]).astype(BF)
        t.mid[48:80, :] = total(t.sum_zo[pl.ds(self.x_window(n.x), 32), :], *[t.got_ox[i] for i in range(3)]).astype(BF)
        self.start(self.third_copies())

    def finish(self):
        self.wait(self.third_copies())
        return total(self.t.mid[...], *[self.t.got_y[i] for i in range(3)])


def group_squares(n, final):
    matrix, other = final[0:48, :], final[48:80, :]
    row = lax.broadcasted_iota(jnp.int32, (48, 384), 0)
    low = 4 * n.x
    squares = jnp.sum(jnp.where((row >= low) & (row < low + 36), matrix * matrix, 0.0), axis=0, keepdims=True)
    lane = lax.broadcasted_iota(jnp.int32, (32, 384), 1)
    row = lax.broadcasted_iota(jnp.int32, (32, 384), 0) + x_row(n.core, n.z, n.x)
    for yh in range(2):
        lat = 2 * yh + n.core
        at = lane - C * yh
        index = (row + lat_row(lat)) * WT + at
        low = 975 * (32 * lat + 8 * n.z + 2 * n.x)
        inside = (index >= low) & (index < low + 1950) & (at >= 0) & (at < WT)
        squares = squares + jnp.sum(jnp.where(inside, other * other, 0.0), axis=0, keepdims=True)
    return jnp.sum(squares, axis=1, keepdims=True)


def own_lanes(n, final):
    return jnp.where(n.yh == 1, pltpu.roll(final, C, 1), final)[:, 0:256]


INPUTS = ["tok", "cot", "gains", "w_qkv", "w_proj", "w_up", "w_down", "bias", "to_win", "to_nat", "send_win", "win_send", "send_nat", "to_slots", "from_slots"]
PERMS = INPUTS[8:]
OUTPUTS = [("gtok", (NT, C), BF), ("m", (18, 2, C), F32), ("o", (2, 975), F32)]
COPIED = ["to_win", "tok", "w_qkv", "bias", "w_proj", "w_up", "w_down", "send_win", "send_nat", "cot", "to_slots", "from_slots", "win_send", "to_nat"]
SHAPES = {
    "tok": (NT, C), "cot": (NT, C), "w_qkv": (2, C, 3 * C), "w_proj": (2, C, C), "w_up": (2, C, FFN), "w_down": (2, C, FFN), "bias": (2, BROWS, WT),
    "to_win": (NT, NT), "to_nat": (NT, NT), "send_win": (NR, NT), "win_send": (NT, NR), "send_nat": (NR, NT), "to_slots": (NT, NR), "from_slots": (NR, NT),
}
BLOCK = [
    ("x", (NT, C), BF), ("wq", (3, C, C), BF), ("q", (NT, C), BF), ("k", (NT, C), BF), ("v", (NT, C), BF), ("p", (4 * BROWS, WT), BF),
    ("mix", (NT, C), BF), ("hid", (NT, C), F32), ("a", (NT, FFN), BF), ("gp", (NT, FFN), BF), ("dout", (NT, C), BF), ("part", (2, 816, 384), BF),
    ("got_core", (816, 384), BF), ("sum_m", (4, 144, 384), BF), ("sum_o", (240, 384), BF),
    ("got_x", (3, 4, 48, 256), BF), ("got_o", (3, 80, 384), BF), ("got_z", (3, 144, 128), BF),
    ("sum_x", (4, 48, 256), BF), ("sum_zo", (80, 384), BF), ("sum_z", (144, 128), BF),
    ("got_xz", (3, 48, 256), BF), ("got_ox", (3, 32, 384), BF), ("got_zx", (3, 48, 128), BF),
    ("mid", (80, 384), BF), ("got_y", (3, 80, 384), BF),
    ("db", (OROWS, WT), F32), ("dg", (2, C), F32),
]
SHARED = [
    ("out", (NT, C), BF), ("dx", (NT, C), BF), ("u", (NT, C), BF), ("n2", (NT, C), BF), ("datt", (NT, C), BF), ("dq", (NT, C), BF), ("dk", (NT, C), BF),
    ("dv", (NT, C), BF), ("dup", (NT, FFN), BF),
    ("lbias", (3, BROWS, WT), F32), ("db_b", (BROWS, WT), F32), ("parts", (24, 8, 128), F32), ("own", (2, 80, 256), F32),
    ("cot_src", (NR, C), BF), ("cot_dst", (NR, C), BF), ("mid_src", (NR, C), BF), ("mid_dst", (NR, C), BF), ("back_src", (NR, C), BF), ("back_dst", (NR, C), BF),
]
SEMS = 15 + 44 + 16


def place(nlat, nlon):
    n = types.SimpleNamespace()
    n.b, n.j = lax.axis_index("lat"), lax.axis_index("lon")
    n.east, n.west = lax.rem(n.j + 1, nlon), lax.rem(n.j + nlon - 1, nlon)
    n.up, n.down = jnp.maximum(n.b - 1, 0), jnp.minimum(n.b + 1, nlat - 1)
    n.first, n.last = n.b == 0, n.b == nlat - 1
    n.inner_up, n.inner_down = n.b > 0, n.b < nlat - 1
    n.yh, n.core = n.b // 2, n.b % 2
    n.z, n.x, n.yl = n.j // 8, (n.j // 2) % 4, n.j % 2

    def device(yh=n.yh, core=n.core, z=n.z, x=n.x, yl=n.yl):
        return (yh * 2 + core, z * 8 + x * 2 + yl)

    n.device = device
    return n


def kernel(nlat, nlon, reduce, *refs):
    names = INPUTS + [o[0] for o in OUTPUTS] + ["first_" + e[0] for e in BLOCK] + ["second_" + e[0] for e in BLOCK] + [e[0] for e in SHARED] + ["in_" + k for k in COPIED] + ["send_sem", "recv_sem", "in_sem"]
    r = dict(zip(names, refs, strict=True))
    loads = {k: pltpu.make_async_copy(r[k], r["in_" + k], r["in_sem"].at[i]) for i, k in enumerate(COPIED)}
    for copy in loads.values():
        copy.start()

    def need(*keys):
        for k in keys:
            loads[k].wait()

    weights = {k: r["in_" + k] if k in COPIED else r[k] for k in INPUTS}
    blocks = []
    for label in ("first_", "second_"):
        blocks.append(types.SimpleNamespace(**weights, **{e[0]: r[e[0]] for e in SHARED}, **{e[0]: r[label + e[0]] for e in BLOCK}))
    one, two = blocks
    n = place(nlat, nlon)
    sems = (r["send_sem"], r["recv_sem"])
    here = (n.b, n.j)
    ex_cot = Exchange(moves_out(n), one.cot_src, one.cot_dst, *sems, 0, here)
    ex_mid = Exchange(moves_out(n), one.mid_src, one.mid_dst, *sems, 5, here)
    ex_back = Exchange(moves_back(n), one.back_src, one.back_dst, *sems, 10, here)

    plane = [(dz, dx) for dz in range(4) for dx in range(4) if (dz, dx) != (0, 0)]
    plane_dev = [n.device(z=(n.z + dz) % 4, x=(n.x + dx) % 4) for dz, dx in plane]
    pal = n.device(core=1 - n.core)
    y_dev = [n.device(yl=1 - n.yl), n.device(yh=1 - n.yh), n.device(yl=1 - n.yl, yh=1 - n.yh)]
    far = plane_dev + y_dev + [pal] if reduce else []
    greet(
        [(None, (n.b, n.east)), (None, (n.b, n.west)), (n.inner_up, (n.up, n.j)), (n.inner_down, (n.down, n.j)), (n.inner_up, (n.up, n.east)), (n.inner_down, (n.down, n.west))]
        + [(None, d) for d in far]
    )

    need("to_win", "tok")
    one.x[...] = shuffle(one.to_win[...], one.tok[...])
    need("w_qkv")
    for b, t in enumerate(blocks):
        for i in range(3):
            t.wq[i] = t.w_qkv[b, :, C * i:C * i + C]
    need("bias")
    one.lbias[0] = one.bias[0] * LOG2E
    need("w_proj", "w_up", "w_down")
    forward_windows(one, 0, lambda w, h: one.lbias[0, h * WT:h * WT + WT, :], False)
    need("send_win")
    one.mid_src[...] = shuffle(one.send_win[...], one.out[...])
    pl.semaphore_wait(pltpu.get_barrier_semaphore(), jnp.where(jnp.logical_or(n.first, n.last), 4, 6) + len(far))
    ex_mid.start()
    need("send_nat", "cot")
    one.cot_src[...] = shuffle(one.send_nat[...], one.cot[...])
    ex_cot.start()
    need("to_slots", "from_slots", "win_send", "to_nat")

    for group in range(2):
        polar = n.first if group == 0 else n.last

        @pl.when(polar)
        def _():
            for h in range(HEADS):
                rows = slice(h * WT, h * WT + WT)
                two.lbias[1 + group, rows, :] = polar_bias(two.bias[1, rows, :] * LOG2E, group == 1)

        @pl.when(jnp.logical_not(polar))
        def _():
            two.lbias[1 + group] = two.bias[1] * LOG2E

    two.db[...] = jnp.zeros((OROWS, WT), F32)
    two.db_b[...] = jnp.zeros((BROWS, WT), F32)
    ex_mid.finish()
    two.x[...] = shuffle(two.to_slots[...], two.mid_dst[...])
    forward_windows(two, 1, lambda w, h: two.lbias[1 + w // 2, h * WT:h * WT + WT, :], True)

    def dbias_two(w, h, ds):
        rows = slice(h * WT, h * WT + WT)

        @pl.when(w < 2)
        def _():
            two.db[rows, :] += ds

        @pl.when(w >= 2)
        def _():
            two.db_b[rows, :] += ds

    ex_cot.finish()
    two.dout[...] = shuffle(two.to_slots[...], two.cot_dst[...])
    backward_windows(two, 1, dbias_two, lambda w: None)
    two.back_src[...] = shuffle(two.from_slots[...], two.dx[...])
    ex_back.start()
    for group, ref in enumerate((two.db, two.db_b)):
        @pl.when(n.first if group == 0 else n.last)
        def _():
            for h in range(HEADS):
                rows = slice(h * WT, h * WT + WT)
                ref[rows, :] = polar_back(ref[rows, :], group == 1)

    two.db[0:BROWS, :] += two.db_b[...]
    weight_products(two, two.part)
    other_rows(two, two.part)
    red_one = Reduce(n, one, *sems, 15)
    red_two = Reduce(n, two, *sems, 37)
    if reduce:
        red_two.core_start()

    ex_back.finish()
    one.dout[...] = shuffle(one.win_send[...], one.back_dst[...])
    one.db[...] = jnp.zeros((OROWS, WT), F32)

    def dbias_one(w, h, ds):
        one.db[h * WT:h * WT + WT, :] += ds

    def step(w):
        if reduce:
            pl.when(w == 1)(red_two.core_to_first)

    backward_windows(one, 0, dbias_one, step)
    weight_products(one, one.part)
    other_rows(one, one.part)
    if reduce:
        red_one.core_start()
    r["gtok"][...] = shuffle(one.to_nat[...], one.dx[...])
    if not reduce:
        return
    red_two.first_to_second()
    red_one.core_to_first()
    red_two.second_to_third()
    two_final = red_two.finish()
    squares = group_squares(n, two_final)
    red_one.first_to_second()
    red_one.second_to_third()
    one_final = red_one.finish()

    parts = one.parts
    parts[0] = jnp.broadcast_to(squares + group_squares(n, one_final), (8, 128))

    def spread(base, source, target, devices):
        copies = [
            pltpu.make_async_remote_copy(src_ref=parts.at[source], dst_ref=parts.at[target + i], send_sem=sems[0].at[base + i], recv_sem=sems[1].at[base + i], device_id=d, device_id_type=MESH)
            for i, d in enumerate(devices)
        ]
        for c in copies:
            c.start()
        for c in copies:
            c.wait()
        acc = parts[source]
        for i in range(len(devices)):
            acc = acc + parts[target + i]
        return acc

    parts[16] = spread(59, 0, 1, plane_dev)
    acc = spread(74, 16, 17, [pal])
    ceiling = math.sqrt(24 * C * C + 2 * VECB)
    factor = jnp.minimum(1.0, ceiling / (jnp.sqrt(acc) + 1e-06))[0:1, 0:1]
    first_row = 4 * n.x + 18 * n.yl
    start = 975 * (32 * n.b + n.j) - (lat_row(n.b) + x_row(n.core, n.z, n.x)) * WT
    rows = []
    for b, final in enumerate((one_final, two_final)):
        one.own[b] = own_lanes(n, final) * factor
        for i in range(18):
            r["m"][i, b:b + 1, :] = one.own[b, pl.ds(first_row + i, 1), 0:C]
        rows.append(jnp.concatenate([one.own[b, pl.ds(48 + start // WT + i, 1), 0:WT] for i in range(8)], axis=1))
    flat = jnp.concatenate(rows + [jnp.zeros((6, 8 * WT), F32)], axis=0)
    r["o"][...] = pltpu.roll(flat, 8 * WT - start % WT, 1)[0:2, 0:975]


def run(nlat, nlon, reduce, tokens, cotangent, norm_gains, w_qkv, w_proj, w_up, w_down, pos_bias):
    args = [tokens.reshape(NT, C), cotangent.reshape(NT, C), norm_gains, w_qkv, w_proj, w_up, jnp.swapaxes(w_down, 1, 2), pos_bias.reshape(2, BROWS, WT)]
    args += [const(p) for p in PERMS]
    vmem = pl.BlockSpec(memory_space=pltpu.VMEM)
    anywhere = pl.BlockSpec(memory_space=pl.ANY)
    return pl.pallas_call(
        functools.partial(kernel, nlat, nlon, reduce),
        in_specs=[anywhere if k in COPIED else vmem for k in INPUTS],
        out_specs=[vmem] * len(OUTPUTS),
        out_shape=[jax.ShapeDtypeStruct(s, d) for _, s, d in OUTPUTS],
        scratch_shapes=[pltpu.VMEM(s, d) for _, s, d in BLOCK + BLOCK + SHARED] + [pltpu.VMEM(SHAPES[k], F32 if k == "bias" else BF) for k in COPIED]
        + [pltpu.SemaphoreType.DMA((SEMS,))] * 2 + [pltpu.SemaphoreType.DMA((len(COPIED),))],
        compiler_params=pltpu.CompilerParams(vmem_limit_bytes=VMEM_LIMIT, collective_id=1, has_side_effects=True),
        name="two_blocks",
    )(*args)


def shards(nlat, nlon, tokens, *args):
    gtok, m, o = run(nlat, nlon, True, tokens, *args)
    return gtok.reshape(tokens.shape), m.transpose(1, 2, 0), o


def solution(mesh):
    grid = P(None, "lat", "lon", None)
    return jax.shard_map(
        functools.partial(shards, mesh.shape["lat"], mesh.shape["lon"]),
        mesh=mesh,
        in_specs=(grid, grid) + (P(),) * 6,
        out_specs=(grid, P(None, None, ("lat", "lon")), P(None, ("lat", "lon"))),
        check_vma=False,
    )
```

```python
import functools
import math
import types

import jax
import jax.numpy as jnp
import numpy as np
from jax import lax
from jax.experimental import pallas as pl
from jax.experimental.pallas import tpu as pltpu
from jax.sharding import PartitionSpec as P

C = 192
HEADS = 6
HEAD = 32
FFN = 768
WT = 144
NT = 576
NR = 640
QT = 160
MAIN = 112
VECB = 124800
BROWS = HEADS * WT
MROWS = 2304
OROWS = 880
GROWS = MROWS + OROWS
LOG2E = math.log2(math.e)
MESH = pl.DeviceIdType.MESH
BF = jnp.bfloat16
F32 = jnp.float32
VMEM_LIMIT = 56 * 1024 * 1024


def nat(l, r, c):
    return l * 288 + r * 48 + c


def one_hot(sources, width):
    mat = np.zeros((len(sources), width), np.float32)
    for i, s in enumerate(sources):
        if s >= 0:
            mat[i, s] = 1.0
    return mat


@functools.cache
def orders():
    win = [nat(l, r, 12 * w + c) for w in range(4) for l in range(2) for r in range(6) for c in range(12)]

    def cells(rows, cols, size):
        out = [nat(l, r, c) for l in range(2) for r in rows for c in cols]
        return out + [-1] * (size - len(out))

    top, low = range(0, 3), range(3, 6)
    send = []
    for rows in (top, low):
        send += cells(rows, range(0, 18), MAIN)
        send += cells(rows, range(42, 48), QT - MAIN)
        send += cells(rows, range(24, 42), MAIN)
        send += cells(rows, range(18, 24), QT - MAIN)
    slots = []
    for s in range(4):
        for l in range(2):
            for half in range(2):
                for r in range(3):
                    for cc in range(12):
                        col = 12 * (s % 2) + cc
                        base = QT * (2 * (s // 2) + half)
                        if col >= 6:
                            slots.append(base + (l * 3 + r) * 18 + col - 6)
                        else:
                            slots.append(base + MAIN + (l * 3 + r) * 6 + col)
    win_at = {n: i for i, n in enumerate(win)}
    send_win = [win_at[n] if n >= 0 else -1 for n in send]
    to_win = one_hot(win, NT)
    send_from_win = one_hot(send_win, NT)
    send_from_nat = one_hot(send, NT)
    to_slots = one_hot(slots, NR)
    return {
        "to_win": to_win,
        "to_nat": to_win.T.copy(),
        "send_win": send_from_win,
        "win_send": send_from_win.T.copy(),
        "send_nat": send_from_nat,
        "to_slots": to_slots,
        "from_slots": to_slots.T.copy(),
    }


def const(name):
    return jnp.asarray(orders()[name], BF)


def nn(a, b):
    return lax.dot_general(a, b, (((1,), (0,)), ((), ())), preferred_element_type=F32)


def nt(a, b):
    return lax.dot_general(a, b, (((1,), (1,)), ((), ())), preferred_element_type=F32)


def tn(a, b):
    return lax.dot_general(a, b, (((0,), (0,)), ((), ())), preferred_element_type=F32)


def shuffle(mat, x):
    return nn(mat, x).astype(BF)


def stats(x):
    center = x - jnp.mean(x, axis=-1, keepdims=True)
    r = lax.rsqrt(jnp.mean(center * center, axis=-1, keepdims=True) + 1e-05)
    return center * r, r


def norm_back(dn, gain, xhat, r):
    t = dn * gain
    return r * (t - jnp.mean(t, axis=-1, keepdims=True) - xhat * jnp.mean(t * xhat, axis=-1, keepdims=True))


def head_mask(h, dtype):
    lane = lax.broadcasted_iota(jnp.int32, (1, C), 1)
    return ((lane >= h * HEAD) & (lane < (h + 1) * HEAD)).astype(F32).astype(dtype)


def forward_windows(t, b, bias_of, last):
    g0, g1 = t.gains[b, 0:1, :], t.gains[b, 1:2, :]

    def window(w, carry):
        rows = pl.ds(pl.multiple_of(w * WT, WT), WT)
        x = t.x[rows, :].astype(F32)
        u = (stats(x)[0] * g0).astype(BF)
        q = nn(u, t.wq[0]).astype(BF)
        k = nn(u, t.wq[1]).astype(BF)
        v = nn(u, t.wq[2]).astype(BF)
        t.q[rows, :] = q
        t.k[rows, :] = k
        t.v[rows, :] = v
        mixed = jnp.zeros((WT, C), F32)
        for h in range(HEADS):
            s = nt(q * head_mask(h, BF), k) * (HEAD ** -0.5 * LOG2E) + bias_of(w, h)
            e = jnp.exp2(s - jnp.max(s, axis=-1, keepdims=True))
            p = (e * (1.0 / jnp.sum(e, axis=-1, keepdims=True))).astype(BF)
            t.p[pl.ds(pl.multiple_of(w * BROWS + h * WT, WT), WT), :] = p
            mixed = mixed + nn(p, v) * head_mask(h, F32)
        mixed = mixed.astype(BF)
        t.mix[rows, :] = mixed
        attended = nn(mixed, t.w_proj[b]).astype(BF)
        hidden = x + attended.astype(F32)
        t.hid[rows, :] = hidden
        n2 = (stats(hidden)[0] * g1).astype(BF)
        total = hidden
        for j in range(3):
            cols = slice(256 * j, 256 * j + 256)
            up = nn(n2, t.w_up[b, :, cols])
            cdf = 0.5 + 0.5 * lax.erf(up * (0.5 ** 0.5))
            slope = cdf + up * jnp.exp2(up * up * (-0.5 * LOG2E)) * (1.0 / math.sqrt(2 * math.pi))
            act = (up * cdf).astype(BF)
            t.a[rows, cols] = act
            t.gp[rows, cols] = slope.astype(BF)
            if not last:
                total = total + nt(act, t.w_down[b, :, cols])
        if not last:
            t.out[rows, :] = total.astype(BF)
        return carry

    lax.fori_loop(0, 4, window, 0, unroll=2)


def backward_windows(t, b, dbias_of):
    g0, g1 = t.gains[b, 0:1, :], t.gains[b, 1:2, :]
    t.dg[...] = jnp.zeros((2, C), F32)

    def window(w, carry):
        rows = pl.ds(pl.multiple_of(w * WT, WT), WT)
        dy = t.dout[rows, :]
        dn2 = jnp.zeros((WT, C), F32)
        for j in range(3):
            cols = slice(256 * j, 256 * j + 256)
            da = nn(dy, t.w_down[b, :, cols]).astype(BF).astype(F32)
            dup = (da * t.gp[rows, cols].astype(F32)).astype(BF)
            t.dup[rows, cols] = dup
            dn2 = dn2 + nt(dup, t.w_up[b, :, cols])
        dn2 = dn2.astype(BF).astype(F32)
        xhat, r = stats(t.hid[rows, :])
        t.n2[rows, :] = (xhat * g1).astype(BF)
        t.dg[1:2, :] += jnp.sum(dn2 * xhat, axis=0, keepdims=True)
        dhid = dy.astype(F32) + norm_back(dn2, g1, xhat, r)
        datt = dhid.astype(BF)
        t.datt[rows, :] = datt
        dmix = nt(datt, t.w_proj[b]).astype(BF)
        q = t.q[rows, :]
        k = t.k[rows, :]
        v = t.v[rows, :]
        doms = jnp.concatenate([dmix * head_mask(h, BF) for h in range(HEADS)], axis=0)
        qms = jnp.concatenate([q * head_mask(h, BF) for h in range(HEADS)], axis=0)
        dps = nt(doms, v)
        pw = t.p[pl.ds(pl.multiple_of(w * BROWS, WT), BROWS), :]
        dss = []
        for h in range(HEADS):
            part = slice(h * WT, h * WT + WT)
            p = pw[part].astype(F32)
            pd = p * dps[part]
            ds = pd - p * jnp.sum(pd, axis=-1, keepdims=True)
            dbias_of(w, h, ds)
            dss.append(ds.astype(BF))
        dss = jnp.concatenate(dss, axis=0)
        dqs = nn(dss, k)
        dq = dqs[0:WT] * head_mask(0, F32)
        for h in range(1, HEADS):
            dq = dq + dqs[h * WT:h * WT + WT] * head_mask(h, F32)
        dq = (dq * HEAD ** -0.5).astype(BF)
        dk = (tn(dss, qms) * HEAD ** -0.5).astype(BF)
        dv = tn(pw, doms).astype(BF)
        t.dq[rows, :] = dq
        t.dk[rows, :] = dk
        t.dv[rows, :] = dv
        du = nt(dq, t.wq[0]) + nt(dk, t.wq[1]) + nt(dv, t.wq[2])
        du = du.astype(BF).astype(F32)
        xhat, r = stats(t.x[rows, :].astype(F32))
        t.u[rows, :] = (xhat * g0).astype(BF)
        t.dg[0:1, :] += jnp.sum(du * xhat, axis=0, keepdims=True)
        dx = norm_back(du, g0, xhat, r).astype(BF).astype(F32) + datt.astype(F32)
        t.dx[rows, :] = dx.astype(BF)
        return carry

    lax.fori_loop(0, 4, window, 0, unroll=2)


def weight_products(t, part):
    pad = jnp.zeros((NT, 64), BF)

    def left(lhs, x):
        return tn(lhs, jnp.concatenate([x, pad], axis=1))

    def right(lhs, x):
        return tn(lhs, jnp.concatenate([pad, x], axis=1))

    def put(core, row, lft, rgt):
        rows = slice(row, row + lft.shape[0])
        part[core, rows, 0:128] = lft[:, 0:128].astype(BF)
        part[core, rows, 128:256] = (lft[:, 128:256] + rgt[:, 0:128]).astype(BF)
        part[core, rows, 256:384] = rgt[:, 128:256].astype(BF)

    u, n2, dout = t.u[...], t.n2[...], t.dout[...]
    up_low = left(t.dup[:, 0:384], n2)
    up_high = right(t.dup[:, 384:768], n2)
    put(0, 0, left(t.dq[...], u), up_high[0:192])
    put(0, 192, left(t.dk[...], u), up_high[192:384])
    down = right(t.a[:, 0:384], dout)
    put(0, 384, left(t.dv[...], u), down[0:192])
    put(1, 0, left(t.datt[...], t.mix[...]), down[192:384])
    down = right(t.a[:, 384:768], dout)
    put(1, 192, up_low[0:192], down[0:192])
    put(1, 384, up_low[192:384], down[192:384])


def other_rows(t, part):
    flat = jnp.concatenate([t.dg[0:1, :], t.dg[1:2, :], jnp.zeros((1, 3 * WT - 2 * C), F32)], axis=1)
    t.db[BROWS:OROWS, :] = jnp.concatenate([flat[:, 0:WT], flat[:, WT:2 * WT], flat[:, 2 * WT:3 * WT], jnp.zeros((OROWS - BROWS - 3, WT), F32)], axis=0)
    gap = jnp.zeros((240, 48), F32)
    for core in range(2):
        lft = t.db[lat_row(core):lat_row(core) + 240, :]
        rgt = t.db[lat_row(2 + core):lat_row(2 + core) + 240, :]
        part[core, 576:816, :] = jnp.concatenate([lft, gap, rgt, gap], axis=1).astype(BF)


def half_of(shape, axis):
    return (lax.broadcasted_iota(jnp.int32, shape, axis) // 36) % 2


def lane_moves(low):
    src = lax.broadcasted_iota(jnp.int32, (WT, WT), 0)
    dst = lax.broadcasted_iota(jnp.int32, (WT, WT), 1)
    keep = dst - 36 * ((dst // 36) % 2) + (0 if low else 36)
    return (src == keep).astype(F32)


def polar_bias(table, low):
    moved = jnp.dot(table, lane_moves(low), precision=lax.Precision.HIGHEST, preferred_element_type=F32)
    half = half_of((WT, WT), 0)
    if low:
        moved = jnp.where(half == 0, moved, pltpu.roll(moved, 36, 0))
    else:
        moved = jnp.where(half == 1, moved, pltpu.roll(moved, WT - 36, 0))
    return jnp.where(half == half_of((WT, WT), 1), moved, -1e30)


def polar_back(grad, low):
    half = half_of((WT, WT), 0)
    if low:
        folded = jnp.where(half == 0, grad + pltpu.roll(grad, WT - 36, 0), 0.0)
    else:
        folded = jnp.where(half == 1, grad + pltpu.roll(grad, 36, 0), 0.0)
    return lax.dot_general(folded, lane_moves(low), (((1,), (1,)), ((), ())), precision=lax.Precision.HIGHEST, preferred_element_type=F32)


def greet(peers):
    barrier = pltpu.get_barrier_semaphore()
    for cond, dev in peers:
        if cond is None:
            pl.semaphore_signal(barrier, inc=1, device_id=dev, device_id_type=MESH)
        else:
            @pl.when(cond)
            def _():
                pl.semaphore_signal(barrier, inc=1, device_id=dev, device_id_type=MESH)


def guarded(cond, act):
    if cond is None:
        act()
    else:
        pl.when(cond)(act)


class Exchange:
    def __init__(self, moves, src, dst, send_sem, recv_sem, base, here):
        self.sends, self.locals, self.recvs = moves
        self.src, self.dst, self.send_sem, self.recv_sem, self.base, self.here = src, dst, send_sem, recv_sem, base, here

    def remote(self, i, s, d, size, dev):
        return pltpu.make_async_remote_copy(
            src_ref=self.src.at[pl.ds(s, size), :], dst_ref=self.dst.at[pl.ds(d, size), :], send_sem=self.send_sem.at[self.base + i],
            recv_sem=self.recv_sem.at[self.base + i], device_id=dev, device_id_type=MESH)

    def start(self):
        for i, cond, s, d, size, dev in self.sends:
            guarded(cond, lambda: self.remote(i, s, d, size, dev).start())
        for cond, s, d, size in self.locals:
            def keep():
                self.dst[d:d + size, :] = self.src[s:s + size, :]
            guarded(cond, keep)

    def finish(self):
        for i, cond, d, size in self.recvs:
            guarded(cond, lambda: self.remote(i, 0, d, size, self.here).wait_recv())
        for i, cond, s, d, size, dev in self.sends:
            guarded(cond, lambda: self.remote(i, s, d, size, dev).wait_send())


def moves_out(n):
    sends = [
        (0, None, 432, 432, 48, (n.b, n.east)),
        (1, n.inner_up, 112, 592, 48, (n.up, n.east)),
        (2, n.first, 112, 112, 48, (n.b, n.east)),
        (3, n.inner_up, 0, 480, 112, (n.up, n.j)),
        (4, n.inner_down, 480, 0, 160, (n.down, n.j)),
    ]
    locals_ = [(None, 160, 160, 272), (n.first, 0, 0, 112), (n.last, 480, 480, 160)]
    recvs = [(0, None, 432, 48), (1, n.inner_down, 592, 48), (2, n.first, 112, 48), (3, n.inner_down, 480, 112), (4, n.inner_up, 0, 160)]
    return sends, locals_, recvs


def moves_back(n):
    sends = [
        (0, None, 432, 432, 48, (n.b, n.west)),
        (1, n.inner_down, 592, 112, 48, (n.down, n.west)),
        (2, n.first, 112, 112, 48, (n.b, n.west)),
        (3, n.inner_down, 480, 0, 112, (n.down, n.j)),
        (4, n.inner_up, 0, 480, 160, (n.up, n.j)),
    ]
    locals_ = [(None, 160, 160, 272), (n.first, 0, 0, 112), (n.last, 480, 480, 160)]
    recvs = [(0, None, 432, 48), (1, n.inner_up, 112, 48), (2, n.first, 112, 48), (3, n.inner_up, 0, 112), (4, n.inner_down, 480, 160)]
    return sends, locals_, recvs


def lat_row(lat):
    return ((650 * lat) // 48) * 16


def z_row(core, z):
    return ((52 * core + 325 * z) // 96) * 16


def x_row(core, z, x):
    return ((208 * core + 1300 * z + 325 * x) // 384) * 16


def al(v):
    return pl.multiple_of(v, 16)


def total(*terms):
    out = terms[0].astype(F32)
    for term in terms[1:]:
        out = out + term.astype(F32)
    return out


class Reduce:
    def __init__(self, n, t, send_sem, recv_sem, base):
        self.n, self.t, self.send_sem, self.recv_sem, self.base = n, t, send_sem, recv_sem, base

    def remote(self, i, s, d, dev):
        i = self.base + i
        return pltpu.make_async_remote_copy(src_ref=s, dst_ref=d, send_sem=self.send_sem.at[i], recv_sem=self.recv_sem.at[i], device_id=dev, device_id_type=MESH)

    def core_copies(self):
        n, t = self.n, self.t
        return [self.remote(0, t.part.at[1 - n.core], t.got_core, n.device(core=1 - n.core))]

    def first_copies(self):
        n, t = self.n, self.t
        out = []
        for d in range(1, 4):
            i = 3 * d - 2
            z = (n.z + d) % 4
            x = (n.x + d) % 4
            out.append(self.remote(i, t.sum_m.at[:, pl.ds(al(32 * x), 48), pl.ds(128, 256)], t.got_x.at[d - 1], n.device(x=x)))
            dev = n.device(z=z)
            out.append(self.remote(i + 1, t.sum_o.at[pl.ds(al(z_row(n.core, z)), 80), :], t.got_o.at[d - 1], dev))
            out.append(self.remote(i + 2, t.sum_m.at[z, :, pl.ds(0, 128)], t.got_z.at[d - 1], dev))
        return out

    def x_window(self, x):
        return al(x_row(self.n.core, self.n.z, x) - z_row(self.n.core, self.n.z))

    def second_copies(self):
        n, t = self.n, self.t
        out = []
        for d in range(1, 4):
            i = 3 * d + 7
            z = (n.z + d) % 4
            x = (n.x + d) % 4
            out.append(self.remote(i, t.sum_x.at[z], t.got_xz.at[d - 1], n.device(z=z)))
            dev = n.device(x=x)
            out.append(self.remote(i + 1, t.sum_zo.at[pl.ds(self.x_window(x), 32), :], t.got_ox.at[d - 1], dev))
            out.append(self.remote(i + 2, t.sum_z.at[pl.ds(al(32 * x), 48), :], t.got_zx.at[d - 1], dev))
        return out

    def third_copies(self):
        n, t = self.n, self.t
        devices = [n.device(yl=1 - n.yl), n.device(yh=1 - n.yh), n.device(yl=1 - n.yl, yh=1 - n.yh)]
        return [self.remote(19 + i, t.mid, t.got_y.at[i], dev) for i, dev in enumerate(devices)]

    def start(self, copies):
        for c in copies:
            c.start()

    def wait(self, copies):
        for c in copies:
            c.wait()

    def core_start(self):
        self.start(self.core_copies())

    def core_to_first(self):
        n, t = self.n, self.t
        self.wait(self.core_copies())
        for z in range(4):
            rows = slice(144 * z, 144 * z + 144)
            t.sum_m[z] = total(t.part[n.core, rows, :], t.got_core[rows, :]).astype(BF)
        t.sum_o[...] = total(t.part[n.core, 576:816, :], t.got_core[576:816, :]).astype(BF)
        self.start(self.first_copies())

    def first_to_second(self):
        n, t = self.n, self.t
        self.wait(self.first_copies())
        t.sum_x[...] = total(t.sum_m[:, pl.ds(al(32 * n.x), 48), 128:384], *[t.got_x[i] for i in range(3)]).astype(BF)
        t.sum_zo[...] = total(t.sum_o[pl.ds(al(z_row(n.core, n.z)), 80), :], *[t.got_o[i] for i in range(3)]).astype(BF)
        t.sum_z[...] = total(t.sum_m[n.z, :, 0:128], *[t.got_z[i] for i in range(3)]).astype(BF)
        self.start(self.second_copies())

    def second_to_third(self):
        n, t = self.n, self.t
        self.wait(self.second_copies())
        t.mid[0:48, 0:128] = total(t.sum_z[pl.ds(al(32 * n.x), 48), :], *[t.got_zx[i] for i in range(3)]).astype(BF)
        t.mid[0:48, 128:384] = total(t.sum_x[n.z], *[t.got_xz[i] for i in range(3)]).astype(BF)
        t.mid[48:80, :] = total(t.sum_zo[pl.ds(self.x_window(n.x), 32), :], *[t.got_ox[i] for i in range(3)]).astype(BF)
        self.start(self.third_copies())

    def finish(self):
        self.wait(self.third_copies())
        return total(self.t.mid[...], *[self.t.got_y[i] for i in range(3)])


def group_squares(n, final):
    matrix, other = final[0:48, :], final[48:80, :]
    row = lax.broadcasted_iota(jnp.int32, (48, 384), 0)
    low = 4 * n.x
    squares = jnp.sum(jnp.where((row >= low) & (row < low + 36), matrix * matrix, 0.0), axis=0, keepdims=True)
    lane = lax.broadcasted_iota(jnp.int32, (32, 384), 1)
    row = lax.broadcasted_iota(jnp.int32, (32, 384), 0) + x_row(n.core, n.z, n.x)
    for yh in range(2):
        lat = 2 * yh + n.core
        at = lane - C * yh
        index = (row + lat_row(lat)) * WT + at
        low = 975 * (32 * lat + 8 * n.z + 2 * n.x)
        inside = (index >= low) & (index < low + 1950) & (at >= 0) & (at < WT)
        squares = squares + jnp.sum(jnp.where(inside, other * other, 0.0), axis=0, keepdims=True)
    return jnp.sum(squares, axis=1, keepdims=True)


def own_lanes(n, final):
    return jnp.where(n.yh == 1, pltpu.roll(final, C, 1), final)[:, 0:256]


INPUTS = ["tok", "cot", "gains", "w_qkv", "w_proj", "w_up", "w_down", "bias", "to_win", "to_nat", "send_win", "win_send", "send_nat", "to_slots", "from_slots"]
PERMS = INPUTS[8:]
OUTPUTS = [("gtok", (NT, C), BF), ("m", (18, 2, C), F32), ("o", (2, 975), F32)]
COPIED = ["to_win", "tok", "w_qkv", "bias", "w_proj", "w_up", "w_down", "send_win", "send_nat", "cot", "to_slots", "from_slots", "win_send", "to_nat"]
SHAPES = {
    "tok": (NT, C), "cot": (NT, C), "w_qkv": (2, C, 3 * C), "w_proj": (2, C, C), "w_up": (2, C, FFN), "w_down": (2, C, FFN), "bias": (2, BROWS, WT),
    "to_win": (NT, NT), "to_nat": (NT, NT), "send_win": (NR, NT), "win_send": (NT, NR), "send_nat": (NR, NT), "to_slots": (NT, NR), "from_slots": (NR, NT),
}
BLOCK = [
    ("x", (NT, C), BF), ("wq", (3, C, C), BF), ("q", (NT, C), BF), ("k", (NT, C), BF), ("v", (NT, C), BF), ("p", (4 * BROWS, WT), BF),
    ("mix", (NT, C), BF), ("hid", (NT, C), F32), ("a", (NT, FFN), BF), ("gp", (NT, FFN), BF), ("dout", (NT, C), BF), ("part", (2, 816, 384), BF),
    ("got_core", (816, 384), BF), ("sum_m", (4, 144, 384), BF), ("sum_o", (240, 384), BF),
    ("got_x", (3, 4, 48, 256), BF), ("got_o", (3, 80, 384), BF), ("got_z", (3, 144, 128), BF),
    ("sum_x", (4, 48, 256), BF), ("sum_zo", (80, 384), BF), ("sum_z", (144, 128), BF),
    ("got_xz", (3, 48, 256), BF), ("got_ox", (3, 32, 384), BF), ("got_zx", (3, 48, 128), BF),
    ("mid", (80, 384), BF), ("got_y", (3, 80, 384), BF),
    ("db", (OROWS, WT), F32), ("dg", (2, C), F32),
]
SHARED = [
    ("out", (NT, C), BF), ("dx", (NT, C), BF), ("u", (NT, C), BF), ("n2", (NT, C), BF), ("datt", (NT, C), BF), ("dq", (NT, C), BF), ("dk", (NT, C), BF),
    ("dv", (NT, C), BF), ("dup", (NT, FFN), BF),
    ("lbias", (3, BROWS, WT), F32), ("db_pair", (2, BROWS, WT), F32), ("parts", (32, 1, 128), F32), ("own", (2, 80, 256), F32),
    ("cot_src", (NR, 256), BF), ("cot_dst", (NR, 256), BF), ("mid_src", (NR, 256), BF), ("mid_dst", (NR, 256), BF), ("back_src", (NR, 256), BF), ("back_dst", (NR, 256), BF),
]
SEMS = 15 + 44 + 31


def place(nlat, nlon):
    n = types.SimpleNamespace()
    n.b, n.j = lax.axis_index("lat"), lax.axis_index("lon")
    n.east, n.west = lax.rem(n.j + 1, nlon), lax.rem(n.j + nlon - 1, nlon)
    n.up, n.down = jnp.maximum(n.b - 1, 0), jnp.minimum(n.b + 1, nlat - 1)
    n.first, n.last = n.b == 0, n.b == nlat - 1
    n.inner_up, n.inner_down = n.b > 0, n.b < nlat - 1
    n.yh, n.core = n.b // 2, n.b % 2
    n.z, n.x, n.yl = n.j // 8, (n.j // 2) % 4, n.j % 2

    def device(yh=n.yh, core=n.core, z=n.z, x=n.x, yl=n.yl):
        return (yh * 2 + core, z * 8 + x * 2 + yl)

    n.device = device
    return n


def kernel(nlat, nlon, reduce, *refs):
    names = INPUTS + [o[0] for o in OUTPUTS] + ["first_" + e[0] for e in BLOCK] + ["second_" + e[0] for e in BLOCK] + [e[0] for e in SHARED] + ["in_" + k for k in COPIED] + ["send_sem", "recv_sem", "in_sem"]
    r = dict(zip(names, refs, strict=True))
    loads = {k: pltpu.make_async_copy(r[k], r["in_" + k], r["in_sem"].at[i]) for i, k in enumerate(COPIED)}
    for copy in loads.values():
        copy.start()

    def need(*keys):
        for k in keys:
            loads[k].wait()

    weights = {k: r["in_" + k] if k in COPIED else r[k] for k in INPUTS}
    blocks = []
    for label in ("first_", "second_"):
        blocks.append(types.SimpleNamespace(**weights, **{e[0]: r[e[0]] for e in SHARED}, **{e[0]: r[label + e[0]] for e in BLOCK}))
    one, two = blocks
    n = place(nlat, nlon)
    sems = (r["send_sem"], r["recv_sem"])
    here = (n.b, n.j)
    ex_cot = Exchange(moves_out(n), one.cot_src, one.cot_dst, *sems, 0, here)
    ex_mid = Exchange(moves_out(n), one.mid_src, one.mid_dst, *sems, 5, here)
    ex_back = Exchange(moves_back(n), one.back_src, one.back_dst, *sems, 10, here)

    level = [(e, dz, dx) for e in range(2) for dz in range(4) for dx in range(4) if (e, dz, dx) != (0, 0, 0)]
    level_dev = [n.device(core=(n.core + e) % 2, z=(n.z + dz) % 4, x=(n.x + dx) % 4) for e, dz, dx in level]
    y_dev = [n.device(yl=1 - n.yl), n.device(yh=1 - n.yh), n.device(yl=1 - n.yl, yh=1 - n.yh)]
    far = level_dev + y_dev if reduce else []
    greet(
        [(None, (n.b, n.east)), (None, (n.b, n.west)), (n.inner_up, (n.up, n.j)), (n.inner_down, (n.down, n.j)), (n.inner_up, (n.up, n.east)), (n.inner_down, (n.down, n.west))]
        + [(None, d) for d in far]
    )

    need("to_win", "tok")
    one.x[...] = shuffle(one.to_win[...], one.tok[...])
    need("w_qkv")
    for b, t in enumerate(blocks):
        for i in range(3):
            t.wq[i] = t.w_qkv[b, :, C * i:C * i + C]
    need("bias")
    one.lbias[0] = one.bias[0] * LOG2E
    need("w_proj", "w_up", "w_down")
    forward_windows(one, 0, lambda w, h: one.lbias[0, h * WT:h * WT + WT, :], False)
    need("send_win")
    one.mid_src[:, 0:C] = shuffle(one.send_win[...], one.out[...])
    pl.semaphore_wait(pltpu.get_barrier_semaphore(), jnp.where(jnp.logical_or(n.first, n.last), 4, 6) + len(far))
    ex_mid.start()
    need("send_nat", "cot")
    one.cot_src[:, 0:C] = shuffle(one.send_nat[...], one.cot[...])
    ex_cot.start()
    need("to_slots", "from_slots", "win_send", "to_nat")

    for group in range(2):
        polar = n.first if group == 0 else n.last

        @pl.when(polar)
        def _():
            for h in range(HEADS):
                rows = slice(h * WT, h * WT + WT)
                two.lbias[1 + group, rows, :] = polar_bias(two.bias[1, rows, :] * LOG2E, group == 1)

        @pl.when(jnp.logical_not(polar))
        def _():
            two.lbias[1 + group] = two.bias[1] * LOG2E

    two.db_pair[...] = jnp.zeros((2, BROWS, WT), F32)
    ex_mid.finish()
    two.x[...] = shuffle(two.to_slots[...], two.mid_dst[:, 0:C])
    forward_windows(two, 1, lambda w, h: two.lbias[1 + w // 2, h * WT:h * WT + WT, :], True)

    def dbias_two(w, h, ds):
        two.db_pair[w // 2, h * WT:h * WT + WT, :] += ds

    ex_cot.finish()
    two.dout[...] = shuffle(two.to_slots[...], two.cot_dst[:, 0:C])
    backward_windows(two, 1, dbias_two)
    two.back_src[:, 0:C] = shuffle(two.from_slots[...], two.dx[...])
    ex_back.start()
    for group in range(2):
        @pl.when(n.first if group == 0 else n.last)
        def _():
            for h in range(HEADS):
                rows = slice(h * WT, h * WT + WT)
                two.db_pair[group, rows, :] = polar_back(two.db_pair[group, rows, :], group == 1)

    two.db[0:BROWS, :] = two.db_pair[0] + two.db_pair[1]
    weight_products(two, two.part)
    other_rows(two, two.part)
    red_one = Reduce(n, one, *sems, 15)
    red_two = Reduce(n, two, *sems, 37)
    if reduce:
        red_two.core_start()

    ex_back.finish()
    if reduce:
        red_two.core_to_first()
    one.dout[...] = shuffle(one.win_send[...], one.back_dst[:, 0:C])
    one.db[...] = jnp.zeros((OROWS, WT), F32)

    def dbias_one(w, h, ds):
        one.db[h * WT:h * WT + WT, :] += ds

    backward_windows(one, 0, dbias_one)
    weight_products(one, one.part)
    other_rows(one, one.part)
    if reduce:
        red_one.core_start()
    r["gtok"][...] = shuffle(one.to_nat[...], one.dx[...])
    if not reduce:
        return
    red_two.first_to_second()
    red_one.core_to_first()
    red_two.second_to_third()
    two_final = red_two.finish()
    squares = group_squares(n, two_final)
    red_one.first_to_second()
    red_one.second_to_third()
    one_final = red_one.finish()

    parts = one.parts
    parts[0] = jnp.broadcast_to(squares + group_squares(n, one_final), (1, 128))
    copies = [
        pltpu.make_async_remote_copy(src_ref=parts.at[0], dst_ref=parts.at[1 + i], send_sem=sems[0].at[59 + i], recv_sem=sems[1].at[59 + i], device_id=d, device_id_type=MESH)
        for i, d in enumerate(level_dev)
    ]
    for c in copies:
        c.start()
    for c in copies:
        c.wait()
    acc = parts[0]
    for i in range(len(copies)):
        acc = acc + parts[1 + i]
    ceiling = math.sqrt(24 * C * C + 2 * VECB)
    factor = jnp.minimum(1.0, ceiling / (jnp.sqrt(acc) + 1e-06))[0:1, 0:1]
    first_row = 4 * n.x + 18 * n.yl
    start = 975 * (32 * n.b + n.j) - (lat_row(n.b) + x_row(n.core, n.z, n.x)) * WT
    rows = []
    for b, final in enumerate((one_final, two_final)):
        one.own[b] = own_lanes(n, final) * factor
        for i in range(18):
            r["m"][i, b:b + 1, :] = one.own[b, pl.ds(first_row + i, 1), 0:C]
        rows.append(jnp.concatenate([one.own[b, pl.ds(48 + start // WT + i, 1), 0:WT] for i in range(8)], axis=1))
    flat = jnp.concatenate(rows + [jnp.zeros((6, 8 * WT), F32)], axis=0)
    r["o"][...] = pltpu.roll(flat, 8 * WT - start % WT, 1)[0:2, 0:975]


def run(nlat, nlon, reduce, tokens, cotangent, norm_gains, w_qkv, w_proj, w_up, w_down, pos_bias):
    args = [tokens.reshape(NT, C), cotangent.reshape(NT, C), norm_gains, w_qkv, w_proj, w_up, jnp.swapaxes(w_down, 1, 2), pos_bias.reshape(2, BROWS, WT)]
    args += [const(p) for p in PERMS]
    vmem = pl.BlockSpec(memory_space=pltpu.VMEM)
    anywhere = pl.BlockSpec(memory_space=pl.ANY)
    return pl.pallas_call(
        functools.partial(kernel, nlat, nlon, reduce),
        in_specs=[anywhere if k in COPIED else vmem for k in INPUTS],
        out_specs=[vmem] * len(OUTPUTS),
        out_shape=[jax.ShapeDtypeStruct(s, d) for _, s, d in OUTPUTS],
        scratch_shapes=[pltpu.VMEM(s, d) for _, s, d in BLOCK + BLOCK + SHARED] + [pltpu.VMEM(SHAPES[k], F32 if k == "bias" else BF) for k in COPIED]
        + [pltpu.SemaphoreType.DMA((SEMS,))] * 2 + [pltpu.SemaphoreType.DMA((len(COPIED),))],
        compiler_params=pltpu.CompilerParams(vmem_limit_bytes=VMEM_LIMIT, collective_id=1, has_side_effects=True),
        name="two_blocks",
    )(*args)


def copy_out(*refs):
    half = len(OUTPUTS)
    copies = [pltpu.make_async_copy(refs[i], refs[half + i], refs[2 * half].at[i]) for i in range(half)]
    for c in copies:
        c.start()
    for c in copies:
        c.wait()


def run_copy_out(results):
    anywhere = pl.BlockSpec(memory_space=pl.ANY)
    return pl.pallas_call(
        copy_out,
        in_specs=[anywhere] * len(results),
        out_specs=[anywhere] * len(results),
        out_shape=[jax.ShapeDtypeStruct(s, d) for _, s, d in OUTPUTS],
        scratch_shapes=[pltpu.SemaphoreType.DMA((len(OUTPUTS),))],
        name="copy_out",
    )(*results)


def shards(nlat, nlon, tokens, *args):
    gtok, m, o = run_copy_out(run(nlat, nlon, True, tokens, *args))
    return gtok.reshape(tokens.shape), m.transpose(1, 2, 0), o


def solution(mesh):
    grid = P(None, "lat", "lon", None)
    return jax.shard_map(
        functools.partial(shards, mesh.shape["lat"], mesh.shape["lon"]),
        mesh=mesh,
        in_specs=(grid, grid) + (P(),) * 6,
        out_specs=(grid, P(None, None, ("lat", "lon")), P(None, ("lat", "lon"))),
        check_vma=False,
    )
```

```python
import functools
import math
import types

import jax
import jax.numpy as jnp
import numpy as np
from jax import lax
from jax.experimental import pallas as pl
from jax.experimental.pallas import tpu as pltpu
from jax.sharding import PartitionSpec as P

C = 192
HEADS = 6
HEAD = 32
FFN = 768
WT = 144
NT = 576
NR = 640
QT = 160
MAIN = 112
VECB = 124800
BROWS = HEADS * WT
MROWS = 2304
OROWS = 880
GROWS = MROWS + OROWS
LOG2E = math.log2(math.e)
MESH = pl.DeviceIdType.MESH
BF = jnp.bfloat16
F32 = jnp.float32
VMEM_LIMIT = 56 * 1024 * 1024


def nat(l, r, c):
    return l * 288 + r * 48 + c


def one_hot(sources, width):
    mat = np.zeros((len(sources), width), np.float32)
    for i, s in enumerate(sources):
        if s >= 0:
            mat[i, s] = 1.0
    return mat


@functools.cache
def orders():
    win = [nat(l, r, 12 * w + c) for w in range(4) for l in range(2) for r in range(6) for c in range(12)]

    def cells(rows, cols, size):
        out = [nat(l, r, c) for l in range(2) for r in rows for c in cols]
        return out + [-1] * (size - len(out))

    top, low = range(0, 3), range(3, 6)
    send = []
    for rows in (top, low):
        send += cells(rows, range(0, 18), MAIN)
        send += cells(rows, range(42, 48), QT - MAIN)
        send += cells(rows, range(24, 42), MAIN)
        send += cells(rows, range(18, 24), QT - MAIN)
    slots = []
    for s in range(4):
        for l in range(2):
            for half in range(2):
                for r in range(3):
                    for cc in range(12):
                        col = 12 * (s % 2) + cc
                        base = QT * (2 * (s // 2) + half)
                        if col >= 6:
                            slots.append(base + (l * 3 + r) * 18 + col - 6)
                        else:
                            slots.append(base + MAIN + (l * 3 + r) * 6 + col)
    win_at = {n: i for i, n in enumerate(win)}
    send_win = [win_at[n] if n >= 0 else -1 for n in send]
    to_win = one_hot(win, NT)
    send_from_win = one_hot(send_win, NT)
    send_from_nat = one_hot(send, NT)
    to_slots = one_hot(slots, NR)
    return {
        "to_win": to_win,
        "to_nat": to_win.T.copy(),
        "send_win": send_from_win,
        "win_send": send_from_win.T.copy(),
        "send_nat": send_from_nat,
        "to_slots": to_slots,
        "from_slots": to_slots.T.copy(),
    }


def const(name):
    return jnp.asarray(orders()[name], BF)


def nn(a, b):
    return lax.dot_general(a, b, (((1,), (0,)), ((), ())), preferred_element_type=F32)


def nt(a, b):
    return lax.dot_general(a, b, (((1,), (1,)), ((), ())), preferred_element_type=F32)


def tn(a, b):
    return lax.dot_general(a, b, (((0,), (0,)), ((), ())), preferred_element_type=F32)


def shuffle(mat, x):
    return nn(mat, x).astype(BF)


def stats(x):
    center = x - jnp.mean(x, axis=-1, keepdims=True)
    r = lax.rsqrt(jnp.mean(center * center, axis=-1, keepdims=True) + 1e-05)
    return center * r, r


def norm_back(dn, gain, xhat, r):
    t = dn * gain
    return r * (t - jnp.mean(t, axis=-1, keepdims=True) - xhat * jnp.mean(t * xhat, axis=-1, keepdims=True))


def head_mask(h, dtype):
    lane = lax.broadcasted_iota(jnp.int32, (1, C), 1)
    return ((lane >= h * HEAD) & (lane < (h + 1) * HEAD)).astype(F32).astype(dtype)


def forward_windows(t, b, bias_of, last):
    g0, g1 = t.gains[b, 0:1, :], t.gains[b, 1:2, :]

    def window(w, carry):
        rows = pl.ds(pl.multiple_of(w * WT, WT), WT)
        x = t.x[rows, :].astype(F32)
        u = (stats(x)[0] * g0).astype(BF)
        q = nn(u, t.wq[0]).astype(BF)
        k = nn(u, t.wq[1]).astype(BF)
        v = nn(u, t.wq[2]).astype(BF)
        t.q[rows, :] = q
        t.k[rows, :] = k
        t.v[rows, :] = v
        mixed = jnp.zeros((WT, C), F32)
        for h in range(HEADS):
            s = nt(q * head_mask(h, BF), k) * (HEAD ** -0.5 * LOG2E) + bias_of(w, h)
            e = jnp.exp2(s - jnp.max(s, axis=-1, keepdims=True))
            p = (e * (1.0 / jnp.sum(e, axis=-1, keepdims=True))).astype(BF)
            t.p[pl.ds(pl.multiple_of(w * BROWS + h * WT, WT), WT), :] = p
            mixed = mixed + nn(p, v) * head_mask(h, F32)
        mixed = mixed.astype(BF)
        t.mix[rows, :] = mixed
        attended = nn(mixed, t.w_proj[b]).astype(BF)
        hidden = x + attended.astype(F32)
        t.hid[rows, :] = hidden
        n2 = (stats(hidden)[0] * g1).astype(BF)
        total = hidden
        for j in range(3):
            cols = slice(256 * j, 256 * j + 256)
            up = nn(n2, t.w_up[b, :, cols])
            cdf = 0.5 + 0.5 * lax.erf(up * (0.5 ** 0.5))
            slope = cdf + up * jnp.exp2(up * up * (-0.5 * LOG2E)) * (1.0 / math.sqrt(2 * math.pi))
            act = (up * cdf).astype(BF)
            t.a[rows, cols] = act
            t.gp[rows, cols] = slope.astype(BF)
            if not last:
                total = total + nt(act, t.w_down[b, :, cols])
        if not last:
            t.out[rows, :] = total.astype(BF)
        return carry

    lax.fori_loop(0, 4, window, 0, unroll=2)


def pairs(window, after_first=None):
    def body(i, carry):
        window(2 * i)
        window(2 * i + 1)
        if after_first is not None:
            pl.when(i == 0)(after_first)
        return carry

    lax.fori_loop(0, 2, body, 0)


def backward_feed(t, b):
    g1 = t.gains[b, 1:2, :]
    t.dg[...] = jnp.zeros((2, C), F32)

    def window(w):
        rows = pl.ds(pl.multiple_of(w * WT, WT), WT)
        dy = t.dout[rows, :]
        dn2 = jnp.zeros((WT, C), F32)
        for j in range(3):
            cols = slice(256 * j, 256 * j + 256)
            da = nn(dy, t.w_down[b, :, cols]).astype(BF).astype(F32)
            dup = (da * t.gp[rows, cols].astype(F32)).astype(BF)
            t.dup[rows, cols] = dup
            dn2 = dn2 + nt(dup, t.w_up[b, :, cols])
        dn2 = dn2.astype(BF).astype(F32)
        xhat, r = stats(t.hid[rows, :])
        t.n2[rows, :] = (xhat * g1).astype(BF)
        t.dg[1:2, :] += jnp.sum(dn2 * xhat, axis=0, keepdims=True)
        t.datt[rows, :] = (dy.astype(F32) + norm_back(dn2, g1, xhat, r)).astype(BF)

    pairs(window)


def backward_attention(t, b, dbias_of, after_first):
    g0 = t.gains[b, 0:1, :]

    def window(w):
        rows = pl.ds(pl.multiple_of(w * WT, WT), WT)
        datt = t.datt[rows, :]
        dmix = nt(datt, t.w_proj[b]).astype(BF)
        q = t.q[rows, :]
        k = t.k[rows, :]
        v = t.v[rows, :]
        doms = jnp.concatenate([dmix * head_mask(h, BF) for h in range(HEADS)], axis=0)
        qms = jnp.concatenate([q * head_mask(h, BF) for h in range(HEADS)], axis=0)
        dps = nt(doms, v)
        pw = t.p[pl.ds(pl.multiple_of(w * BROWS, WT), BROWS), :]
        dss = []
        for h in range(HEADS):
            part = slice(h * WT, h * WT + WT)
            p = pw[part].astype(F32)
            pd = p * dps[part]
            ds = pd - p * jnp.sum(pd, axis=-1, keepdims=True)
            dbias_of(w, h, ds)
            dss.append(ds.astype(BF))
        dss = jnp.concatenate(dss, axis=0)
        dqs = nn(dss, k)
        dq = dqs[0:WT] * head_mask(0, F32)
        for h in range(1, HEADS):
            dq = dq + dqs[h * WT:h * WT + WT] * head_mask(h, F32)
        dq = (dq * HEAD ** -0.5).astype(BF)
        dk = (tn(dss, qms) * HEAD ** -0.5).astype(BF)
        dv = tn(pw, doms).astype(BF)
        t.dq[rows, :] = dq
        t.dk[rows, :] = dk
        t.dv[rows, :] = dv
        du = nt(dq, t.wq[0]) + nt(dk, t.wq[1]) + nt(dv, t.wq[2])
        du = du.astype(BF).astype(F32)
        xhat, r = stats(t.x[rows, :].astype(F32))
        t.u[rows, :] = (xhat * g0).astype(BF)
        t.dg[0:1, :] += jnp.sum(du * xhat, axis=0, keepdims=True)
        dx = norm_back(du, g0, xhat, r).astype(BF).astype(F32) + datt.astype(F32)
        t.dx[rows, :] = dx.astype(BF)

    pairs(window, after_first)


def product_left(lhs, x):
    return tn(lhs, jnp.concatenate([x, jnp.zeros((NT, 64), BF)], axis=1))


def product_right(lhs, x):
    return tn(lhs, jnp.concatenate([jnp.zeros((NT, 64), BF), x], axis=1))


def products_early(t):
    n2, dout = t.n2[...], t.dout[...]
    down_low = product_right(t.a[:, 0:384], dout)
    up_high = product_right(t.dup[:, 384:768], n2)
    for i, right in enumerate((up_high[0:192], up_high[192:384], down_low[0:192])):
        t.part[0, 192 * i:192 * i + 192, 128:384] = right.astype(BF)
    down_high = product_right(t.a[:, 384:768], dout)
    up_low = product_left(t.dup[:, 0:384], n2)
    proj = product_left(t.datt[...], t.mix[...])
    for i, (left, right) in enumerate(((proj, down_low[192:384]), (up_low[0:192], down_high[0:192]), (up_low[192:384], down_high[192:384]))):
        rows = slice(192 * i, 192 * i + 192)
        t.part[1, rows, 0:128] = left[:, 0:128].astype(BF)
        t.part[1, rows, 128:256] = (left[:, 128:256] + right[:, 0:128]).astype(BF)
        t.part[1, rows, 256:384] = right[:, 128:256].astype(BF)


def products_late(t):
    u = t.u[...]
    for i, ref in enumerate((t.dq, t.dk, t.dv)):
        rows = slice(192 * i, 192 * i + 192)
        left = product_left(ref[...], u)
        t.part[0, rows, 0:128] = left[:, 0:128].astype(BF)
        t.part[0, rows, 128:256] = (left[:, 128:256] + t.part[0, rows, 128:256].astype(F32)).astype(BF)


def other_rows(t):
    flat = jnp.concatenate([t.dg[0:1, :], t.dg[1:2, :], jnp.zeros((1, 3 * WT - 2 * C), F32)], axis=1)
    t.db[BROWS:OROWS, :] = jnp.concatenate([flat[:, 0:WT], flat[:, WT:2 * WT], flat[:, 2 * WT:3 * WT], jnp.zeros((OROWS - BROWS - 3, WT), F32)], axis=0)
    gap = jnp.zeros((240, 48), F32)
    for core in range(2):
        lft = t.db[lat_row(core):lat_row(core) + 240, :]
        rgt = t.db[lat_row(2 + core):lat_row(2 + core) + 240, :]
        t.part[core, 576:816, :] = jnp.concatenate([lft, gap, rgt, gap], axis=1).astype(BF)


def half_of(shape, axis):
    return (lax.broadcasted_iota(jnp.int32, shape, axis) // 36) % 2


def lane_moves(low):
    src = lax.broadcasted_iota(jnp.int32, (WT, WT), 0)
    dst = lax.broadcasted_iota(jnp.int32, (WT, WT), 1)
    keep = dst - 36 * ((dst // 36) % 2) + (0 if low else 36)
    return (src == keep).astype(F32)


def polar_bias(table, low):
    moved = jnp.dot(table, lane_moves(low), precision=lax.Precision.HIGHEST, preferred_element_type=F32)
    half = half_of((WT, WT), 0)
    if low:
        moved = jnp.where(half == 0, moved, pltpu.roll(moved, 36, 0))
    else:
        moved = jnp.where(half == 1, moved, pltpu.roll(moved, WT - 36, 0))
    return jnp.where(half == half_of((WT, WT), 1), moved, -1e30)


def polar_back(grad, low):
    half = half_of((WT, WT), 0)
    if low:
        folded = jnp.where(half == 0, grad + pltpu.roll(grad, WT - 36, 0), 0.0)
    else:
        folded = jnp.where(half == 1, grad + pltpu.roll(grad, 36, 0), 0.0)
    return lax.dot_general(folded, lane_moves(low), (((1,), (1,)), ((), ())), precision=lax.Precision.HIGHEST, preferred_element_type=F32)


def greet(peers):
    barrier = pltpu.get_barrier_semaphore()
    for cond, dev in peers:
        if cond is None:
            pl.semaphore_signal(barrier, inc=1, device_id=dev, device_id_type=MESH)
        else:
            @pl.when(cond)
            def _():
                pl.semaphore_signal(barrier, inc=1, device_id=dev, device_id_type=MESH)


def guarded(cond, act):
    if cond is None:
        act()
    else:
        pl.when(cond)(act)


class Exchange:
    def __init__(self, moves, src, dst, send_sem, recv_sem, base, here):
        self.sends, self.locals, self.recvs = moves
        self.src, self.dst, self.send_sem, self.recv_sem, self.base, self.here = src, dst, send_sem, recv_sem, base, here

    def remote(self, i, s, d, size, dev):
        return pltpu.make_async_remote_copy(
            src_ref=self.src.at[pl.ds(s, size), :], dst_ref=self.dst.at[pl.ds(d, size), :], send_sem=self.send_sem.at[self.base + i],
            recv_sem=self.recv_sem.at[self.base + i], device_id=dev, device_id_type=MESH)

    def start(self):
        for i, cond, s, d, size, dev in self.sends:
            guarded(cond, lambda: self.remote(i, s, d, size, dev).start())
        for cond, s, d, size in self.locals:
            def keep():
                self.dst[d:d + size, :] = self.src[s:s + size, :]
            guarded(cond, keep)

    def finish(self):
        for i, cond, d, size in self.recvs:
            guarded(cond, lambda: self.remote(i, 0, d, size, self.here).wait_recv())
        for i, cond, s, d, size, dev in self.sends:
            guarded(cond, lambda: self.remote(i, s, d, size, dev).wait_send())


def moves_out(n):
    sends = [
        (0, None, 432, 432, 48, (n.b, n.east)),
        (1, n.inner_up, 112, 592, 48, (n.up, n.east)),
        (2, n.first, 112, 112, 48, (n.b, n.east)),
        (3, n.inner_up, 0, 480, 112, (n.up, n.j)),
        (4, n.inner_down, 480, 0, 160, (n.down, n.j)),
    ]
    locals_ = [(None, 160, 160, 272), (n.first, 0, 0, 112), (n.last, 480, 480, 160)]
    recvs = [(0, None, 432, 48), (1, n.inner_down, 592, 48), (2, n.first, 112, 48), (3, n.inner_down, 480, 112), (4, n.inner_up, 0, 160)]
    return sends, locals_, recvs


def moves_back(n):
    sends = [
        (0, None, 432, 432, 48, (n.b, n.west)),
        (1, n.inner_down, 592, 112, 48, (n.down, n.west)),
        (2, n.first, 112, 112, 48, (n.b, n.west)),
        (3, n.inner_down, 480, 0, 112, (n.down, n.j)),
        (4, n.inner_up, 0, 480, 160, (n.up, n.j)),
    ]
    locals_ = [(None, 160, 160, 272), (n.first, 0, 0, 112), (n.last, 480, 480, 160)]
    recvs = [(0, None, 432, 48), (1, n.inner_up, 112, 48), (2, n.first, 112, 48), (3, n.inner_up, 0, 112), (4, n.inner_down, 480, 160)]
    return sends, locals_, recvs


def lat_row(lat):
    return ((650 * lat) // 48) * 16


def z_row(core, z):
    return ((52 * core + 325 * z) // 96) * 16


def x_row(core, z, x):
    return ((208 * core + 1300 * z + 325 * x) // 384) * 16


def al(v):
    return pl.multiple_of(v, 16)


def total(*terms):
    out = terms[0].astype(F32)
    for term in terms[1:]:
        out = out + term.astype(F32)
    return out


class Reduce:
    def __init__(self, n, t, send_sem, recv_sem, base):
        self.n, self.t, self.send_sem, self.recv_sem, self.base = n, t, send_sem, recv_sem, base

    def remote(self, i, s, d, dev):
        i = self.base + i
        return pltpu.make_async_remote_copy(src_ref=s, dst_ref=d, send_sem=self.send_sem.at[i], recv_sem=self.recv_sem.at[i], device_id=dev, device_id_type=MESH)

    def core_copies(self):
        n, t = self.n, self.t
        pal = n.device(core=1 - n.core)
        return (
            self.remote(0, t.part.at[1, pl.ds(0, 576), :], t.got_core.at[pl.ds(0, 576), :], pal),
            self.remote(1, t.part.at[0, pl.ds(0, 576), pl.ds(256, 128)], t.got_core.at[pl.ds(0, 576), pl.ds(256, 128)], pal),
            self.remote(2, t.part.at[1 - n.core, pl.ds(576, 240), :], t.got_core.at[pl.ds(576, 240), :], pal),
            self.remote(3, t.part.at[0, pl.ds(0, 576), pl.ds(0, 256)], t.got_core.at[pl.ds(0, 576), pl.ds(0, 256)], pal),
        )

    def first_copies(self):
        n, t = self.n, self.t
        tile2, tiles01, other = [], [], []
        for d in range(1, 4):
            i = 4 * d
            z = (n.z + d) % 4
            x = (n.x + d) % 4
            to_x, to_z = n.device(x=x), n.device(z=z)
            rows = pl.ds(al(32 * x), 48)
            tile2.append(self.remote(i, t.sum_m.at[:, rows, pl.ds(256, 128)], t.got_x.at[d - 1, :, :, pl.ds(128, 128)], to_x))
            tiles01.append(self.remote(i + 1, t.sum_m.at[:, rows, pl.ds(128, 128)], t.got_x.at[d - 1, :, :, pl.ds(0, 128)], to_x))
            tiles01.append(self.remote(i + 2, t.sum_m.at[z, :, pl.ds(0, 128)], t.got_z.at[d - 1], to_z))
            other.append(self.remote(i + 3, t.sum_o.at[pl.ds(al(z_row(n.core, z)), 80), :], t.got_o.at[d - 1], to_z))
        return tile2, tiles01, other

    def x_window(self, x):
        return al(x_row(self.n.core, self.n.z, x) - z_row(self.n.core, self.n.z))

    def second_copies(self):
        n, t = self.n, self.t
        out = []
        for d in range(1, 4):
            i = 3 * d + 13
            z = (n.z + d) % 4
            x = (n.x + d) % 4
            out.append(self.remote(i, t.sum_x.at[z], t.got_xz.at[d - 1], n.device(z=z)))
            dev = n.device(x=x)
            out.append(self.remote(i + 1, t.sum_zo.at[pl.ds(self.x_window(x), 32), :], t.got_ox.at[d - 1], dev))
            out.append(self.remote(i + 2, t.sum_z.at[pl.ds(al(32 * x), 48), :], t.got_zx.at[d - 1], dev))
        return out

    def third_copies(self):
        n, t = self.n, self.t
        devices = [n.device(yl=1 - n.yl), n.device(yh=1 - n.yh), n.device(yl=1 - n.yl, yh=1 - n.yh)]
        return [self.remote(25 + i, t.mid, t.got_y.at[i], dev) for i, dev in enumerate(devices)]

    def start(self, copies):
        for c in copies:
            c.start()

    def wait(self, copies):
        for c in copies:
            c.wait()

    def early_start(self):
        both = self.core_copies()
        for core in range(2):
            pl.when(self.n.core == core)(both[core].start)

    def early_to_first(self):
        n, t = self.n, self.t
        copies = self.core_copies()
        tile2, tiles01, _ = self.first_copies()

        @pl.when(n.core == 0)
        def _():
            copies[1].wait_recv()
            for z in range(4):
                rows = slice(144 * z, 144 * z + 144)
                t.sum_m[z, :, 256:384] = total(t.part[0, rows, 256:384], t.got_core[rows, 256:384]).astype(BF)
            self.start(tile2)
            copies[0].wait_send()

        @pl.when(n.core == 1)
        def _():
            copies[0].wait_recv()
            for z in range(4):
                rows = slice(144 * z, 144 * z + 144)
                t.sum_m[z] = total(t.part[1, rows, :], t.got_core[rows, :]).astype(BF)
            self.start(tile2 + tiles01)
            copies[1].wait_send()

    def late_start(self):
        copies = self.core_copies()
        pl.when(self.n.core == 1)(copies[3].start)
        copies[2].start()

    def late_to_first(self):
        n, t = self.n, self.t
        copies = self.core_copies()
        _, tiles01, other = self.first_copies()

        @pl.when(n.core == 0)
        def _():
            copies[3].wait_recv()
            for z in range(4):
                rows = slice(144 * z, 144 * z + 144)
                t.sum_m[z, :, 0:256] = total(t.part[0, rows, 0:256], t.got_core[rows, 0:256]).astype(BF)
            self.start(tiles01)

        copies[2].wait_recv()
        t.sum_o[...] = total(t.part[n.core, 576:816, :], t.got_core[576:816, :]).astype(BF)
        self.start(other)
        copies[2].wait_send()
        pl.when(n.core == 1)(copies[3].wait_send)

    def first_to_second(self):
        n, t = self.n, self.t
        for copies in self.first_copies():
            self.wait(copies)
        t.sum_x[...] = total(t.sum_m[:, pl.ds(al(32 * n.x), 48), 128:384], *[t.got_x[i] for i in range(3)]).astype(BF)
        t.sum_zo[...] = total(t.sum_o[pl.ds(al(z_row(n.core, n.z)), 80), :], *[t.got_o[i] for i in range(3)]).astype(BF)
        t.sum_z[...] = total(t.sum_m[n.z, :, 0:128], *[t.got_z[i] for i in range(3)]).astype(BF)
        self.start(self.second_copies())

    def second_to_third(self):
        n, t = self.n, self.t
        self.wait(self.second_copies())
        t.mid[0:48, 0:128] = total(t.sum_z[pl.ds(al(32 * n.x), 48), :], *[t.got_zx[i] for i in range(3)]).astype(BF)
        t.mid[0:48, 128:384] = total(t.sum_x[n.z], *[t.got_xz[i] for i in range(3)]).astype(BF)
        t.mid[48:80, :] = total(t.sum_zo[pl.ds(self.x_window(n.x), 32), :], *[t.got_ox[i] for i in range(3)]).astype(BF)
        self.start(self.third_copies())

    def finish(self):
        self.wait(self.third_copies())
        return total(self.t.mid[...], *[self.t.got_y[i] for i in range(3)])


def group_squares(n, final):
    matrix, other = final[0:48, :], final[48:80, :]
    row = lax.broadcasted_iota(jnp.int32, (48, 384), 0)
    low = 4 * n.x
    squares = jnp.sum(jnp.where((row >= low) & (row < low + 36), matrix * matrix, 0.0), axis=0, keepdims=True)
    lane = lax.broadcasted_iota(jnp.int32, (32, 384), 1)
    row = lax.broadcasted_iota(jnp.int32, (32, 384), 0) + x_row(n.core, n.z, n.x)
    for yh in range(2):
        lat = 2 * yh + n.core
        at = lane - C * yh
        index = (row + lat_row(lat)) * WT + at
        low = 975 * (32 * lat + 8 * n.z + 2 * n.x)
        inside = (index >= low) & (index < low + 1950) & (at >= 0) & (at < WT)
        squares = squares + jnp.sum(jnp.where(inside, other * other, 0.0), axis=0, keepdims=True)
    return jnp.sum(squares, axis=1, keepdims=True)


def own_lanes(n, final):
    return jnp.where(n.yh == 1, pltpu.roll(final, C, 1), final)[:, 0:256]


INPUTS = ["tok", "cot", "gains", "w_qkv", "w_proj", "w_up", "w_down", "bias", "to_win", "to_nat", "send_win", "win_send", "send_nat", "to_slots", "from_slots"]
PERMS = INPUTS[8:]
OUTPUTS = [("gtok", (NT, C), BF), ("m", (18, 2, C), F32), ("o", (2, 975), F32)]
COPIED = ["to_win", "tok", "w_qkv", "bias", "w_proj", "w_up", "w_down", "send_win", "send_nat", "cot", "to_slots", "from_slots", "win_send", "to_nat"]
SHAPES = {
    "tok": (NT, C), "cot": (NT, C), "w_qkv": (2, C, 3 * C), "w_proj": (2, C, C), "w_up": (2, C, FFN), "w_down": (2, C, FFN), "bias": (2, BROWS, WT),
    "to_win": (NT, NT), "to_nat": (NT, NT), "send_win": (NR, NT), "win_send": (NT, NR), "send_nat": (NR, NT), "to_slots": (NT, NR), "from_slots": (NR, NT),
}
BLOCK = [
    ("x", (NT, C), BF), ("wq", (3, C, C), BF), ("q", (NT, C), BF), ("k", (NT, C), BF), ("v", (NT, C), BF), ("p", (4 * BROWS, WT), BF),
    ("mix", (NT, C), BF), ("hid", (NT, C), F32), ("a", (NT, FFN), BF), ("gp", (NT, FFN), BF), ("dout", (NT, C), BF), ("part", (2, 816, 384), BF),
    ("got_core", (816, 384), BF), ("sum_m", (4, 144, 384), BF), ("sum_o", (240, 384), BF),
    ("got_x", (3, 4, 48, 256), BF), ("got_o", (3, 80, 384), BF), ("got_z", (3, 144, 128), BF),
    ("sum_x", (4, 48, 256), BF), ("sum_zo", (80, 384), BF), ("sum_z", (144, 128), BF),
    ("got_xz", (3, 48, 256), BF), ("got_ox", (3, 32, 384), BF), ("got_zx", (3, 48, 128), BF),
    ("mid", (80, 384), BF), ("got_y", (3, 80, 384), BF),
    ("db", (OROWS, WT), F32), ("dg", (2, C), F32),
]
SHARED = [
    ("out", (NT, C), BF), ("dx", (NT, C), BF), ("u", (NT, C), BF), ("n2", (NT, C), BF), ("datt", (NT, C), BF), ("dq", (NT, C), BF), ("dk", (NT, C), BF),
    ("dv", (NT, C), BF), ("dup", (NT, FFN), BF),
    ("lbias", (3, BROWS, WT), F32), ("db_pair", (2, BROWS, WT), F32), ("parts", (32, 1, 128), F32), ("own", (2, 80, 256), F32),
    ("cot_src", (NR, 256), BF), ("cot_dst", (NR, 256), BF), ("mid_src", (NR, 256), BF), ("mid_dst", (NR, 256), BF), ("back_src", (NR, 256), BF), ("back_dst", (NR, 256), BF),
]
SEMS = 15 + 56 + 31


def place(nlat, nlon):
    n = types.SimpleNamespace()
    n.b, n.j = lax.axis_index("lat"), lax.axis_index("lon")
    n.east, n.west = lax.rem(n.j + 1, nlon), lax.rem(n.j + nlon - 1, nlon)
    n.up, n.down = jnp.maximum(n.b - 1, 0), jnp.minimum(n.b + 1, nlat - 1)
    n.first, n.last = n.b == 0, n.b == nlat - 1
    n.inner_up, n.inner_down = n.b > 0, n.b < nlat - 1
    n.yh, n.core = n.b // 2, n.b % 2
    n.z, n.x, n.yl = n.j // 8, (n.j // 2) % 4, n.j % 2

    def device(yh=n.yh, core=n.core, z=n.z, x=n.x, yl=n.yl):
        return (yh * 2 + core, z * 8 + x * 2 + yl)

    n.device = device
    return n


def kernel(nlat, nlon, reduce, *refs):
    names = INPUTS + [o[0] for o in OUTPUTS] + ["first_" + e[0] for e in BLOCK] + ["second_" + e[0] for e in BLOCK] + [e[0] for e in SHARED] + ["in_" + k for k in COPIED] + ["send_sem", "recv_sem", "in_sem"]
    r = dict(zip(names, refs, strict=True))
    loads = {k: pltpu.make_async_copy(r[k], r["in_" + k], r["in_sem"].at[i]) for i, k in enumerate(COPIED)}
    for copy in loads.values():
        copy.start()

    def need(*keys):
        for k in keys:
            loads[k].wait()

    weights = {k: r["in_" + k] if k in COPIED else r[k] for k in INPUTS}
    blocks = []
    for label in ("first_", "second_"):
        blocks.append(types.SimpleNamespace(**weights, **{e[0]: r[e[0]] for e in SHARED}, **{e[0]: r[label + e[0]] for e in BLOCK}))
    one, two = blocks
    n = place(nlat, nlon)
    sems = (r["send_sem"], r["recv_sem"])
    here = (n.b, n.j)
    ex_cot = Exchange(moves_out(n), one.cot_src, one.cot_dst, *sems, 0, here)
    ex_mid = Exchange(moves_out(n), one.mid_src, one.mid_dst, *sems, 5, here)
    ex_back = Exchange(moves_back(n), one.back_src, one.back_dst, *sems, 10, here)

    level = [(e, dz, dx) for e in range(2) for dz in range(4) for dx in range(4) if (e, dz, dx) != (0, 0, 0)]
    level_dev = [n.device(core=(n.core + e) % 2, z=(n.z + dz) % 4, x=(n.x + dx) % 4) for e, dz, dx in level]
    y_dev = [n.device(yl=1 - n.yl), n.device(yh=1 - n.yh), n.device(yl=1 - n.yl, yh=1 - n.yh)]
    far = level_dev + y_dev if reduce else []
    greet(
        [(None, (n.b, n.east)), (None, (n.b, n.west)), (n.inner_up, (n.up, n.j)), (n.inner_down, (n.down, n.j)), (n.inner_up, (n.up, n.east)), (n.inner_down, (n.down, n.west))]
        + [(None, d) for d in far]
    )

    need("to_win", "tok")
    one.x[...] = shuffle(one.to_win[...], one.tok[...])
    need("w_qkv")
    for b, t in enumerate(blocks):
        for i in range(3):
            t.wq[i] = t.w_qkv[b, :, C * i:C * i + C]
    need("bias")
    one.lbias[0] = one.bias[0] * LOG2E
    need("w_proj", "w_up", "w_down")
    forward_windows(one, 0, lambda w, h: one.lbias[0, h * WT:h * WT + WT, :], False)
    need("send_win")
    one.mid_src[:, 0:C] = shuffle(one.send_win[...], one.out[...])
    pl.semaphore_wait(pltpu.get_barrier_semaphore(), jnp.where(jnp.logical_or(n.first, n.last), 4, 6) + len(far))
    ex_mid.start()
    need("send_nat", "cot")
    one.cot_src[:, 0:C] = shuffle(one.send_nat[...], one.cot[...])
    ex_cot.start()
    need("to_slots", "from_slots", "win_send", "to_nat")

    for group in range(2):
        polar = n.first if group == 0 else n.last

        @pl.when(polar)
        def _():
            for h in range(HEADS):
                rows = slice(h * WT, h * WT + WT)
                two.lbias[1 + group, rows, :] = polar_bias(two.bias[1, rows, :] * LOG2E, group == 1)

        @pl.when(jnp.logical_not(polar))
        def _():
            two.lbias[1 + group] = two.bias[1] * LOG2E

    two.db_pair[...] = jnp.zeros((2, BROWS, WT), F32)
    ex_mid.finish()
    two.x[...] = shuffle(two.to_slots[...], two.mid_dst[:, 0:C])
    forward_windows(two, 1, lambda w, h: two.lbias[1 + w // 2, h * WT:h * WT + WT, :], True)

    def dbias_two(w, h, ds):
        two.db_pair[w // 2, h * WT:h * WT + WT, :] += ds

    ex_cot.finish()
    two.dout[...] = shuffle(two.to_slots[...], two.cot_dst[:, 0:C])
    red_one = Reduce(n, one, *sems, 15)
    red_two = Reduce(n, two, *sems, 43)

    def only_reducing(act):
        if reduce:
            act()

    backward_feed(two, 1)
    products_early(two)
    only_reducing(red_two.early_start)
    backward_attention(two, 1, dbias_two, red_two.early_to_first if reduce else None)
    two.back_src[:, 0:C] = shuffle(two.from_slots[...], two.dx[...])
    ex_back.start()
    for group in range(2):
        @pl.when(n.first if group == 0 else n.last)
        def _():
            for h in range(HEADS):
                rows = slice(h * WT, h * WT + WT)
                two.db_pair[group, rows, :] = polar_back(two.db_pair[group, rows, :], group == 1)

    two.db[0:BROWS, :] = two.db_pair[0] + two.db_pair[1]
    products_late(two)
    other_rows(two)
    only_reducing(red_two.late_start)

    ex_back.finish()
    only_reducing(red_two.late_to_first)
    one.dout[...] = shuffle(one.win_send[...], one.back_dst[:, 0:C])
    one.db[...] = jnp.zeros((OROWS, WT), F32)

    def dbias_one(w, h, ds):
        one.db[h * WT:h * WT + WT, :] += ds

    backward_feed(one, 0)
    products_early(one)
    only_reducing(red_one.early_start)
    backward_attention(one, 0, dbias_one, red_one.early_to_first if reduce else None)
    products_late(one)
    other_rows(one)
    only_reducing(red_one.late_start)
    r["gtok"][...] = shuffle(one.to_nat[...], one.dx[...])
    if not reduce:
        return
    red_two.first_to_second()
    red_one.late_to_first()
    red_two.second_to_third()
    two_final = red_two.finish()
    squares = group_squares(n, two_final)
    red_one.first_to_second()
    red_one.second_to_third()
    one_final = red_one.finish()

    parts = one.parts
    parts[0] = jnp.broadcast_to(squares + group_squares(n, one_final), (1, 128))
    copies = [
        pltpu.make_async_remote_copy(src_ref=parts.at[0], dst_ref=parts.at[1 + i], send_sem=sems[0].at[71 + i], recv_sem=sems[1].at[71 + i], device_id=d, device_id_type=MESH)
        for i, d in enumerate(level_dev)
    ]
    for c in copies:
        c.start()
    for c in copies:
        c.wait()
    acc = parts[0]
    for i in range(len(copies)):
        acc = acc + parts[1 + i]
    ceiling = math.sqrt(24 * C * C + 2 * VECB)
    factor = jnp.minimum(1.0, ceiling / (jnp.sqrt(acc) + 1e-06))[0:1, 0:1]
    first_row = 4 * n.x + 18 * n.yl
    start = 975 * (32 * n.b + n.j) - (lat_row(n.b) + x_row(n.core, n.z, n.x)) * WT
    rows = []
    for b, final in enumerate((one_final, two_final)):
        one.own[b] = own_lanes(n, final) * factor
        for i in range(18):
            r["m"][i, b:b + 1, :] = one.own[b, pl.ds(first_row + i, 1), 0:C]
        rows.append(jnp.concatenate([one.own[b, pl.ds(48 + start // WT + i, 1), 0:WT] for i in range(8)], axis=1))
    flat = jnp.concatenate(rows + [jnp.zeros((6, 8 * WT), F32)], axis=0)
    r["o"][...] = pltpu.roll(flat, 8 * WT - start % WT, 1)[0:2, 0:975]


def run(nlat, nlon, reduce, tokens, cotangent, norm_gains, w_qkv, w_proj, w_up, w_down, pos_bias):
    args = [tokens.reshape(NT, C), cotangent.reshape(NT, C), norm_gains, w_qkv, w_proj, w_up, jnp.swapaxes(w_down, 1, 2), pos_bias.reshape(2, BROWS, WT)]
    args += [const(p) for p in PERMS]
    vmem = pl.BlockSpec(memory_space=pltpu.VMEM)
    anywhere = pl.BlockSpec(memory_space=pl.ANY)
    return pl.pallas_call(
        functools.partial(kernel, nlat, nlon, reduce),
        in_specs=[anywhere if k in COPIED else vmem for k in INPUTS],
        out_specs=[vmem] * len(OUTPUTS),
        out_shape=[jax.ShapeDtypeStruct(s, d) for _, s, d in OUTPUTS],
        scratch_shapes=[pltpu.VMEM(s, d) for _, s, d in BLOCK + BLOCK + SHARED] + [pltpu.VMEM(SHAPES[k], F32 if k == "bias" else BF) for k in COPIED]
        + [pltpu.SemaphoreType.DMA((SEMS,))] * 2 + [pltpu.SemaphoreType.DMA((len(COPIED),))],
        compiler_params=pltpu.CompilerParams(vmem_limit_bytes=VMEM_LIMIT, collective_id=1, has_side_effects=True),
        name="two_blocks",
    )(*args)


def copy_out(*refs):
    k = len(OUTPUTS)
    sem = refs[3 * k]
    loads = [pltpu.make_async_copy(refs[i], refs[2 * k + i], sem.at[i]) for i in range(k)]
    stores = [pltpu.make_async_copy(refs[2 * k + i], refs[k + i], sem.at[k + i]) for i in range(k)]
    for c in loads:
        c.start()
    for c, d in zip(loads[::-1], stores[::-1]):
        c.wait()
        d.start()
    for d in stores:
        d.wait()


def run_copy_out(results):
    anywhere = pl.BlockSpec(memory_space=pl.ANY)
    return pl.pallas_call(
        copy_out,
        in_specs=[anywhere] * len(results),
        out_specs=[anywhere] * len(results),
        out_shape=[jax.ShapeDtypeStruct(s, d) for _, s, d in OUTPUTS],
        scratch_shapes=[pltpu.VMEM(s, d) for _, s, d in OUTPUTS] + [pltpu.SemaphoreType.DMA((2 * len(OUTPUTS),))],
        name="copy_out",
    )(*results)


def shards(nlat, nlon, tokens, *args):
    gtok, m, o = run_copy_out(run(nlat, nlon, True, tokens, *args))
    return gtok.reshape(tokens.shape), m.transpose(1, 2, 0), o


def solution(mesh):
    grid = P(None, "lat", "lon", None)
    return jax.shard_map(
        functools.partial(shards, mesh.shape["lat"], mesh.shape["lon"]),
        mesh=mesh,
        in_specs=(grid, grid) + (P(),) * 6,
        out_specs=(grid, P(None, None, ("lat", "lon")), P(None, ("lat", "lon"))),
        check_vma=False,
    )
```

```python
import functools
import math
import types

import jax
import jax.numpy as jnp
import numpy as np
from jax import lax
from jax.experimental import pallas as pl
from jax.experimental.pallas import tpu as pltpu
from jax.sharding import PartitionSpec as P

C = 192
HEADS = 6
HEAD = 32
FFN = 768
WT = 144
NT = 576
NR = 640
QT = 160
MAIN = 112
VECB = 124800
BROWS = HEADS * WT
MROWS = 2304
OROWS = 880
GROWS = MROWS + OROWS
LOG2E = math.log2(math.e)
MESH = pl.DeviceIdType.MESH
BF = jnp.bfloat16
F32 = jnp.float32
VMEM_LIMIT = 56 * 1024 * 1024


def nat(l, r, c):
    return l * 288 + r * 48 + c


def one_hot(sources, width):
    mat = np.zeros((len(sources), width), np.float32)
    for i, s in enumerate(sources):
        if s >= 0:
            mat[i, s] = 1.0
    return mat


@functools.cache
def orders():
    win = [nat(l, r, 12 * w + c) for w in range(4) for l in range(2) for r in range(6) for c in range(12)]

    def cells(rows, cols, size):
        out = [nat(l, r, c) for l in range(2) for r in rows for c in cols]
        return out + [-1] * (size - len(out))

    top, low = range(0, 3), range(3, 6)
    send = []
    for rows in (top, low):
        send += cells(rows, range(0, 18), MAIN)
        send += cells(rows, range(42, 48), QT - MAIN)
        send += cells(rows, range(24, 42), MAIN)
        send += cells(rows, range(18, 24), QT - MAIN)
    slots = []
    for s in range(4):
        for l in range(2):
            for half in range(2):
                for r in range(3):
                    for cc in range(12):
                        col = 12 * (s % 2) + cc
                        base = QT * (2 * (s // 2) + half)
                        if col >= 6:
                            slots.append(base + (l * 3 + r) * 18 + col - 6)
                        else:
                            slots.append(base + MAIN + (l * 3 + r) * 6 + col)
    win_at = {n: i for i, n in enumerate(win)}
    send_win = [win_at[n] if n >= 0 else -1 for n in send]
    to_win = one_hot(win, NT)
    send_from_win = one_hot(send_win, NT)
    send_from_nat = one_hot(send, NT)
    to_slots = one_hot(slots, NR)
    return {
        "to_win": to_win,
        "to_nat": to_win.T.copy(),
        "send_win": send_from_win,
        "win_send": send_from_win.T.copy(),
        "send_nat": send_from_nat,
        "to_slots": to_slots,
        "from_slots": to_slots.T.copy(),
    }


def const(name):
    return jnp.asarray(orders()[name], BF)


def nn(a, b):
    return lax.dot_general(a, b, (((1,), (0,)), ((), ())), preferred_element_type=F32)


def nt(a, b):
    return lax.dot_general(a, b, (((1,), (1,)), ((), ())), preferred_element_type=F32)


def tn(a, b):
    return lax.dot_general(a, b, (((0,), (0,)), ((), ())), preferred_element_type=F32)


def shuffle(mat, x):
    return nn(mat, x).astype(BF)


def stats(x):
    center = x - jnp.mean(x, axis=-1, keepdims=True)
    r = lax.rsqrt(jnp.mean(center * center, axis=-1, keepdims=True) + 1e-05)
    return center * r, r


def norm_back(dn, gain, xhat, r):
    t = dn * gain
    return r * (t - jnp.mean(t, axis=-1, keepdims=True) - xhat * jnp.mean(t * xhat, axis=-1, keepdims=True))


def head_mask(h, dtype):
    lane = lax.broadcasted_iota(jnp.int32, (1, C), 1)
    return ((lane >= h * HEAD) & (lane < (h + 1) * HEAD)).astype(F32).astype(dtype)


def forward_windows(t, b, bias_of, last):
    g0, g1 = t.gains[b, 0:1, :], t.gains[b, 1:2, :]

    def window(w, carry):
        rows = pl.ds(pl.multiple_of(w * WT, WT), WT)
        x = t.x[rows, :].astype(F32)
        u = (stats(x)[0] * g0).astype(BF)
        q = nn(u, t.wq[0]).astype(BF)
        k = nn(u, t.wq[1]).astype(BF)
        v = nn(u, t.wq[2]).astype(BF)
        t.q[rows, :] = q
        t.k[rows, :] = k
        t.v[rows, :] = v
        mixed = jnp.zeros((WT, C), F32)
        for h in range(HEADS):
            s = nt(q * head_mask(h, BF), k) * (HEAD ** -0.5 * LOG2E) + bias_of(w, h)
            e = jnp.exp2(s - jnp.max(s, axis=-1, keepdims=True))
            p = (e * (1.0 / jnp.sum(e, axis=-1, keepdims=True))).astype(BF)
            t.p[pl.ds(pl.multiple_of(w * BROWS + h * WT, WT), WT), :] = p
            mixed = mixed + nn(p, v) * head_mask(h, F32)
        mixed = mixed.astype(BF)
        t.mix[rows, :] = mixed
        attended = nn(mixed, t.w_proj[b]).astype(BF)
        hidden = x + attended.astype(F32)
        t.hid[rows, :] = hidden
        n2 = (stats(hidden)[0] * g1).astype(BF)
        total = hidden
        for j in range(3):
            cols = slice(256 * j, 256 * j + 256)
            up = nn(n2, t.w_up[b, :, cols])
            cdf = 0.5 + 0.5 * lax.erf(up * (0.5 ** 0.5))
            slope = cdf + up * jnp.exp2(up * up * (-0.5 * LOG2E)) * (1.0 / math.sqrt(2 * math.pi))
            act = (up * cdf).astype(BF)
            t.a[rows, cols] = act
            t.gp[rows, cols] = slope.astype(BF)
            if not last:
                total = total + nt(act, t.w_down[b, :, cols])
        if not last:
            t.out[rows, :] = total.astype(BF)
        return carry

    lax.fori_loop(0, 4, window, 0, unroll=2)


def pairs(window, after_first=None):
    def body(i, carry):
        window(2 * i)
        window(2 * i + 1)
        if after_first is not None:
            pl.when(i == 0)(after_first)
        return carry

    lax.fori_loop(0, 2, body, 0)


def backward_feed(t, b):
    g1 = t.gains[b, 1:2, :]
    t.dg[...] = jnp.zeros((2, C), F32)

    def window(w):
        rows = pl.ds(pl.multiple_of(w * WT, WT), WT)
        dy = t.dout[rows, :]
        dn2 = jnp.zeros((WT, C), F32)
        for j in range(3):
            cols = slice(256 * j, 256 * j + 256)
            da = nn(dy, t.w_down[b, :, cols]).astype(BF).astype(F32)
            dup = (da * t.gp[rows, cols].astype(F32)).astype(BF)
            t.dup[rows, cols] = dup
            dn2 = dn2 + nt(dup, t.w_up[b, :, cols])
        dn2 = dn2.astype(BF).astype(F32)
        xhat, r = stats(t.hid[rows, :])
        t.n2[rows, :] = (xhat * g1).astype(BF)
        t.dg[1:2, :] += jnp.sum(dn2 * xhat, axis=0, keepdims=True)
        t.datt[rows, :] = (dy.astype(F32) + norm_back(dn2, g1, xhat, r)).astype(BF)

    pairs(window)


def backward_attention(t, b, dbias_of, after_first):
    g0 = t.gains[b, 0:1, :]

    def window(w):
        rows = pl.ds(pl.multiple_of(w * WT, WT), WT)
        datt = t.datt[rows, :]
        dmix = nt(datt, t.w_proj[b]).astype(BF)
        q = t.q[rows, :]
        k = t.k[rows, :]
        v = t.v[rows, :]
        doms = jnp.concatenate([dmix * head_mask(h, BF) for h in range(HEADS)], axis=0)
        qms = jnp.concatenate([q * head_mask(h, BF) for h in range(HEADS)], axis=0)
        dps = nt(doms, v)
        pw = t.p[pl.ds(pl.multiple_of(w * BROWS, WT), BROWS), :]
        dss = []
        for h in range(HEADS):
            part = slice(h * WT, h * WT + WT)
            p = pw[part].astype(F32)
            pd = p * dps[part]
            ds = pd - p * jnp.sum(pd, axis=-1, keepdims=True)
            dbias_of(w, h, ds)
            dss.append(ds.astype(BF))
        dss = jnp.concatenate(dss, axis=0)
        dqs = nn(dss, k)
        dq = dqs[0:WT] * head_mask(0, F32)
        for h in range(1, HEADS):
            dq = dq + dqs[h * WT:h * WT + WT] * head_mask(h, F32)
        dq = (dq * HEAD ** -0.5).astype(BF)
        dk = (tn(dss, qms) * HEAD ** -0.5).astype(BF)
        dv = tn(pw, doms).astype(BF)
        t.dq[rows, :] = dq
        t.dk[rows, :] = dk
        t.dv[rows, :] = dv
        du = nt(dq, t.wq[0]) + nt(dk, t.wq[1]) + nt(dv, t.wq[2])
        du = du.astype(BF).astype(F32)
        xhat, r = stats(t.x[rows, :].astype(F32))
        t.u[rows, :] = (xhat * g0).astype(BF)
        t.dg[0:1, :] += jnp.sum(du * xhat, axis=0, keepdims=True)
        dx = norm_back(du, g0, xhat, r).astype(BF).astype(F32) + datt.astype(F32)
        t.dx[rows, :] = dx.astype(BF)

    pairs(window, after_first)


def product_left(lhs, x):
    return tn(lhs, jnp.concatenate([x, jnp.zeros((NT, 64), BF)], axis=1))


def product_right(lhs, x):
    return tn(lhs, jnp.concatenate([jnp.zeros((NT, 64), BF), x], axis=1))


def products_early(t):
    n2, dout = t.n2[...], t.dout[...]
    down_low = product_right(t.a[:, 0:384], dout)
    up_high = product_right(t.dup[:, 384:768], n2)
    for i, right in enumerate((up_high[0:192], up_high[192:384], down_low[0:192])):
        t.part[0, 192 * i:192 * i + 192, 128:384] = right.astype(BF)
    down_high = product_right(t.a[:, 384:768], dout)
    up_low = product_left(t.dup[:, 0:384], n2)
    proj = product_left(t.datt[...], t.mix[...])
    for i, (left, right) in enumerate(((proj, down_low[192:384]), (up_low[0:192], down_high[0:192]), (up_low[192:384], down_high[192:384]))):
        rows = slice(192 * i, 192 * i + 192)
        t.part[1, rows, 0:128] = left[:, 0:128].astype(BF)
        t.part[1, rows, 128:256] = (left[:, 128:256] + right[:, 0:128]).astype(BF)
        t.part[1, rows, 256:384] = right[:, 128:256].astype(BF)


def products_late(t):
    u = t.u[...]
    for i, ref in enumerate((t.dq, t.dk, t.dv)):
        rows = slice(192 * i, 192 * i + 192)
        left = product_left(ref[...], u)
        t.part[0, rows, 0:128] = left[:, 0:128].astype(BF)
        t.part[0, rows, 128:256] = (left[:, 128:256] + t.part[0, rows, 128:256].astype(F32)).astype(BF)


def other_rows(t):
    flat = jnp.concatenate([t.dg[0:1, :], t.dg[1:2, :], jnp.zeros((1, 3 * WT - 2 * C), F32)], axis=1)
    t.db[BROWS:OROWS, :] = jnp.concatenate([flat[:, 0:WT], flat[:, WT:2 * WT], flat[:, 2 * WT:3 * WT], jnp.zeros((OROWS - BROWS - 3, WT), F32)], axis=0)
    gap = jnp.zeros((240, 48), F32)
    for core in range(2):
        lft = t.db[lat_row(core):lat_row(core) + 240, :]
        rgt = t.db[lat_row(2 + core):lat_row(2 + core) + 240, :]
        t.part[core, 576:816, :] = jnp.concatenate([lft, gap, rgt, gap], axis=1).astype(BF)


def half_of(shape, axis):
    return (lax.broadcasted_iota(jnp.int32, shape, axis) // 36) % 2


def lane_moves(low):
    src = lax.broadcasted_iota(jnp.int32, (WT, WT), 0)
    dst = lax.broadcasted_iota(jnp.int32, (WT, WT), 1)
    keep = dst - 36 * ((dst // 36) % 2) + (0 if low else 36)
    return (src == keep).astype(F32)


def polar_bias(table, low):
    moved = jnp.dot(table, lane_moves(low), precision=lax.Precision.HIGHEST, preferred_element_type=F32)
    half = half_of((WT, WT), 0)
    if low:
        moved = jnp.where(half == 0, moved, pltpu.roll(moved, 36, 0))
    else:
        moved = jnp.where(half == 1, moved, pltpu.roll(moved, WT - 36, 0))
    return jnp.where(half == half_of((WT, WT), 1), moved, -1e30)


def polar_back(grad, low):
    half = half_of((WT, WT), 0)
    if low:
        folded = jnp.where(half == 0, grad + pltpu.roll(grad, WT - 36, 0), 0.0)
    else:
        folded = jnp.where(half == 1, grad + pltpu.roll(grad, 36, 0), 0.0)
    return lax.dot_general(folded, lane_moves(low), (((1,), (1,)), ((), ())), precision=lax.Precision.HIGHEST, preferred_element_type=F32)


def greet(peers):
    barrier = pltpu.get_barrier_semaphore()
    for cond, dev in peers:
        if cond is None:
            pl.semaphore_signal(barrier, inc=1, device_id=dev, device_id_type=MESH)
        else:
            @pl.when(cond)
            def _():
                pl.semaphore_signal(barrier, inc=1, device_id=dev, device_id_type=MESH)


def guarded(cond, act):
    if cond is None:
        act()
    else:
        pl.when(cond)(act)


class Exchange:
    def __init__(self, moves, src, dst, send_sem, recv_sem, base, here):
        self.sends, self.locals, self.recvs = moves
        self.src, self.dst, self.send_sem, self.recv_sem, self.base, self.here = src, dst, send_sem, recv_sem, base, here

    def remote(self, i, s, d, size, dev):
        return pltpu.make_async_remote_copy(
            src_ref=self.src.at[pl.ds(s, size), :], dst_ref=self.dst.at[pl.ds(d, size), :], send_sem=self.send_sem.at[self.base + i],
            recv_sem=self.recv_sem.at[self.base + i], device_id=dev, device_id_type=MESH)

    def start(self):
        for i, cond, s, d, size, dev in self.sends:
            guarded(cond, lambda: self.remote(i, s, d, size, dev).start())
        for cond, s, d, size in self.locals:
            def keep():
                self.dst[d:d + size, :] = self.src[s:s + size, :]
            guarded(cond, keep)

    def finish(self):
        for i, cond, d, size in self.recvs:
            guarded(cond, lambda: self.remote(i, 0, d, size, self.here).wait_recv())
        for i, cond, s, d, size, dev in self.sends:
            guarded(cond, lambda: self.remote(i, s, d, size, dev).wait_send())


def moves_out(n):
    sends = [
        (0, None, 432, 432, 48, (n.b, n.east)),
        (1, n.inner_up, 112, 592, 48, (n.up, n.east)),
        (2, n.first, 112, 112, 48, (n.b, n.east)),
        (3, n.inner_up, 0, 480, 112, (n.up, n.j)),
        (4, n.inner_down, 480, 0, 160, (n.down, n.j)),
    ]
    locals_ = [(None, 160, 160, 272), (n.first, 0, 0, 112), (n.last, 480, 480, 160)]
    recvs = [(0, None, 432, 48), (1, n.inner_down, 592, 48), (2, n.first, 112, 48), (3, n.inner_down, 480, 112), (4, n.inner_up, 0, 160)]
    return sends, locals_, recvs


def moves_back(n):
    sends = [
        (0, None, 432, 432, 48, (n.b, n.west)),
        (1, n.inner_down, 592, 112, 48, (n.down, n.west)),
        (2, n.first, 112, 112, 48, (n.b, n.west)),
        (3, n.inner_down, 480, 0, 112, (n.down, n.j)),
        (4, n.inner_up, 0, 480, 160, (n.up, n.j)),
    ]
    locals_ = [(None, 160, 160, 272), (n.first, 0, 0, 112), (n.last, 480, 480, 160)]
    recvs = [(0, None, 432, 48), (1, n.inner_up, 112, 48), (2, n.first, 112, 48), (3, n.inner_up, 0, 112), (4, n.inner_down, 480, 160)]
    return sends, locals_, recvs


def lat_row(lat):
    return ((650 * lat) // 48) * 16


def z_row(core, z):
    return ((52 * core + 325 * z) // 96) * 16


def x_row(core, z, x):
    return ((208 * core + 1300 * z + 325 * x) // 384) * 16


def al(v):
    return pl.multiple_of(v, 16)


def total(*terms):
    out = terms[0].astype(F32)
    for term in terms[1:]:
        out = out + term.astype(F32)
    return out


class Reduce:
    def __init__(self, n, t, send_sem, recv_sem, base):
        self.n, self.t, self.send_sem, self.recv_sem, self.base = n, t, send_sem, recv_sem, base

    def remote(self, i, s, d, dev):
        i = self.base + i
        return pltpu.make_async_remote_copy(src_ref=s, dst_ref=d, send_sem=self.send_sem.at[i], recv_sem=self.recv_sem.at[i], device_id=dev, device_id_type=MESH)

    def core_copies(self):
        n, t = self.n, self.t
        pal = n.device(core=1 - n.core)
        return (
            self.remote(0, t.part.at[1, pl.ds(0, 576), :], t.got_core.at[pl.ds(0, 576), :], pal),
            self.remote(1, t.part.at[0, pl.ds(0, 576), pl.ds(256, 128)], t.got_core.at[pl.ds(0, 576), pl.ds(256, 128)], pal),
            self.remote(2, t.part.at[1 - n.core, pl.ds(576, 240), :], t.got_core.at[pl.ds(576, 240), :], pal),
            self.remote(3, t.part.at[0, pl.ds(0, 576), pl.ds(0, 256)], t.got_core.at[pl.ds(0, 576), pl.ds(0, 256)], pal),
        )

    def first_copies(self):
        n, t = self.n, self.t
        tile2, tiles01, other = [], [], []
        for d in range(1, 4):
            i = 4 * d
            z = (n.z + d) % 4
            x = (n.x + d) % 4
            to_x, to_z = n.device(x=x), n.device(z=z)
            rows = pl.ds(al(32 * x), 48)
            tile2.append(self.remote(i, t.sum_m.at[:, rows, pl.ds(256, 128)], t.got_x.at[d - 1, :, :, pl.ds(128, 128)], to_x))
            tiles01.append(self.remote(i + 1, t.sum_m.at[:, rows, pl.ds(128, 128)], t.got_x.at[d - 1, :, :, pl.ds(0, 128)], to_x))
            tiles01.append(self.remote(i + 2, t.sum_m.at[z, :, pl.ds(0, 128)], t.got_z.at[d - 1], to_z))
            other.append(self.remote(i + 3, t.sum_o.at[pl.ds(al(z_row(n.core, z)), 80), :], t.got_o.at[d - 1], to_z))
        return tile2, tiles01, other

    def x_window(self, x):
        return al(x_row(self.n.core, self.n.z, x) - z_row(self.n.core, self.n.z))

    def second_copies(self):
        n, t = self.n, self.t
        out = []
        for d in range(1, 4):
            i = 3 * d + 13
            z = (n.z + d) % 4
            x = (n.x + d) % 4
            out.append(self.remote(i, t.sum_x.at[z], t.got_xz.at[d - 1], n.device(z=z)))
            dev = n.device(x=x)
            out.append(self.remote(i + 1, t.sum_zo.at[pl.ds(self.x_window(x), 32), :], t.got_ox.at[d - 1], dev))
            out.append(self.remote(i + 2, t.sum_z.at[pl.ds(al(32 * x), 48), :], t.got_zx.at[d - 1], dev))
        return out

    def third_copies(self):
        n, t = self.n, self.t
        devices = [n.device(yl=1 - n.yl), n.device(yh=1 - n.yh), n.device(yl=1 - n.yl, yh=1 - n.yh)]
        return [self.remote(25 + i, t.mid, t.got_y.at[i], dev) for i, dev in enumerate(devices)]

    def start(self, copies):
        for c in copies:
            c.start()

    def wait(self, copies):
        for c in copies:
            c.wait()

    def early_start(self):
        both = self.core_copies()
        for core in range(2):
            pl.when(self.n.core == core)(both[core].start)

    def early_to_first(self):
        n, t = self.n, self.t
        copies = self.core_copies()
        tile2, tiles01, _ = self.first_copies()

        @pl.when(n.core == 0)
        def _():
            copies[1].wait_recv()
            for z in range(4):
                rows = slice(144 * z, 144 * z + 144)
                t.sum_m[z, :, 256:384] = total(t.part[0, rows, 256:384], t.got_core[rows, 256:384]).astype(BF)
            self.start(tile2)
            copies[0].wait_send()

        @pl.when(n.core == 1)
        def _():
            copies[0].wait_recv()
            for z in range(4):
                rows = slice(144 * z, 144 * z + 144)
                t.sum_m[z] = total(t.part[1, rows, :], t.got_core[rows, :]).astype(BF)
            self.start(tile2 + tiles01)
            copies[1].wait_send()

    def late_start(self):
        copies = self.core_copies()
        pl.when(self.n.core == 1)(copies[3].start)
        copies[2].start()

    def late_to_first(self):
        n, t = self.n, self.t
        copies = self.core_copies()
        _, tiles01, other = self.first_copies()

        @pl.when(n.core == 0)
        def _():
            copies[3].wait_recv()
            for z in range(4):
                rows = slice(144 * z, 144 * z + 144)
                t.sum_m[z, :, 0:256] = total(t.part[0, rows, 0:256], t.got_core[rows, 0:256]).astype(BF)
            self.start(tiles01)

        copies[2].wait_recv()
        t.sum_o[...] = total(t.part[n.core, 576:816, :], t.got_core[576:816, :]).astype(BF)
        self.start(other)
        copies[2].wait_send()
        pl.when(n.core == 1)(copies[3].wait_send)

    def first_to_second(self):
        n, t = self.n, self.t
        for copies in self.first_copies():
            self.wait(copies)
        t.sum_x[...] = total(t.sum_m[:, pl.ds(al(32 * n.x), 48), 128:384], *[t.got_x[i] for i in range(3)]).astype(BF)
        t.sum_zo[...] = total(t.sum_o[pl.ds(al(z_row(n.core, n.z)), 80), :], *[t.got_o[i] for i in range(3)]).astype(BF)
        t.sum_z[...] = total(t.sum_m[n.z, :, 0:128], *[t.got_z[i] for i in range(3)]).astype(BF)
        self.start(self.second_copies())

    def second_to_third(self):
        n, t = self.n, self.t
        self.wait(self.second_copies())
        t.mid[0:48, 0:128] = total(t.sum_z[pl.ds(al(32 * n.x), 48), :], *[t.got_zx[i] for i in range(3)]).astype(BF)
        t.mid[0:48, 128:384] = total(t.sum_x[n.z], *[t.got_xz[i] for i in range(3)]).astype(BF)
        t.mid[48:80, :] = total(t.sum_zo[pl.ds(self.x_window(n.x), 32), :], *[t.got_ox[i] for i in range(3)]).astype(BF)
        self.start(self.third_copies())

    def finish(self):
        self.wait(self.third_copies())
        return total(self.t.mid[...], *[self.t.got_y[i] for i in range(3)])


def group_squares(n, final):
    matrix, other = final[0:48, :], final[48:80, :]
    row = lax.broadcasted_iota(jnp.int32, (48, 384), 0)
    low = 4 * n.x
    squares = jnp.sum(jnp.where((row >= low) & (row < low + 36), matrix * matrix, 0.0), axis=0, keepdims=True)
    lane = lax.broadcasted_iota(jnp.int32, (32, 384), 1)
    row = lax.broadcasted_iota(jnp.int32, (32, 384), 0) + x_row(n.core, n.z, n.x)
    for yh in range(2):
        lat = 2 * yh + n.core
        at = lane - C * yh
        index = (row + lat_row(lat)) * WT + at
        low = 975 * (32 * lat + 8 * n.z + 2 * n.x)
        inside = (index >= low) & (index < low + 1950) & (at >= 0) & (at < WT)
        squares = squares + jnp.sum(jnp.where(inside, other * other, 0.0), axis=0, keepdims=True)
    return jnp.sum(squares, axis=1, keepdims=True)


def own_lanes(n, final):
    return jnp.where(n.yh == 1, pltpu.roll(final, C, 1), final)[:, 0:256]


INPUTS = ["tok", "cot", "gains", "w_qkv", "w_proj", "w_up", "w_down", "bias", "to_win", "to_nat", "send_win", "win_send", "send_nat", "to_slots", "from_slots"]
PERMS = INPUTS[8:]
OUTPUTS = [("gtok", (NT, C), BF), ("m", (18, 2, C), F32), ("o", (2, 975), F32)]
COPIED = ["to_win", "tok", "w_qkv", "bias", "w_proj", "w_up", "w_down", "send_win", "send_nat", "cot", "to_slots", "from_slots", "win_send", "to_nat"]
SHAPES = {
    "tok": (NT, C), "cot": (NT, C), "w_qkv": (2, C, 3 * C), "w_proj": (2, C, C), "w_up": (2, C, FFN), "w_down": (2, C, FFN), "bias": (2, BROWS, WT),
    "to_win": (NT, NT), "to_nat": (NT, NT), "send_win": (NR, NT), "win_send": (NT, NR), "send_nat": (NR, NT), "to_slots": (NT, NR), "from_slots": (NR, NT),
}
BLOCK = [
    ("x", (NT, C), BF), ("wq", (3, C, C), BF), ("q", (NT, C), BF), ("k", (NT, C), BF), ("v", (NT, C), BF), ("p", (4 * BROWS, WT), BF),
    ("mix", (NT, C), BF), ("hid", (NT, C), F32), ("a", (NT, FFN), BF), ("gp", (NT, FFN), BF), ("dout", (NT, C), BF), ("part", (2, 816, 384), BF),
    ("got_core", (816, 384), BF), ("sum_m", (4, 144, 384), BF), ("sum_o", (240, 384), BF),
    ("got_x", (3, 4, 48, 256), BF), ("got_o", (3, 80, 384), BF), ("got_z", (3, 144, 128), BF),
    ("sum_x", (4, 48, 256), BF), ("sum_zo", (80, 384), BF), ("sum_z", (144, 128), BF),
    ("got_xz", (3, 48, 256), BF), ("got_ox", (3, 32, 384), BF), ("got_zx", (3, 48, 128), BF),
    ("mid", (80, 384), BF), ("got_y", (3, 80, 384), BF),
    ("db", (OROWS, WT), F32), ("dg", (2, C), F32),
]
SHARED = [
    ("out", (NT, C), BF), ("dx", (NT, C), BF), ("u", (NT, C), BF), ("n2", (NT, C), BF), ("datt", (NT, C), BF), ("dq", (NT, C), BF), ("dk", (NT, C), BF),
    ("dv", (NT, C), BF), ("dup", (NT, FFN), BF),
    ("lbias", (3, BROWS, WT), F32), ("db_pair", (2, BROWS, WT), F32), ("parts", (32, 1, 128), F32), ("own", (2, 80, 256), F32),
    ("cot_src", (NR, 256), BF), ("cot_dst", (NR, 256), BF), ("mid_src", (NR, 256), BF), ("mid_dst", (NR, 256), BF), ("back_src", (NR, 256), BF), ("back_dst", (NR, 256), BF),
]
SEMS = 15 + 56 + 31


def place(nlat, nlon):
    n = types.SimpleNamespace()
    n.b, n.j = lax.axis_index("lat"), lax.axis_index("lon")
    n.east, n.west = lax.rem(n.j + 1, nlon), lax.rem(n.j + nlon - 1, nlon)
    n.up, n.down = jnp.maximum(n.b - 1, 0), jnp.minimum(n.b + 1, nlat - 1)
    n.first, n.last = n.b == 0, n.b == nlat - 1
    n.inner_up, n.inner_down = n.b > 0, n.b < nlat - 1
    n.yh, n.core = n.b // 2, n.b % 2
    n.z, n.x, n.yl = n.j // 8, (n.j // 2) % 4, n.j % 2

    def device(yh=n.yh, core=n.core, z=n.z, x=n.x, yl=n.yl):
        return (yh * 2 + core, z * 8 + x * 2 + yl)

    n.device = device
    return n


def kernel(nlat, nlon, reduce, *refs):
    names = INPUTS + [o[0] for o in OUTPUTS] + ["first_" + e[0] for e in BLOCK] + ["second_" + e[0] for e in BLOCK] + [e[0] for e in SHARED] + ["in_" + k for k in COPIED] + ["send_sem", "recv_sem", "in_sem"]
    r = dict(zip(names, refs, strict=True))
    loads = {}
    for i, k in enumerate(COPIED):
        src, dst = r[k], r["in_" + k]
        if k == "bias":
            loads["bias"] = pltpu.make_async_copy(src.at[0], dst.at[0], r["in_sem"].at[i])
        else:
            loads[k] = pltpu.make_async_copy(src, dst, r["in_sem"].at[i])
        if k == "w_down":
            loads["bias_two"] = pltpu.make_async_copy(r["bias"].at[1], r["in_bias"].at[1], r["in_sem"].at[len(COPIED)])
    for copy in loads.values():
        copy.start()

    def need(*keys):
        for k in keys:
            loads[k].wait()

    weights = {k: r["in_" + k] if k in COPIED else r[k] for k in INPUTS}
    blocks = []
    for label in ("first_", "second_"):
        blocks.append(types.SimpleNamespace(**weights, **{e[0]: r[e[0]] for e in SHARED}, **{e[0]: r[label + e[0]] for e in BLOCK}))
    one, two = blocks
    n = place(nlat, nlon)
    sems = (r["send_sem"], r["recv_sem"])
    here = (n.b, n.j)
    ex_cot = Exchange(moves_out(n), one.cot_src, one.cot_dst, *sems, 0, here)
    ex_mid = Exchange(moves_out(n), one.mid_src, one.mid_dst, *sems, 5, here)
    ex_back = Exchange(moves_back(n), one.back_src, one.back_dst, *sems, 10, here)

    level = [(e, dz, dx) for e in range(2) for dz in range(4) for dx in range(4) if (e, dz, dx) != (0, 0, 0)]
    level_dev = [n.device(core=(n.core + e) % 2, z=(n.z + dz) % 4, x=(n.x + dx) % 4) for e, dz, dx in level]
    y_dev = [n.device(yl=1 - n.yl), n.device(yh=1 - n.yh), n.device(yl=1 - n.yl, yh=1 - n.yh)]
    far = level_dev + y_dev if reduce else []
    greet(
        [(None, (n.b, n.east)), (None, (n.b, n.west)), (n.inner_up, (n.up, n.j)), (n.inner_down, (n.down, n.j)), (n.inner_up, (n.up, n.east)), (n.inner_down, (n.down, n.west))]
        + [(None, d) for d in far]
    )

    need("to_win", "tok")
    one.x[...] = shuffle(one.to_win[...], one.tok[...])
    need("w_qkv")
    for b, t in enumerate(blocks):
        for i in range(3):
            t.wq[i] = t.w_qkv[b, :, C * i:C * i + C]
    need("bias")
    one.lbias[0] = one.bias[0] * LOG2E
    need("w_proj", "w_up", "w_down")
    forward_windows(one, 0, lambda w, h: one.lbias[0, h * WT:h * WT + WT, :], False)
    need("send_win")
    one.mid_src[:, 0:C] = shuffle(one.send_win[...], one.out[...])
    pl.semaphore_wait(pltpu.get_barrier_semaphore(), jnp.where(jnp.logical_or(n.first, n.last), 4, 6) + len(far))
    ex_mid.start()
    need("send_nat", "cot")
    one.cot_src[:, 0:C] = shuffle(one.send_nat[...], one.cot[...])
    ex_cot.start()
    need("bias_two", "to_slots", "from_slots", "win_send", "to_nat")

    for group in range(2):
        polar = n.first if group == 0 else n.last

        @pl.when(polar)
        def _():
            for h in range(HEADS):
                rows = slice(h * WT, h * WT + WT)
                two.lbias[1 + group, rows, :] = polar_bias(two.bias[1, rows, :] * LOG2E, group == 1)

        @pl.when(jnp.logical_not(polar))
        def _():
            two.lbias[1 + group] = two.bias[1] * LOG2E

    two.db_pair[...] = jnp.zeros((2, BROWS, WT), F32)
    ex_mid.finish()
    two.x[...] = shuffle(two.to_slots[...], two.mid_dst[:, 0:C])
    forward_windows(two, 1, lambda w, h: two.lbias[1 + w // 2, h * WT:h * WT + WT, :], True)

    def dbias_two(w, h, ds):
        two.db_pair[w // 2, h * WT:h * WT + WT, :] += ds

    ex_cot.finish()
    two.dout[...] = shuffle(two.to_slots[...], two.cot_dst[:, 0:C])
    red_one = Reduce(n, one, *sems, 15)
    red_two = Reduce(n, two, *sems, 43)

    def only_reducing(act):
        if reduce:
            act()

    backward_feed(two, 1)
    products_early(two)
    only_reducing(red_two.early_start)
    backward_attention(two, 1, dbias_two, red_two.early_to_first if reduce else None)
    two.back_src[:, 0:C] = shuffle(two.from_slots[...], two.dx[...])
    ex_back.start()
    for group in range(2):
        @pl.when(n.first if group == 0 else n.last)
        def _():
            for h in range(HEADS):
                rows = slice(h * WT, h * WT + WT)
                two.db_pair[group, rows, :] = polar_back(two.db_pair[group, rows, :], group == 1)

    two.db[0:BROWS, :] = two.db_pair[0] + two.db_pair[1]
    products_late(two)
    other_rows(two)
    only_reducing(red_two.late_start)

    ex_back.finish()
    only_reducing(red_two.late_to_first)
    one.dout[...] = shuffle(one.win_send[...], one.back_dst[:, 0:C])
    one.db[...] = jnp.zeros((OROWS, WT), F32)

    def dbias_one(w, h, ds):
        one.db[h * WT:h * WT + WT, :] += ds

    backward_feed(one, 0)
    products_early(one)
    only_reducing(red_one.early_start)

    def middle():
        red_two.first_to_second()
        red_one.early_to_first()

    backward_attention(one, 0, dbias_one, middle if reduce else None)
    products_late(one)
    other_rows(one)
    only_reducing(red_one.late_start)
    r["gtok"][...] = shuffle(one.to_nat[...], one.dx[...])
    if not reduce:
        return
    red_two.second_to_third()
    red_one.late_to_first()
    two_final = red_two.finish()
    squares = group_squares(n, two_final)
    red_one.first_to_second()
    red_one.second_to_third()
    one_final = red_one.finish()

    parts = one.parts
    parts[0] = jnp.broadcast_to(squares + group_squares(n, one_final), (1, 128))
    copies = [
        pltpu.make_async_remote_copy(src_ref=parts.at[0], dst_ref=parts.at[1 + i], send_sem=sems[0].at[71 + i], recv_sem=sems[1].at[71 + i], device_id=d, device_id_type=MESH)
        for i, d in enumerate(level_dev)
    ]
    for c in copies:
        c.start()
    for c in copies:
        c.wait()
    acc = parts[0]
    for i in range(len(copies)):
        acc = acc + parts[1 + i]
    ceiling = math.sqrt(24 * C * C + 2 * VECB)
    factor = jnp.minimum(1.0, ceiling / (jnp.sqrt(acc) + 1e-06))[0:1, 0:1]
    first_row = 4 * n.x + 18 * n.yl
    start = 975 * (32 * n.b + n.j) - (lat_row(n.b) + x_row(n.core, n.z, n.x)) * WT
    rows = []
    for b, final in enumerate((one_final, two_final)):
        one.own[b] = own_lanes(n, final) * factor
        for i in range(18):
            r["m"][i, b:b + 1, :] = one.own[b, pl.ds(first_row + i, 1), 0:C]
        rows.append(jnp.concatenate([one.own[b, pl.ds(48 + start // WT + i, 1), 0:WT] for i in range(8)], axis=1))
    flat = jnp.concatenate(rows + [jnp.zeros((6, 8 * WT), F32)], axis=0)
    r["o"][...] = pltpu.roll(flat, 8 * WT - start % WT, 1)[0:2, 0:975]


def run(nlat, nlon, reduce, tokens, cotangent, norm_gains, w_qkv, w_proj, w_up, w_down, pos_bias):
    args = [tokens.reshape(NT, C), cotangent.reshape(NT, C), norm_gains, w_qkv, w_proj, w_up, jnp.swapaxes(w_down, 1, 2), pos_bias.reshape(2, BROWS, WT)]
    args += [const(p) for p in PERMS]
    vmem = pl.BlockSpec(memory_space=pltpu.VMEM)
    anywhere = pl.BlockSpec(memory_space=pl.ANY)
    return pl.pallas_call(
        functools.partial(kernel, nlat, nlon, reduce),
        in_specs=[anywhere if k in COPIED else vmem for k in INPUTS],
        out_specs=[vmem] * len(OUTPUTS),
        out_shape=[jax.ShapeDtypeStruct(s, d) for _, s, d in OUTPUTS],
        scratch_shapes=[pltpu.VMEM(s, d) for _, s, d in BLOCK + BLOCK + SHARED] + [pltpu.VMEM(SHAPES[k], F32 if k == "bias" else BF) for k in COPIED]
        + [pltpu.SemaphoreType.DMA((SEMS,))] * 2 + [pltpu.SemaphoreType.DMA((len(COPIED) + 1,))],
        compiler_params=pltpu.CompilerParams(vmem_limit_bytes=VMEM_LIMIT, collective_id=1, has_side_effects=True),
        name="two_blocks",
    )(*args)


def copy_out(*refs):
    k = len(OUTPUTS)
    sem = refs[3 * k]
    loads = [pltpu.make_async_copy(refs[i], refs[2 * k + i], sem.at[i]) for i in range(k)]
    stores = [pltpu.make_async_copy(refs[2 * k + i], refs[k + i], sem.at[k + i]) for i in range(k)]
    for c in loads:
        c.start()
    for c, d in zip(loads[::-1], stores[::-1]):
        c.wait()
        d.start()
    for d in stores:
        d.wait()


def run_copy_out(results):
    anywhere = pl.BlockSpec(memory_space=pl.ANY)
    return pl.pallas_call(
        copy_out,
        in_specs=[anywhere] * len(results),
        out_specs=[anywhere] * len(results),
        out_shape=[jax.ShapeDtypeStruct(s, d) for _, s, d in OUTPUTS],
        scratch_shapes=[pltpu.VMEM(s, d) for _, s, d in OUTPUTS] + [pltpu.SemaphoreType.DMA((2 * len(OUTPUTS),))],
        name="copy_out",
    )(*results)


def shards(nlat, nlon, tokens, *args):
    gtok, m, o = run_copy_out(run(nlat, nlon, True, tokens, *args))
    return gtok.reshape(tokens.shape), m.transpose(1, 2, 0), o


def solution(mesh):
    grid = P(None, "lat", "lon", None)
    return jax.shard_map(
        functools.partial(shards, mesh.shape["lat"], mesh.shape["lon"]),
        mesh=mesh,
        in_specs=(grid, grid) + (P(),) * 6,
        out_specs=(grid, P(None, None, ("lat", "lon")), P(None, ("lat", "lon"))),
        check_vma=False,
    )
```

```python
import functools
import math
import types

import jax
import jax.numpy as jnp
import numpy as np
from jax import lax
from jax.experimental import pallas as pl
from jax.experimental.pallas import tpu as pltpu
from jax.sharding import PartitionSpec as P

C = 192
HEADS = 6
HEAD = 32
FFN = 768
WT = 144
NT = 576
NR = 640
QT = 160
MAIN = 112
VECB = 124800
BROWS = HEADS * WT
MROWS = 2304
OROWS = 880
GROWS = MROWS + OROWS
LOG2E = math.log2(math.e)
MESH = pl.DeviceIdType.MESH
BF = jnp.bfloat16
F32 = jnp.float32
VMEM_LIMIT = 56 * 1024 * 1024


def nat(l, r, c):
    return l * 288 + r * 48 + c


def one_hot(sources, width):
    mat = np.zeros((len(sources), width), np.float32)
    for i, s in enumerate(sources):
        if s >= 0:
            mat[i, s] = 1.0
    return mat


@functools.cache
def orders():
    win = [nat(l, r, 12 * w + c) for w in range(4) for l in range(2) for r in range(6) for c in range(12)]

    def cells(rows, cols, size):
        out = [nat(l, r, c) for l in range(2) for r in rows for c in cols]
        return out + [-1] * (size - len(out))

    top, low = range(0, 3), range(3, 6)
    send = []
    for rows in (top, low):
        send += cells(rows, range(0, 18), MAIN)
        send += cells(rows, range(42, 48), QT - MAIN)
        send += cells(rows, range(24, 42), MAIN)
        send += cells(rows, range(18, 24), QT - MAIN)
    slots = []
    for s in range(4):
        for l in range(2):
            for half in range(2):
                for r in range(3):
                    for cc in range(12):
                        col = 12 * (s % 2) + cc
                        base = QT * (2 * (s // 2) + half)
                        if col >= 6:
                            slots.append(base + (l * 3 + r) * 18 + col - 6)
                        else:
                            slots.append(base + MAIN + (l * 3 + r) * 6 + col)
    win_at = {n: i for i, n in enumerate(win)}
    send_win = [win_at[n] if n >= 0 else -1 for n in send]
    to_win = one_hot(win, NT)
    send_from_win = one_hot(send_win, NT)
    send_from_nat = one_hot(send, NT)
    to_slots = one_hot(slots, NR)
    return {
        "to_win": to_win,
        "to_nat": to_win.T.copy(),
        "send_win": send_from_win,
        "win_send": send_from_win.T.copy(),
        "send_nat": send_from_nat,
        "to_slots": to_slots,
        "from_slots": to_slots.T.copy(),
    }


def const(name):
    return jnp.asarray(orders()[name], BF)


def nn(a, b):
    return lax.dot_general(a, b, (((1,), (0,)), ((), ())), preferred_element_type=F32)


def nt(a, b):
    return lax.dot_general(a, b, (((1,), (1,)), ((), ())), preferred_element_type=F32)


def tn(a, b):
    return lax.dot_general(a, b, (((0,), (0,)), ((), ())), preferred_element_type=F32)


def shuffle(mat, x):
    return nn(mat, x).astype(BF)


def stats(x):
    center = x - jnp.mean(x, axis=-1, keepdims=True)
    r = lax.rsqrt(jnp.mean(center * center, axis=-1, keepdims=True) + 1e-05)
    return center * r, r


def norm_back(dn, gain, xhat, r):
    t = dn * gain
    return r * (t - jnp.mean(t, axis=-1, keepdims=True) - xhat * jnp.mean(t * xhat, axis=-1, keepdims=True))


def head_mask(h, dtype):
    lane = lax.broadcasted_iota(jnp.int32, (1, C), 1)
    return ((lane >= h * HEAD) & (lane < (h + 1) * HEAD)).astype(F32).astype(dtype)


def forward_windows(t, b, bias_of, last):
    g0, g1 = t.gains[b, 0:1, :], t.gains[b, 1:2, :]

    def window(w, carry):
        rows = pl.ds(pl.multiple_of(w * WT, WT), WT)
        x = t.x[rows, :].astype(F32)
        u = (stats(x)[0] * g0).astype(BF)
        q = nn(u, t.wq[0]).astype(BF)
        k = nn(u, t.wq[1]).astype(BF)
        v = nn(u, t.wq[2]).astype(BF)
        t.q[rows, :] = q
        t.k[rows, :] = k
        t.v[rows, :] = v
        mixed = jnp.zeros((WT, C), F32)
        for h in range(HEADS):
            s = nt(q * head_mask(h, BF), k) * (HEAD ** -0.5 * LOG2E) + bias_of(w, h)
            e = jnp.exp2(s - jnp.max(s, axis=-1, keepdims=True))
            p = (e * (1.0 / jnp.sum(e, axis=-1, keepdims=True))).astype(BF)
            t.p[pl.ds(pl.multiple_of(w * BROWS + h * WT, WT), WT), :] = p
            mixed = mixed + nn(p, v) * head_mask(h, F32)
        mixed = mixed.astype(BF)
        t.mix[rows, :] = mixed
        attended = nn(mixed, t.w_proj[b]).astype(BF)
        hidden = x + attended.astype(F32)
        t.hid[rows, :] = hidden
        n2 = (stats(hidden)[0] * g1).astype(BF)
        total = hidden
        for j in range(3):
            cols = slice(256 * j, 256 * j + 256)
            up = nn(n2, t.w_up[b, :, cols])
            cdf = 0.5 + 0.5 * lax.erf(up * (0.5 ** 0.5))
            slope = cdf + up * jnp.exp2(up * up * (-0.5 * LOG2E)) * (1.0 / math.sqrt(2 * math.pi))
            act = (up * cdf).astype(BF)
            t.a[rows, cols] = act
            t.gp[rows, cols] = slope.astype(BF)
            if not last:
                total = total + nt(act, t.w_down[b, :, cols])
        if not last:
            t.out[rows, :] = total.astype(BF)
        return carry

    lax.fori_loop(0, 4, window, 0, unroll=2)


def pairs(window, after_first=None):
    def body(i, carry):
        window(2 * i)
        window(2 * i + 1)
        if after_first is not None:
            pl.when(i == 0)(after_first)
        return carry

    lax.fori_loop(0, 2, body, 0)


def backward_feed(t, b):
    g1 = t.gains[b, 1:2, :]
    t.dg[...] = jnp.zeros((2, C), F32)

    def window(w):
        rows = pl.ds(pl.multiple_of(w * WT, WT), WT)
        dy = t.dout[rows, :]
        dn2 = jnp.zeros((WT, C), F32)
        for j in range(3):
            cols = slice(256 * j, 256 * j + 256)
            da = nn(dy, t.w_down[b, :, cols]).astype(BF).astype(F32)
            dup = (da * t.gp[rows, cols].astype(F32)).astype(BF)
            t.dup[rows, cols] = dup
            dn2 = dn2 + nt(dup, t.w_up[b, :, cols])
        dn2 = dn2.astype(BF).astype(F32)
        xhat, r = stats(t.hid[rows, :])
        t.n2[rows, :] = (xhat * g1).astype(BF)
        t.dg[1:2, :] += jnp.sum(dn2 * xhat, axis=0, keepdims=True)
        t.datt[rows, :] = (dy.astype(F32) + norm_back(dn2, g1, xhat, r)).astype(BF)

    pairs(window)


def backward_attention(t, b, dbias_of, after_first):
    g0 = t.gains[b, 0:1, :]

    def window(w):
        rows = pl.ds(pl.multiple_of(w * WT, WT), WT)
        datt = t.datt[rows, :]
        dmix = nt(datt, t.w_proj[b]).astype(BF)
        q = t.q[rows, :]
        k = t.k[rows, :]
        v = t.v[rows, :]
        doms = jnp.concatenate([dmix * head_mask(h, BF) for h in range(HEADS)], axis=0)
        qms = jnp.concatenate([q * head_mask(h, BF) for h in range(HEADS)], axis=0)
        dps = nt(doms, v)
        pw = t.p[pl.ds(pl.multiple_of(w * BROWS, WT), BROWS), :]
        dss = []
        for h in range(HEADS):
            part = slice(h * WT, h * WT + WT)
            p = pw[part].astype(F32)
            pd = p * dps[part]
            ds = pd - p * jnp.sum(pd, axis=-1, keepdims=True)
            dbias_of(w, h, ds)
            dss.append(ds.astype(BF))
        dss = jnp.concatenate(dss, axis=0)
        dqs = nn(dss, k)
        dq = dqs[0:WT] * head_mask(0, F32)
        for h in range(1, HEADS):
            dq = dq + dqs[h * WT:h * WT + WT] * head_mask(h, F32)
        dq = (dq * HEAD ** -0.5).astype(BF)
        dk = (tn(dss, qms) * HEAD ** -0.5).astype(BF)
        dv = tn(pw, doms).astype(BF)
        t.dq[rows, :] = dq
        t.dk[rows, :] = dk
        t.dv[rows, :] = dv
        du = nt(dq, t.wq[0]) + nt(dk, t.wq[1]) + nt(dv, t.wq[2])
        du = du.astype(BF).astype(F32)
        xhat, r = stats(t.x[rows, :].astype(F32))
        t.u[rows, :] = (xhat * g0).astype(BF)
        t.dg[0:1, :] += jnp.sum(du * xhat, axis=0, keepdims=True)
        dx = norm_back(du, g0, xhat, r).astype(BF).astype(F32) + datt.astype(F32)
        t.dx[rows, :] = dx.astype(BF)

    pairs(window, after_first)


def product_left(lhs, x):
    return tn(lhs, jnp.concatenate([x, jnp.zeros((NT, 64), BF)], axis=1))


def product_right(lhs, x):
    return tn(lhs, jnp.concatenate([jnp.zeros((NT, 64), BF), x], axis=1))


def products_early(t):
    n2, dout = t.n2[...], t.dout[...]
    down_low = product_right(t.a[:, 0:384], dout)
    up_high = product_right(t.dup[:, 384:768], n2)
    for i, right in enumerate((up_high[0:192], up_high[192:384], down_low[0:192])):
        t.part[0, 192 * i:192 * i + 192, 128:384] = right.astype(BF)
    down_high = product_right(t.a[:, 384:768], dout)
    up_low = product_left(t.dup[:, 0:384], n2)
    proj = product_left(t.datt[...], t.mix[...])
    for i, (left, right) in enumerate(((proj, down_low[192:384]), (up_low[0:192], down_high[0:192]), (up_low[192:384], down_high[192:384]))):
        rows = slice(192 * i, 192 * i + 192)
        t.part[1, rows, 0:128] = left[:, 0:128].astype(BF)
        t.part[1, rows, 128:256] = (left[:, 128:256] + right[:, 0:128]).astype(BF)
        t.part[1, rows, 256:384] = right[:, 128:256].astype(BF)


def products_late(t):
    u = t.u[...]
    for i, ref in enumerate((t.dq, t.dk, t.dv)):
        rows = slice(192 * i, 192 * i + 192)
        left = product_left(ref[...], u)
        t.part[0, rows, 0:128] = left[:, 0:128].astype(BF)
        t.part[0, rows, 128:256] = (left[:, 128:256] + t.part[0, rows, 128:256].astype(F32)).astype(BF)


def other_rows(t):
    flat = jnp.concatenate([t.dg[0:1, :], t.dg[1:2, :], jnp.zeros((1, 3 * WT - 2 * C), F32)], axis=1)
    t.db[BROWS:OROWS, :] = jnp.concatenate([flat[:, 0:WT], flat[:, WT:2 * WT], flat[:, 2 * WT:3 * WT], jnp.zeros((OROWS - BROWS - 3, WT), F32)], axis=0)
    gap = jnp.zeros((240, 48), F32)
    for core in range(2):
        lft = t.db[lat_row(core):lat_row(core) + 240, :]
        rgt = t.db[lat_row(2 + core):lat_row(2 + core) + 240, :]
        t.part[core, 576:816, :] = jnp.concatenate([lft, gap, rgt, gap], axis=1).astype(BF)


def half_of(shape, axis):
    return (lax.broadcasted_iota(jnp.int32, shape, axis) // 36) % 2


def lane_moves(low):
    src = lax.broadcasted_iota(jnp.int32, (WT, WT), 0)
    dst = lax.broadcasted_iota(jnp.int32, (WT, WT), 1)
    keep = dst - 36 * ((dst // 36) % 2) + (0 if low else 36)
    return (src == keep).astype(F32)


def polar_bias(table, low):
    moved = jnp.dot(table, lane_moves(low), precision=lax.Precision.HIGHEST, preferred_element_type=F32)
    half = half_of((WT, WT), 0)
    if low:
        moved = jnp.where(half == 0, moved, pltpu.roll(moved, 36, 0))
    else:
        moved = jnp.where(half == 1, moved, pltpu.roll(moved, WT - 36, 0))
    return jnp.where(half == half_of((WT, WT), 1), moved, -1e30)


def polar_back(grad, low):
    half = half_of((WT, WT), 0)
    if low:
        folded = jnp.where(half == 0, grad + pltpu.roll(grad, WT - 36, 0), 0.0)
    else:
        folded = jnp.where(half == 1, grad + pltpu.roll(grad, 36, 0), 0.0)
    return lax.dot_general(folded, lane_moves(low), (((1,), (1,)), ((), ())), precision=lax.Precision.HIGHEST, preferred_element_type=F32)


def greet(peers):
    barrier = pltpu.get_barrier_semaphore()
    for cond, dev in peers:
        if cond is None:
            pl.semaphore_signal(barrier, inc=1, device_id=dev, device_id_type=MESH)
        else:
            @pl.when(cond)
            def _():
                pl.semaphore_signal(barrier, inc=1, device_id=dev, device_id_type=MESH)


def guarded(cond, act):
    if cond is None:
        act()
    else:
        pl.when(cond)(act)


class Exchange:
    def __init__(self, moves, src, dst, send_sem, recv_sem, base, here):
        self.sends, self.locals, self.recvs = moves
        self.src, self.dst, self.send_sem, self.recv_sem, self.base, self.here = src, dst, send_sem, recv_sem, base, here

    def remote(self, i, s, d, size, dev):
        return pltpu.make_async_remote_copy(
            src_ref=self.src.at[pl.ds(s, size), :], dst_ref=self.dst.at[pl.ds(d, size), :], send_sem=self.send_sem.at[self.base + i],
            recv_sem=self.recv_sem.at[self.base + i], device_id=dev, device_id_type=MESH)

    def start(self):
        for i, cond, s, d, size, dev in self.sends:
            guarded(cond, lambda: self.remote(i, s, d, size, dev).start())
        for cond, s, d, size in self.locals:
            def keep():
                self.dst[d:d + size, :] = self.src[s:s + size, :]
            guarded(cond, keep)

    def finish(self):
        for i, cond, d, size in self.recvs:
            guarded(cond, lambda: self.remote(i, 0, d, size, self.here).wait_recv())
        for i, cond, s, d, size, dev in self.sends:
            guarded(cond, lambda: self.remote(i, s, d, size, dev).wait_send())


def moves_out(n):
    sends = [
        (0, None, 432, 432, 48, (n.b, n.east)),
        (1, n.inner_up, 112, 592, 48, (n.up, n.east)),
        (2, n.first, 112, 112, 48, (n.b, n.east)),
        (3, n.inner_up, 0, 480, 112, (n.up, n.j)),
        (4, n.inner_down, 480, 0, 160, (n.down, n.j)),
    ]
    locals_ = [(None, 160, 160, 272), (n.first, 0, 0, 112), (n.last, 480, 480, 160)]
    recvs = [(0, None, 432, 48), (1, n.inner_down, 592, 48), (2, n.first, 112, 48), (3, n.inner_down, 480, 112), (4, n.inner_up, 0, 160)]
    return sends, locals_, recvs


def moves_back(n):
    sends = [
        (0, None, 432, 432, 48, (n.b, n.west)),
        (1, n.inner_down, 592, 112, 48, (n.down, n.west)),
        (2, n.first, 112, 112, 48, (n.b, n.west)),
        (3, n.inner_down, 480, 0, 112, (n.down, n.j)),
        (4, n.inner_up, 0, 480, 160, (n.up, n.j)),
    ]
    locals_ = [(None, 160, 160, 272), (n.first, 0, 0, 112), (n.last, 480, 480, 160)]
    recvs = [(0, None, 432, 48), (1, n.inner_up, 112, 48), (2, n.first, 112, 48), (3, n.inner_up, 0, 112), (4, n.inner_down, 480, 160)]
    return sends, locals_, recvs


def lat_row(lat):
    return ((650 * lat) // 48) * 16


def z_row(core, z):
    return ((52 * core + 325 * z) // 96) * 16


def x_row(core, z, x):
    return ((208 * core + 1300 * z + 325 * x) // 384) * 16


def al(v):
    return pl.multiple_of(v, 16)


def total(*terms):
    out = terms[0].astype(F32)
    for term in terms[1:]:
        out = out + term.astype(F32)
    return out


class Reduce:
    def __init__(self, n, t, send_sem, recv_sem, base):
        self.n, self.t, self.send_sem, self.recv_sem, self.base = n, t, send_sem, recv_sem, base

    def remote(self, i, s, d, dev):
        i = self.base + i
        return pltpu.make_async_remote_copy(src_ref=s, dst_ref=d, send_sem=self.send_sem.at[i], recv_sem=self.recv_sem.at[i], device_id=dev, device_id_type=MESH)

    def core_copies(self):
        n, t = self.n, self.t
        pal = n.device(core=1 - n.core)
        return (
            self.remote(0, t.part.at[1, pl.ds(0, 576), :], t.got_core.at[pl.ds(0, 576), :], pal),
            self.remote(1, t.part.at[0, pl.ds(0, 576), pl.ds(256, 128)], t.got_core.at[pl.ds(0, 576), pl.ds(256, 128)], pal),
            self.remote(2, t.part.at[1 - n.core, pl.ds(576, 240), :], t.got_core.at[pl.ds(576, 240), :], pal),
            self.remote(3, t.part.at[0, pl.ds(0, 576), pl.ds(0, 256)], t.got_core.at[pl.ds(0, 576), pl.ds(0, 256)], pal),
        )

    def first_copies(self):
        n, t = self.n, self.t
        tile2, tiles01, other = [], [], []
        for d in range(1, 4):
            i = 4 * d
            z = (n.z + d) % 4
            x = (n.x + d) % 4
            to_x, to_z = n.device(x=x), n.device(z=z)
            rows = pl.ds(al(32 * x), 48)
            tile2.append(self.remote(i, t.sum_m.at[:, rows, pl.ds(256, 128)], t.got_x.at[d - 1, :, :, pl.ds(128, 128)], to_x))
            tiles01.append(self.remote(i + 1, t.sum_m.at[:, rows, pl.ds(128, 128)], t.got_x.at[d - 1, :, :, pl.ds(0, 128)], to_x))
            tiles01.append(self.remote(i + 2, t.sum_m.at[z, :, pl.ds(0, 128)], t.got_z.at[d - 1], to_z))
            other.append(self.remote(i + 3, t.sum_o.at[pl.ds(al(z_row(n.core, z)), 80), :], t.got_o.at[d - 1], to_z))
        return tile2, tiles01, other

    def x_window(self, x):
        return al(x_row(self.n.core, self.n.z, x) - z_row(self.n.core, self.n.z))

    def second_copies(self):
        n, t = self.n, self.t
        out = []
        for d in range(1, 4):
            i = 3 * d + 13
            z = (n.z + d) % 4
            x = (n.x + d) % 4
            out.append(self.remote(i, t.sum_x.at[z], t.got_xz.at[d - 1], n.device(z=z)))
            dev = n.device(x=x)
            out.append(self.remote(i + 1, t.sum_zo.at[pl.ds(self.x_window(x), 32), :], t.got_ox.at[d - 1], dev))
            out.append(self.remote(i + 2, t.sum_z.at[pl.ds(al(32 * x), 48), :], t.got_zx.at[d - 1], dev))
        return out

    def third_copies(self):
        n, t = self.n, self.t
        devices = [n.device(yl=1 - n.yl), n.device(yh=1 - n.yh), n.device(yl=1 - n.yl, yh=1 - n.yh)]
        return [self.remote(25 + i, t.mid, t.got_y.at[i], dev) for i, dev in enumerate(devices)]

    def start(self, copies):
        for c in copies:
            c.start()

    def wait(self, copies):
        for c in copies:
            c.wait()

    def early_start(self):
        both = self.core_copies()
        for core in range(2):
            pl.when(self.n.core == core)(both[core].start)

    def early_to_first(self):
        n, t = self.n, self.t
        copies = self.core_copies()
        tile2, tiles01, _ = self.first_copies()

        @pl.when(n.core == 0)
        def _():
            copies[1].wait_recv()
            for z in range(4):
                rows = slice(144 * z, 144 * z + 144)
                t.sum_m[z, :, 256:384] = total(t.part[0, rows, 256:384], t.got_core[rows, 256:384]).astype(BF)
            self.start(tile2)
            copies[0].wait_send()

        @pl.when(n.core == 1)
        def _():
            copies[0].wait_recv()
            for z in range(4):
                rows = slice(144 * z, 144 * z + 144)
                t.sum_m[z] = total(t.part[1, rows, :], t.got_core[rows, :]).astype(BF)
            self.start(tile2 + tiles01)
            copies[1].wait_send()

    def late_start(self):
        copies = self.core_copies()
        pl.when(self.n.core == 1)(copies[3].start)
        copies[2].start()

    def late_to_first(self):
        n, t = self.n, self.t
        copies = self.core_copies()
        _, tiles01, other = self.first_copies()

        @pl.when(n.core == 0)
        def _():
            copies[3].wait_recv()
            for z in range(4):
                rows = slice(144 * z, 144 * z + 144)
                t.sum_m[z, :, 0:256] = total(t.part[0, rows, 0:256], t.got_core[rows, 0:256]).astype(BF)
            self.start(tiles01)

        copies[2].wait_recv()
        t.sum_o[...] = total(t.part[n.core, 576:816, :], t.got_core[576:816, :]).astype(BF)
        self.start(other)
        copies[2].wait_send()
        pl.when(n.core == 1)(copies[3].wait_send)

    def first_to_second(self):
        n, t = self.n, self.t
        for copies in self.first_copies():
            self.wait(copies)
        t.sum_x[...] = total(t.sum_m[:, pl.ds(al(32 * n.x), 48), 128:384], *[t.got_x[i] for i in range(3)]).astype(BF)
        t.sum_zo[...] = total(t.sum_o[pl.ds(al(z_row(n.core, n.z)), 80), :], *[t.got_o[i] for i in range(3)]).astype(BF)
        t.sum_z[...] = total(t.sum_m[n.z, :, 0:128], *[t.got_z[i] for i in range(3)]).astype(BF)
        self.start(self.second_copies())

    def second_to_third(self):
        n, t = self.n, self.t
        self.wait(self.second_copies())
        t.mid[0:48, 0:128] = total(t.sum_z[pl.ds(al(32 * n.x), 48), :], *[t.got_zx[i] for i in range(3)]).astype(BF)
        t.mid[0:48, 128:384] = total(t.sum_x[n.z], *[t.got_xz[i] for i in range(3)]).astype(BF)
        t.mid[48:80, :] = total(t.sum_zo[pl.ds(self.x_window(n.x), 32), :], *[t.got_ox[i] for i in range(3)]).astype(BF)
        self.start(self.third_copies())

    def finish(self):
        self.wait(self.third_copies())
        return total(self.t.mid[...], *[self.t.got_y[i] for i in range(3)])


def group_squares(n, final):
    matrix, other = final[0:48, :], final[48:80, :]
    row = lax.broadcasted_iota(jnp.int32, (48, 384), 0)
    low = 4 * n.x
    squares = jnp.sum(jnp.where((row >= low) & (row < low + 36), matrix * matrix, 0.0), axis=0, keepdims=True)
    lane = lax.broadcasted_iota(jnp.int32, (32, 384), 1)
    row = lax.broadcasted_iota(jnp.int32, (32, 384), 0) + x_row(n.core, n.z, n.x)
    for yh in range(2):
        lat = 2 * yh + n.core
        at = lane - C * yh
        index = (row + lat_row(lat)) * WT + at
        low = 975 * (32 * lat + 8 * n.z + 2 * n.x)
        inside = (index >= low) & (index < low + 1950) & (at >= 0) & (at < WT)
        squares = squares + jnp.sum(jnp.where(inside, other * other, 0.0), axis=0, keepdims=True)
    return jnp.sum(squares, axis=1, keepdims=True)


def own_lanes(n, final):
    return jnp.where(n.yh == 1, pltpu.roll(final, C, 1), final)[:, 0:256]


INPUTS = ["tok", "cot", "gains", "w_qkv", "w_proj", "w_up", "w_down", "bias", "to_win", "to_nat", "send_win", "win_send", "send_nat", "to_slots", "from_slots"]
PERMS = INPUTS[8:]
OUTPUTS = [("gtok", (NT, C), BF), ("m", (18, 2, C), F32), ("o", (2, 975), F32)]
COPIED = ["to_win", "tok", "w_qkv", "bias", "w_proj", "w_up", "w_down", "send_win", "send_nat", "cot", "to_slots", "from_slots", "win_send", "to_nat"]
SHAPES = {
    "tok": (NT, C), "cot": (NT, C), "w_qkv": (2, C, 3 * C), "w_proj": (2, C, C), "w_up": (2, C, FFN), "w_down": (2, C, FFN), "bias": (2, BROWS, WT),
    "to_win": (NT, NT), "to_nat": (NT, NT), "send_win": (NR, NT), "win_send": (NT, NR), "send_nat": (NR, NT), "to_slots": (NT, NR), "from_slots": (NR, NT),
}
BLOCK = [
    ("x", (NT, C), BF), ("wq", (3, C, C), BF), ("q", (NT, C), BF), ("k", (NT, C), BF), ("v", (NT, C), BF), ("p", (4 * BROWS, WT), BF),
    ("mix", (NT, C), BF), ("hid", (NT, C), F32), ("a", (NT, FFN), BF), ("gp", (NT, FFN), BF), ("dout", (NT, C), BF), ("part", (2, 816, 384), BF),
    ("got_core", (816, 384), BF), ("sum_m", (4, 144, 384), BF), ("sum_o", (240, 384), BF),
    ("got_x", (3, 4, 48, 256), BF), ("got_o", (3, 80, 384), BF), ("got_z", (3, 144, 128), BF),
    ("sum_x", (4, 48, 256), BF), ("sum_zo", (80, 384), BF), ("sum_z", (144, 128), BF),
    ("got_xz", (3, 48, 256), BF), ("got_ox", (3, 32, 384), BF), ("got_zx", (3, 48, 128), BF),
    ("mid", (80, 384), BF), ("got_y", (3, 80, 384), BF),
    ("db", (OROWS, WT), F32), ("dg", (2, C), F32),
]
SHARED = [
    ("out", (NT, C), BF), ("dx", (NT, C), BF), ("u", (NT, C), BF), ("n2", (NT, C), BF), ("datt", (NT, C), BF), ("dq", (NT, C), BF), ("dk", (NT, C), BF),
    ("dv", (NT, C), BF), ("dup", (NT, FFN), BF),
    ("lbias", (3, BROWS, WT), F32), ("db_pair", (2, BROWS, WT), F32), ("parts", (32, 1, 128), F32), ("own", (2, 80, 256), F32),
    ("cot_src", (NR, 256), BF), ("cot_dst", (NR, 256), BF), ("mid_src", (NR, 256), BF), ("mid_dst", (NR, 256), BF), ("back_src", (NR, 256), BF), ("back_dst", (NR, 256), BF),
]
SEMS = 15 + 56 + 31


def place(nlat, nlon):
    n = types.SimpleNamespace()
    n.b, n.j = lax.axis_index("lat"), lax.axis_index("lon")
    n.east, n.west = lax.rem(n.j + 1, nlon), lax.rem(n.j + nlon - 1, nlon)
    n.up, n.down = jnp.maximum(n.b - 1, 0), jnp.minimum(n.b + 1, nlat - 1)
    n.first, n.last = n.b == 0, n.b == nlat - 1
    n.inner_up, n.inner_down = n.b > 0, n.b < nlat - 1
    n.yh, n.core = n.b // 2, n.b % 2
    n.z, n.x, n.yl = n.j // 8, (n.j // 2) % 4, n.j % 2

    def device(yh=n.yh, core=n.core, z=n.z, x=n.x, yl=n.yl):
        return (yh * 2 + core, z * 8 + x * 2 + yl)

    n.device = device
    return n


def kernel(nlat, nlon, reduce, *refs):
    names = INPUTS + [o[0] for o in OUTPUTS] + ["first_" + e[0] for e in BLOCK] + ["second_" + e[0] for e in BLOCK] + [e[0] for e in SHARED] + ["in_" + k for k in COPIED] + ["send_sem", "recv_sem", "in_sem"]
    r = dict(zip(names, refs, strict=True))
    loads = {}
    for i, k in enumerate(COPIED):
        src, dst = r[k], r["in_" + k]
        if k == "bias":
            loads["bias"] = pltpu.make_async_copy(src.at[0], dst.at[0], r["in_sem"].at[i])
        else:
            loads[k] = pltpu.make_async_copy(src, dst, r["in_sem"].at[i])
        if k == "w_down":
            loads["bias_two"] = pltpu.make_async_copy(r["bias"].at[1], r["in_bias"].at[1], r["in_sem"].at[len(COPIED)])
    for copy in loads.values():
        copy.start()

    def need(*keys):
        for k in keys:
            loads[k].wait()

    weights = {k: r["in_" + k] if k in COPIED else r[k] for k in INPUTS}
    blocks = []
    for label in ("first_", "second_"):
        blocks.append(types.SimpleNamespace(**weights, **{e[0]: r[e[0]] for e in SHARED}, **{e[0]: r[label + e[0]] for e in BLOCK}))
    one, two = blocks
    n = place(nlat, nlon)
    sems = (r["send_sem"], r["recv_sem"])
    here = (n.b, n.j)
    ex_cot = Exchange(moves_out(n), one.cot_src, one.cot_dst, *sems, 0, here)
    ex_mid = Exchange(moves_out(n), one.mid_src, one.mid_dst, *sems, 5, here)
    ex_back = Exchange(moves_back(n), one.back_src, one.back_dst, *sems, 10, here)

    level = [(e, dz, dx) for e in range(2) for dz in range(4) for dx in range(4) if (e, dz, dx) != (0, 0, 0)]
    level_dev = [n.device(core=(n.core + e) % 2, z=(n.z + dz) % 4, x=(n.x + dx) % 4) for e, dz, dx in level]
    y_dev = [n.device(yl=1 - n.yl), n.device(yh=1 - n.yh), n.device(yl=1 - n.yl, yh=1 - n.yh)]
    far = level_dev + y_dev if reduce else []
    greet(
        [(None, (n.b, n.east)), (None, (n.b, n.west)), (n.inner_up, (n.up, n.j)), (n.inner_down, (n.down, n.j)), (n.inner_up, (n.up, n.east)), (n.inner_down, (n.down, n.west))]
        + [(None, d) for d in far]
    )

    need("to_win", "tok")
    one.x[...] = shuffle(one.to_win[...], one.tok[...])
    need("w_qkv")
    for b, t in enumerate(blocks):
        for i in range(3):
            t.wq[i] = t.w_qkv[b, :, C * i:C * i + C]
    need("bias")
    one.lbias[0] = one.bias[0] * LOG2E
    need("w_proj", "w_up", "w_down")
    forward_windows(one, 0, lambda w, h: one.lbias[0, h * WT:h * WT + WT, :], False)
    need("send_win")
    one.mid_src[:, 0:C] = shuffle(one.send_win[...], one.out[...])
    pl.semaphore_wait(pltpu.get_barrier_semaphore(), jnp.where(jnp.logical_or(n.first, n.last), 4, 6) + len(far))
    ex_mid.start()
    need("send_nat", "cot")
    one.cot_src[:, 0:C] = shuffle(one.send_nat[...], one.cot[...])
    ex_cot.start()
    need("bias_two", "to_slots", "from_slots", "win_send", "to_nat")

    for group in range(2):
        polar = n.first if group == 0 else n.last

        @pl.when(polar)
        def _():
            for h in range(HEADS):
                rows = slice(h * WT, h * WT + WT)
                two.lbias[1 + group, rows, :] = polar_bias(two.bias[1, rows, :] * LOG2E, group == 1)

        @pl.when(jnp.logical_not(polar))
        def _():
            two.lbias[1 + group] = two.bias[1] * LOG2E

    two.db_pair[...] = jnp.zeros((2, BROWS, WT), F32)
    ex_mid.finish()
    two.x[...] = shuffle(two.to_slots[...], two.mid_dst[:, 0:C])
    forward_windows(two, 1, lambda w, h: two.lbias[1 + w // 2, h * WT:h * WT + WT, :], True)

    def dbias_two(w, h, ds):
        two.db_pair[w // 2, h * WT:h * WT + WT, :] += ds

    ex_cot.finish()
    two.dout[...] = shuffle(two.to_slots[...], two.cot_dst[:, 0:C])
    red_one = Reduce(n, one, *sems, 15)
    red_two = Reduce(n, two, *sems, 43)

    def only_reducing(act):
        if reduce:
            act()

    backward_feed(two, 1)
    products_early(two)
    only_reducing(red_two.early_start)
    backward_attention(two, 1, dbias_two, red_two.early_to_first if reduce else None)
    two.back_src[:, 0:C] = shuffle(two.from_slots[...], two.dx[...])
    ex_back.start()
    for group in range(2):
        @pl.when(n.first if group == 0 else n.last)
        def _():
            for h in range(HEADS):
                rows = slice(h * WT, h * WT + WT)
                two.db_pair[group, rows, :] = polar_back(two.db_pair[group, rows, :], group == 1)

    two.db[0:BROWS, :] = two.db_pair[0] + two.db_pair[1]
    products_late(two)
    other_rows(two)
    only_reducing(red_two.late_start)

    ex_back.finish()
    only_reducing(red_two.late_to_first)
    one.dout[...] = shuffle(one.win_send[...], one.back_dst[:, 0:C])
    one.db[...] = jnp.zeros((OROWS, WT), F32)

    def dbias_one(w, h, ds):
        one.db[h * WT:h * WT + WT, :] += ds

    backward_feed(one, 0)
    products_early(one)
    only_reducing(red_one.early_start)

    def middle():
        red_two.first_to_second()
        red_one.early_to_first()

    backward_attention(one, 0, dbias_one, middle if reduce else None)
    products_late(one)
    other_rows(one)
    only_reducing(red_one.late_start)
    r["gtok"][...] = shuffle(one.to_nat[...], one.dx[...])
    if not reduce:
        return
    red_one.late_to_first()
    red_two.second_to_third()
    two_final = red_two.finish()
    squares = group_squares(n, two_final)
    red_one.first_to_second()
    red_one.second_to_third()
    one_final = red_one.finish()

    parts = one.parts
    parts[0] = jnp.broadcast_to(squares + group_squares(n, one_final), (1, 128))
    copies = [
        pltpu.make_async_remote_copy(src_ref=parts.at[0], dst_ref=parts.at[1 + i], send_sem=sems[0].at[71 + i], recv_sem=sems[1].at[71 + i], device_id=d, device_id_type=MESH)
        for i, d in enumerate(level_dev)
    ]
    for c in copies:
        c.start()
    for c in copies:
        c.wait()
    acc = parts[0]
    for i in range(len(copies)):
        acc = acc + parts[1 + i]
    ceiling = math.sqrt(24 * C * C + 2 * VECB)
    factor = jnp.minimum(1.0, ceiling / (jnp.sqrt(acc) + 1e-06))[0:1, 0:1]
    first_row = 4 * n.x + 18 * n.yl
    start = 975 * (32 * n.b + n.j) - (lat_row(n.b) + x_row(n.core, n.z, n.x)) * WT
    rows = []
    for b, final in enumerate((one_final, two_final)):
        one.own[b] = own_lanes(n, final) * factor
        for i in range(18):
            r["m"][i, b:b + 1, :] = one.own[b, pl.ds(first_row + i, 1), 0:C]
        rows.append(jnp.concatenate([one.own[b, pl.ds(48 + start // WT + i, 1), 0:WT] for i in range(8)], axis=1))
    flat = jnp.concatenate(rows + [jnp.zeros((6, 8 * WT), F32)], axis=0)
    r["o"][...] = pltpu.roll(flat, 8 * WT - start % WT, 1)[0:2, 0:975]


def run(nlat, nlon, reduce, tokens, cotangent, norm_gains, w_qkv, w_proj, w_up, w_down, pos_bias):
    args = [tokens.reshape(NT, C), cotangent.reshape(NT, C), norm_gains, w_qkv, w_proj, w_up, jnp.swapaxes(w_down, 1, 2), pos_bias.reshape(2, BROWS, WT)]
    args += [const(p) for p in PERMS]
    vmem = pl.BlockSpec(memory_space=pltpu.VMEM)
    anywhere = pl.BlockSpec(memory_space=pl.ANY)
    return pl.pallas_call(
        functools.partial(kernel, nlat, nlon, reduce),
        in_specs=[anywhere if k in COPIED else vmem for k in INPUTS],
        out_specs=[vmem] * len(OUTPUTS),
        out_shape=[jax.ShapeDtypeStruct(s, d) for _, s, d in OUTPUTS],
        scratch_shapes=[pltpu.VMEM(s, d) for _, s, d in BLOCK + BLOCK + SHARED] + [pltpu.VMEM(SHAPES[k], F32 if k == "bias" else BF) for k in COPIED]
        + [pltpu.SemaphoreType.DMA((SEMS,))] * 2 + [pltpu.SemaphoreType.DMA((len(COPIED) + 1,))],
        compiler_params=pltpu.CompilerParams(vmem_limit_bytes=VMEM_LIMIT, collective_id=1, has_side_effects=True),
        name="two_blocks",
    )(*args)


def copy_out(*refs):
    k = len(OUTPUTS)
    sem = refs[3 * k]
    loads = [pltpu.make_async_copy(refs[i], refs[2 * k + i], sem.at[i]) for i in range(k)]
    stores = [pltpu.make_async_copy(refs[2 * k + i], refs[k + i], sem.at[k + i]) for i in range(k)]
    for c in loads:
        c.start()
    for c, d in zip(loads[::-1], stores[::-1]):
        c.wait()
        d.start()
    for d in stores:
        d.wait()


def run_copy_out(results):
    anywhere = pl.BlockSpec(memory_space=pl.ANY)
    return pl.pallas_call(
        copy_out,
        in_specs=[anywhere] * len(results),
        out_specs=[anywhere] * len(results),
        out_shape=[jax.ShapeDtypeStruct(s, d) for _, s, d in OUTPUTS],
        scratch_shapes=[pltpu.VMEM(s, d) for _, s, d in OUTPUTS] + [pltpu.SemaphoreType.DMA((2 * len(OUTPUTS),))],
        name="copy_out",
    )(*results)


def shards(nlat, nlon, tokens, *args):
    gtok, m, o = run_copy_out(run(nlat, nlon, True, tokens, *args))
    return gtok.reshape(tokens.shape), m.transpose(1, 2, 0), o


def solution(mesh):
    grid = P(None, "lat", "lon", None)
    return jax.shard_map(
        functools.partial(shards, mesh.shape["lat"], mesh.shape["lon"]),
        mesh=mesh,
        in_specs=(grid, grid) + (P(),) * 6,
        out_specs=(grid, P(None, None, ("lat", "lon")), P(None, ("lat", "lon"))),
        check_vma=False,
    )
```
